32 devices in a mesh: dp: 8 (over y, x, core), mp: 4 (over z).
Axes of the slice: x: 2, y: 2, z: 4, core: 2. Of those that a mesh axis runs over, the one named last changes fastest.
Arguments:
- video: bfloat16 [8, 8, 784, 768], P('mp', 'dp'), may hold values from -6 to 6
- patch_width: int32 [8], P('dp'), may hold values from 196 to 784, as said below
- temporal_gain: float32 [768], replicated, may hold values from 0.25 to 1.75
- temporal_shift: float32 [768], replicated, may hold values from -1.75 to 1.75
- temporal_qkv: bfloat16 [768, 2304], replicated, may hold values from -0.21875 to 0.21875
- temporal_qv_bias: float32 [1536], replicated, may hold values from -1.75 to 1.75
- temporal_proj: bfloat16 [768, 768], replicated, may hold values from -0.625 to 0.625
- temporal_proj_bias: float32 [768], replicated, may hold values from -1.75 to 1.75
- spatial_gain: float32 [768], replicated, may hold values from 0.25 to 1.75
- spatial_shift: float32 [768], replicated, may hold values from -1.75 to 1.75
- spatial_qkv: bfloat16 [768, 2304], replicated, may hold values from -0.21875 to 0.21875
- spatial_qv_bias: float32 [1536], replicated, may hold values from -1.75 to 1.75
- spatial_proj: bfloat16 [768, 768], replicated, may hold values from -2 to 2
- spatial_proj_bias: float32 [768], replicated, may hold values from -1.75 to 1.75
- mlp_gain: float32 [768], replicated, may hold values from 0.25 to 1.75
- mlp_shift: float32 [768], replicated, may hold values from -1.75 to 1.75
- fc1_weight: bfloat16 [768, 3072], P(None, 'mp'), may hold values from -0.21875 to 0.21875
- fc1_bias: bfloat16 [3072], P('mp'), may hold values from -1.75 to 1.75
- fc2_weight: bfloat16 [3072, 768], P('mp'), may hold values from -0.109375 to 0.109375
- fc2_bias: float32 [768], replicated, may hold values from -1.75 to 1.75
- cotangent: bfloat16 [8, 8, 784, 768], P('mp', 'dp'), may hold values from -6 to 6
Outputs:
- output: bfloat16 [8, 8, 784, 768], P('mp', 'dp')
- video_grad: float32 [8, 8, 784, 768], P('mp', 'dp')
- temporal_gain_grad: float32 [768], replicated
- temporal_shift_grad: float32 [768], replicated
- temporal_qkv_grad: float32 [768, 2304], replicated
- temporal_qv_bias_grad: float32 [1536], replicated
- temporal_proj_grad: float32 [768, 768], replicated
- temporal_proj_bias_grad: float32 [768], replicated
- spatial_gain_grad: float32 [768], replicated
- spatial_shift_grad: float32 [768], replicated
- spatial_qkv_grad: float32 [768, 2304], replicated
- spatial_qv_bias_grad: float32 [1536], replicated
- spatial_proj_grad: float32 [768, 768], replicated
- spatial_proj_bias_grad: float32 [768], replicated
- mlp_gain_grad: float32 [768], replicated
- mlp_shift_grad: float32 [768], replicated
- fc1_weight_grad: float32 [768, 3072], P('dp', 'mp')
- fc1_bias_grad: float32 [3072], replicated
- fc2_weight_grad: float32 [3072, 768], P('mp', 'dp')
- fc2_bias_grad: float32 [768], replicated
The draws below stay inside these ranges and needn't reach their ends.
Inputs may be any that keep to these rules, and one draw needn't show every extreme that they name: `patch_width`: each set holds either one clip of 784 patches per frame or four clips of 196; sets of both kinds occur in every draw. Every clip has all 8 frames.
All inputs are finite; a program needn't handle non-finite values.
Results may differ from the reference program's by a relative error of at most 0.017.
Values may be sent and summed in bfloat16 or wider, within the bound.
A program may use at most 384 MiB of HBM per device.

```python
import jax
import jax.numpy as jnp
from jax import lax

D = 768
HEADS = 12
HEAD_DIM = 64
FF = 3072
FRAMES = 8
PATCH = 196
SLOTS = 784
SETS_ALL = 8


def draw_patch_width(key, part):
    key = jax.random.fold_in(key, 11)
    count_key, order_key = jax.random.split(key)
    large_sets = jax.random.randint(count_key, (), SETS_ALL // 4, SETS_ALL // 2 + 1)
    order = jax.random.permutation(order_key, SETS_ALL)
    return jnp.where(order < large_sets, SLOTS, PATCH).astype(jnp.int32)


def level_of(own_key, extent, cuts, low, top_value):
    level = 1.0
    for dim, blocks in cuts:
        heights = jax.random.uniform(jax.random.fold_in(jax.random.fold_in(own_key, 6), dim), (blocks,), jnp.float32, low / len(cuts), top_value / len(cuts))
        level = level * jnp.repeat(jnp.exp(heights), extent[dim] // blocks).reshape((-1,) + (1,) * (len(extent) - 1 - dim))
    return level


def centred(rng, extent, scale, limit, shards=(), held_as=jnp.bfloat16):
    factor_of = level_of(rng, extent, shards, -0.22, 0.18) if shards else 1.0
    entries = jax.random.normal(rng, extent, jnp.float32) * scale * factor_of
    return jnp.minimum(jnp.maximum(entries, -limit), limit).astype(held_as)


def setup_inputs(seed: int = 0) -> dict:
    arg_keys = jax.random.split(jax.random.key(seed), 22)
    return {
        "video": centred(arg_keys[0], (FRAMES, SETS_ALL, SLOTS, D), 1.0, 6.0, ((0, 4), (1, 8))),
        "patch_width": draw_patch_width(jax.random.fold_in(arg_keys[21], 71), 0),
        "temporal_gain": jnp.clip(1.0 + 0.15 * jax.random.normal(arg_keys[2], (D,), jnp.float32), 0.25, 1.75),
        "temporal_shift": centred(arg_keys[3], (D,), 0.3, 1.75, (), jnp.float32),
        "temporal_qkv": centred(arg_keys[4], (D, 3 * D), D ** -0.5, 0.21875),
        "temporal_qv_bias": centred(arg_keys[5], (2 * D,), 0.3, 1.75, (), jnp.float32),
        "temporal_proj": centred(arg_keys[6], (D, D), (D // 8) ** -0.5, 0.625),
        "temporal_proj_bias": centred(arg_keys[7], (D,), 0.3, 1.75, (), jnp.float32),
        "spatial_gain": jnp.clip(1.0 + 0.15 * jax.random.normal(arg_keys[8], (D,), jnp.float32), 0.25, 1.75),
        "spatial_shift": centred(arg_keys[9], (D,), 0.3, 1.75, (), jnp.float32),
        "spatial_qkv": centred(arg_keys[10], (D, 3 * D), D ** -0.5, 0.21875),
        "spatial_qv_bias": centred(arg_keys[11], (2 * D,), 0.3, 1.75, (), jnp.float32),
        "spatial_proj": centred(arg_keys[12], (D, D), (max(D // 96, 1)) ** -0.5, 2.0),
        "spatial_proj_bias": centred(arg_keys[13], (D,), 0.3, 1.75, (), jnp.float32),
        "mlp_gain": jnp.clip(1.0 + 0.15 * jax.random.normal(arg_keys[14], (D,), jnp.float32), 0.25, 1.75),
        "mlp_shift": centred(arg_keys[15], (D,), 0.3, 1.75, (), jnp.float32),
        "fc1_weight": centred(arg_keys[16], (D, FF), D ** -0.5, 0.21875, ((1, 4),)),
        "fc1_bias": centred(arg_keys[17], (FF,), 0.3, 1.75, ((0, 4),)),
        "fc2_weight": centred(arg_keys[18], (FF, D), FF ** -0.5, 0.109375, ((0, 4),)),
        "fc2_bias": centred(arg_keys[19], (D,), 0.3, 1.75, (), jnp.float32),
        "cotangent": centred(arg_keys[20], (FRAMES, SETS_ALL, SLOTS, D), 1.0, 6.0, ((0, 4), (1, 8))),
    }


EPSILON = 1e-06
HIGH = lax.Precision.HIGHEST

@jax.custom_vjp
def low(v):
    return lax.optimization_barrier(v.astype(jnp.bfloat16)).astype(jnp.float32)

@jax.custom_vjp
def low_back(v):
    return v

def low_keep(v):
    return (low(v), None)

def low_pass(kept, grad):
    return (grad,)

def back_keep(v):
    return (v, None)

def back_low(kept, grad):
    return (low(grad),)
low.defvjp(low_keep, low_pass)
low_back.defvjp(back_keep, back_low)

def layer_norm(value, gain, shift):
    centered = value - lax.optimization_barrier(jnp.mean(value, axis=-1, keepdims=True))
    scale = lax.rsqrt(lax.optimization_barrier(jnp.mean(centered * centered, axis=-1, keepdims=True)) + EPSILON)
    return centered * scale * gain + shift

def softmax_rows(scores):
    top = lax.optimization_barrier(jnp.max(scores, axis=-1, keepdims=True))
    lifted = jnp.exp(scores - top)
    return lifted / lax.optimization_barrier(jnp.sum(lifted, axis=-1, keepdims=True))

def both_round(value):
    return low_back(low(value))

def project_in(normed, weight, bias):
    joined = jnp.matmul(low(normed), weight, precision=HIGH)
    queries = both_round(joined[..., :D] + bias[:D])
    keys = both_round(joined[..., D:2 * D])
    values = both_round(joined[..., 2 * D:] + bias[D:])
    shape = normed.shape[:-1] + (HEADS, HEAD_DIM)
    return (queries.reshape(shape), keys.reshape(shape), values.reshape(shape))

def temporal_mix(queries, keys, values):
    scores = low_back(jnp.einsum('fshe,gshe->shfg', queries, keys, precision=HIGH) * HEAD_DIM ** (-0.5))
    mixing = low(softmax_rows(scores))
    return jnp.einsum('shfg,gshe->fshe', mixing, values, precision=HIGH)

def spatial_frame(inputs, same_clip):
    queries, keys, values = inputs
    scores = low_back(jnp.einsum('she,the->hst', queries, keys, precision=HIGH) * HEAD_DIM ** (-0.5))
    scores = jnp.where(same_clip[None], scores, -1e+30)
    mixing = low(softmax_rows(scores))
    return jnp.einsum('hst,the->she', mixing, values, precision=HIGH)

def one_set(params, video_set, width):
    temporal_gain, temporal_shift, temporal_qkv, temporal_qv_bias, temporal_proj, temporal_proj_bias, spatial_gain, spatial_shift, spatial_qkv, spatial_qv_bias, spatial_proj, spatial_proj_bias, mlp_gain, mlp_shift, fc1_weight, fc1_bias, fc2_weight, fc2_bias = params
    normed = layer_norm(video_set, temporal_gain, temporal_shift)
    queries, keys, values = project_in(normed, temporal_qkv, temporal_qv_bias)
    mixed = both_round(temporal_mix(queries, keys, values)).reshape(video_set.shape)
    first = video_set + low_back(jnp.matmul(mixed, temporal_proj, precision=HIGH) + temporal_proj_bias)
    normed = layer_norm(first, spatial_gain, spatial_shift)
    queries, keys, values = project_in(normed, spatial_qkv, spatial_qv_bias)
    clip_id = jnp.arange(SLOTS, dtype=jnp.int32) // width
    same_clip = clip_id[:, None] == clip_id[None, :]
    frame_step = jax.checkpoint(lambda inputs: spatial_frame(inputs, same_clip))
    mixed = both_round(lax.map(frame_step, (queries, keys, values))).reshape(video_set.shape)
    second = first + low_back(jnp.matmul(mixed, spatial_proj, precision=HIGH) + spatial_proj_bias)
    normed = low(layer_norm(second, mlp_gain, mlp_shift))
    inner = low_back(jnp.matmul(normed, fc1_weight, precision=HIGH) + fc1_bias)
    hidden = low(jax.nn.gelu(inner, approximate=False))
    return second + (jnp.matmul(hidden, fc2_weight, precision=HIGH) + fc2_bias)

def reference(video, patch_width, temporal_gain, temporal_shift, temporal_qkv, temporal_qv_bias, temporal_proj, temporal_proj_bias, spatial_gain, spatial_shift, spatial_qkv, spatial_qv_bias, spatial_proj, spatial_proj_bias, mlp_gain, mlp_shift, fc1_weight, fc1_bias, fc2_weight, fc2_bias, cotangent):
    params = tuple((item.astype(jnp.float32) for item in (temporal_gain, temporal_shift, temporal_qkv, temporal_qv_bias, temporal_proj, temporal_proj_bias, spatial_gain, spatial_shift, spatial_qkv, spatial_qv_bias, spatial_proj, spatial_proj_bias, mlp_gain, mlp_shift, fc1_weight, fc1_bias, fc2_weight, fc2_bias)))
    inputs = jnp.swapaxes(video.astype(jnp.float32), 0, 1)

    def forward(weights, tokens):

        def per_set(pair):
            return one_set(weights, pair[0], pair[1])
        return lax.map(jax.checkpoint(per_set), (tokens, patch_width))
    result, pullback = jax.vjp(forward, params, inputs)
    grads, input_grad = pullback(jnp.swapaxes(cotangent.astype(jnp.float32), 0, 1))
    output = jnp.swapaxes(result, 0, 1).astype(jnp.bfloat16)
    return (output, jnp.swapaxes(input_grad, 0, 1), grads[0], grads[1], grads[2], grads[3], grads[4], grads[5], grads[6], grads[7], grads[8], grads[9], grads[10], grads[11], grads[12], grads[13], grads[14], grads[15], grads[16], grads[17])
```

```python
import functools
import jax
import jax.numpy as jnp
from jax import lax
from jax.experimental import pallas as pl
from jax.experimental.pallas import tpu as pltpu
from jax.sharding import PartitionSpec as P

HEADS = 12
HEAD_DIM = 64
GROUP = 4
WIDE = GROUP * HEAD_DIM
EPSILON = 1e-06
F32 = jnp.float32
BF16 = jnp.bfloat16
MIB = 1 << 20


def params(mib=56):
    return pltpu.CompilerParams(vmem_limit_bytes=mib * MIB)


def dot(a, b):
    return jnp.dot(a, b, preferred_element_type=F32)


def dot_nt(a, b):
    return lax.dot_general(a, b, (((1,), (1,)), ((), ())), preferred_element_type=F32)


def dot_tn(a, b):
    return lax.dot_general(a, b, (((0,), (0,)), ((), ())), preferred_element_type=F32)


def head_lanes(rows, head, dtype):
    lane = lax.broadcasted_iota(jnp.int32, (rows, WIDE), 1)
    return (lane // HEAD_DIM == head).astype(dtype)


def windows(slots, clips, rows):
    size = slots // clips
    found = []
    for start in range(0, slots, rows):
        stop = min(start + rows, slots)
        low = start // size * size // 16 * 16
        high = min(-(-(-(-stop // size) * size) // 16) * 16, slots)
        found.append((start, stop, low, high))
    return found


def spatial_fwd_body(width_ref, q_ref, k_ref, v_ref, o_ref, l_ref, *, slots, rows, narrow):
    def attend(chunks, size):
        stats = []
        for start, stop, low, high in chunks:
            count = stop - start
            q = q_ref[start:stop, :]
            k = k_ref[low:high, :]
            v = v_ref[low:high, :]
            if size < slots:
                query_clip = (lax.broadcasted_iota(jnp.int32, (count, high - low), 0) + start) // size
                key_clip = (lax.broadcasted_iota(jnp.int32, (count, high - low), 1) + low) // size
                same = query_clip == key_clip
            total = jnp.zeros((count, WIDE), F32)
            lse = jnp.zeros((count, 128), F32)
            lane = lax.broadcasted_iota(jnp.int32, (count, 128), 1)
            for head in range(GROUP):
                s = dot_nt(q * head_lanes(count, head, BF16), k)
                if size < slots:
                    s = jnp.where(same, s, -1e30)
                top = jnp.max(s, axis=1, keepdims=True)
                e = jnp.exp(s - top)
                norm = jnp.sum(e, axis=1, keepdims=True)
                o = dot(e.astype(BF16), v)
                total = total + o * (head_lanes(count, head, F32) / norm)
                lse = jnp.where(lane == head, top + jnp.log(norm), lse)
            o_ref[start:stop, :] = total.astype(BF16)
            stats.append(lse)
        l_ref[...] = jnp.concatenate(stats, axis=0).T[:8, :]

    wide = width_ref[0] == slots

    @pl.when(wide)
    def _():
        attend(windows(slots, 1, rows or slots), slots)

    @pl.when(jnp.logical_not(wide))
    def _():
        attend(windows(slots, 4, narrow), slots // 4)


def spatial_fwd(width, qkv, frames, slots, rows=None, narrow=256):
    groups = HEADS // GROUP
    qkv = qkv.reshape(frames, slots, -1)
    spec = lambda part: pl.BlockSpec((None, slots, WIDE), lambda f, g, w: (f, 0, part * groups + g))
    out = pl.pallas_call(
        functools.partial(spatial_fwd_body, slots=slots, rows=rows, narrow=narrow),
        grid_spec=pltpu.PrefetchScalarGridSpec(
            num_scalar_prefetch=1,
            grid=(frames, groups),
            in_specs=[spec(0), spec(1), spec(2)],
            out_specs=[
                pl.BlockSpec((None, slots, WIDE), lambda f, g, w: (f, 0, g)),
                pl.BlockSpec((None, None, 8, slots), lambda f, g, w: (f, g, 0, 0)),
            ],
        ),
        out_shape=[
            jax.ShapeDtypeStruct((frames, slots, HEADS * HEAD_DIM), BF16),
            jax.ShapeDtypeStruct((frames, groups, 8, slots), F32),
        ],
        compiler_params=params(),
        name="spatial_fwd",
    )(width, qkv, qkv, qkv)
    return out


def spatial_bwd_body(width_ref, q_ref, k_ref, v_ref, o_ref, l_ref, g_ref, dq_ref, dk_ref, dv_ref, dqt, *, slots, rows, narrow):
    prod = g_ref[...].astype(F32) * o_ref[...].astype(F32)
    high_part = prod.astype(BF16)
    low_part = (prod - high_part.astype(F32)).astype(BF16)
    lane = lax.broadcasted_iota(jnp.int32, (8, WIDE), 1)
    row = lax.broadcasted_iota(jnp.int32, (8, WIDE), 0)
    picks = (lane // HEAD_DIM == row).astype(BF16)
    delta = dot_nt(picks, high_part) + dot_nt(picks, low_part)

    def attend(chunks, size):
        dqt[...] = jnp.zeros_like(dqt)
        kt = k_ref[...].T
        for start, stop, low, high in chunks:
            count = stop - start
            k = k_ref[start:stop, :]
            v = v_ref[start:stop, :]
            q = q_ref[low:high, :]
            g = g_ref[low:high, :]
            if size < slots:
                key_clip = (lax.broadcasted_iota(jnp.int32, (count, high - low), 0) + start) // size
                query_clip = (lax.broadcasted_iota(jnp.int32, (count, high - low), 1) + low) // size
                same = query_clip == key_clip
            dk = jnp.zeros((count, WIDE), F32)
            dv = jnp.zeros((count, WIDE), F32)
            for head in range(GROUP):
                mask = head_lanes(count, head, BF16)
                s = dot_nt(k * mask, q)
                p = jnp.exp(s - l_ref[head : head + 1, low:high])
                if size < slots:
                    p = jnp.where(same, p, 0.0)
                dp = dot_nt(v * mask, g)
                ds = (p * (dp - delta[head : head + 1, low:high])).astype(BF16)
                keep = head_lanes(count, head, F32)
                dv = dv + dot(p.astype(BF16), g) * keep
                dk = dk + dot(ds, q) * keep
                span = slice(head * HEAD_DIM, (head + 1) * HEAD_DIM)
                dqt[span, low:high] += dot(kt[span, start:stop], ds)
            dk_ref[start:stop, :] = dk.astype(BF16)
            dv_ref[start:stop, :] = dv.astype(BF16)
        dq_ref[...] = (dqt[...] * HEAD_DIM**-0.5).T.astype(BF16)

    wide = width_ref[0] == slots

    @pl.when(wide)
    def _():
        attend(windows(slots, 1, rows or slots), slots)

    @pl.when(jnp.logical_not(wide))
    def _():
        attend(windows(slots, 4, narrow), slots // 4)


def spatial_bwd(width, qkv, mixed, lse, grad, frames, slots, rows=None, narrow=208):
    groups = HEADS // GROUP
    width_all = HEADS * HEAD_DIM
    qkv = qkv.reshape(frames, slots, -1)
    spec = lambda part: pl.BlockSpec((None, slots, WIDE), lambda f, g, w: (f, 0, part * groups + g))
    one = pl.BlockSpec((None, slots, WIDE), lambda f, g, w: (f, 0, g))
    out = pl.pallas_call(
        functools.partial(spatial_bwd_body, slots=slots, rows=rows, narrow=narrow),
        grid_spec=pltpu.PrefetchScalarGridSpec(
            num_scalar_prefetch=1,
            grid=(frames, groups),
            in_specs=[
                spec(0), spec(1), spec(2), one,
                pl.BlockSpec((None, None, 8, slots), lambda f, g, w: (f, g, 0, 0)), one,
            ],
            out_specs=[one, one, one],
            scratch_shapes=[pltpu.VMEM((WIDE, slots), F32)],
        ),
        out_shape=[jax.ShapeDtypeStruct((frames, slots, width_all), BF16)] * 3,
        compiler_params=params(),
        name="spatial_bwd",
    )(width, qkv, qkv, qkv, mixed, lse, grad)
    return out


def fixed(shape):
    return pl.BlockSpec(shape, lambda *_: (0,) * len(shape))


def norm_parts(value):
    centered = value - jnp.mean(value, axis=-1, keepdims=True)
    scale = lax.rsqrt(jnp.mean(centered * centered, axis=-1, keepdims=True) + EPSILON)
    return centered * scale, scale


def norm_grad(grad, unit, scale, gain):
    inner = grad * gain
    return scale * (
        inner
        - jnp.mean(inner, axis=-1, keepdims=True)
        - unit * jnp.mean(inner * unit, axis=-1, keepdims=True)
    )


def column_sum(value):
    return jnp.sum(value.astype(F32), axis=0, keepdims=True)


def norm_in_body(video_ref, gain_ref, shift_ref, out_ref):
    unit, _ = norm_parts(video_ref[...].astype(F32))
    slots = video_ref.shape[0]
    out_ref[:slots, :] = (unit * gain_ref[...] + shift_ref[...]).astype(BF16)
    if out_ref.shape[0] > slots:
        out_ref[slots:, :] = jnp.zeros((out_ref.shape[0] - slots, out_ref.shape[1]), BF16)


def norm_in(video, gain, shift, padded):
    frames, slots, width = video.shape
    return pl.pallas_call(
        norm_in_body,
        grid=(frames,),
        in_specs=[pl.BlockSpec((None, slots, width), lambda f: (f, 0, 0)), fixed((1, width)), fixed((1, width))],
        out_specs=pl.BlockSpec((None, padded, width), lambda f: (f, 0, 0)),
        out_shape=jax.ShapeDtypeStruct((frames, padded, width), BF16),
        compiler_params=params(),
        name="norm_in",
    )(video, gain, shift)


STEP = 16


def stacked(block, rows):
    return jnp.concatenate([block * head_lanes(rows, head, BF16) for head in range(GROUP)], axis=0)


def temporal_fwd_body(x_ref, wq_ref, wk_ref, wv_ref, bq_ref, bv_ref, q_ref, k_ref, v_ref, o_ref):
    frames, slots, width = x_ref.shape
    x = x_ref[...].reshape(frames * slots, width)
    shape = (frames, slots, WIDE)
    q_ref[...] = ((dot(x, wq_ref[...]) + bq_ref[...]) * HEAD_DIM**-0.5).astype(BF16).reshape(shape)
    k_ref[...] = dot(x, wk_ref[...]).astype(BF16).reshape(shape)
    v_ref[...] = (dot(x, wv_ref[...]) + bv_ref[...]).astype(BF16).reshape(shape)
    rows = frames * STEP
    row = lax.broadcasted_iota(jnp.int32, (rows, rows), 0)
    col = lax.broadcasted_iota(jnp.int32, (rows, rows), 1)
    same = row % STEP == col % STEP
    for step in range(slots // STEP):
        part = slice(step * STEP, (step + 1) * STEP)
        q = q_ref[:, part, :].reshape(rows, WIDE)
        keys = stacked(k_ref[:, part, :].reshape(rows, WIDE), rows)
        values = stacked(v_ref[:, part, :].reshape(rows, WIDE), rows)
        scores = dot_nt(q, keys)
        mixing = []
        for head in range(GROUP):
            s = jnp.where(same, scores[:, head * rows : (head + 1) * rows], -1e30)
            e = jnp.exp(s - jnp.max(s, axis=1, keepdims=True))
            mixing.append((e / jnp.sum(e, axis=1, keepdims=True)).astype(BF16))
        o = dot(jnp.concatenate(mixing, axis=1), values)
        o_ref[:, part, :] = o.astype(BF16).reshape(frames, STEP, WIDE)


def temporal_fwd(x, weight, bias):
    frames, slots, width = x.shape
    groups = width // WIDE
    w = lambda part: pl.BlockSpec((width, WIDE), lambda g: (0, part * groups + g))
    b = lambda part: pl.BlockSpec((1, WIDE), lambda g: (0, part * groups + g))
    one = pl.BlockSpec((frames, slots, WIDE), lambda g: (0, 0, g))
    return pl.pallas_call(
        temporal_fwd_body,
        grid=(groups,),
        in_specs=[fixed(x.shape), w(0), w(1), w(2), b(0), b(1)],
        out_specs=[one] * 4,
        out_shape=[jax.ShapeDtypeStruct(x.shape, BF16)] * 4,
        compiler_params=params(),
        name="temporal_fwd",
    )(x, weight, weight, weight, bias, bias)


def temporal_bwd_body(
    x_ref, q_ref, k_ref, v_ref, g_ref, wq_ref, wk_ref, wv_ref, gain_ref, shift_ref,
    dq_ref, dk_ref, dv_ref, dx_ref, sums_ref, norm_ref, total_ref,
):
    frames, slots, width = x_ref.shape
    rows = frames * STEP
    row = lax.broadcasted_iota(jnp.int32, (rows, rows), 0)
    col = lax.broadcasted_iota(jnp.int32, (rows, rows), 1)
    same = row % STEP == col % STEP
    shape = (frames, STEP, WIDE)
    for step in range(slots // STEP):
        part = slice(step * STEP, (step + 1) * STEP)
        k = k_ref[:, part, :].reshape(rows, WIDE)
        v = v_ref[:, part, :].reshape(rows, WIDE)
        queries = stacked(q_ref[:, part, :].reshape(rows, WIDE), rows)
        grads = stacked(g_ref[:, part, :].reshape(rows, WIDE), rows)
        scores = dot_nt(k, queries)
        grad_mixing = dot_nt(v, grads)
        mixing, grad_scores = [], []
        for head in range(GROUP):
            span = slice(head * rows, (head + 1) * rows)
            s = jnp.where(same, scores[:, span], -1e30)
            e = jnp.exp(s - jnp.max(s, axis=0, keepdims=True))
            p = e / jnp.sum(e, axis=0, keepdims=True)
            gp = grad_mixing[:, span]
            ds = p * (gp - jnp.sum(p * gp, axis=0, keepdims=True))
            mixing.append(p.astype(BF16))
            grad_scores.append(ds.astype(BF16))
        grad_scores = jnp.concatenate(grad_scores, axis=1)
        dv_ref[:, part, :] = dot(jnp.concatenate(mixing, axis=1), grads).astype(BF16).reshape(shape)
        dk_ref[:, part, :] = dot(grad_scores, queries).astype(BF16).reshape(shape)
        spread = dot_tn(grad_scores, k)
        dq = jnp.zeros((rows, WIDE), F32)
        for head in range(GROUP):
            dq = dq + spread[head * rows : (head + 1) * rows] * head_lanes(rows, head, F32)
        dq_ref[:, part, :] = (dq * HEAD_DIM**-0.5).astype(BF16).reshape(shape)
    flat = (frames * slots, WIDE)
    dq, dk, dv = dq_ref[...].reshape(flat), dk_ref[...].reshape(flat), dv_ref[...].reshape(flat)
    sums_ref[...] = jnp.concatenate([column_sum(dq), column_sum(dv), jnp.zeros((6, WIDE), F32)], axis=0)
    update = dot_nt(dq, wq_ref[...]) + dot_nt(dk, wk_ref[...]) + dot_nt(dv, wv_ref[...])
    group = pl.program_id(0)

    @pl.when(group == 0)
    def _():
        total_ref[...] = update

    @pl.when(group > 0)
    def _():
        total_ref[...] += update

    @pl.when(group == pl.num_programs(0) - 1)
    def _():
        total = total_ref[...]
        dx_ref[...] = total.astype(BF16).reshape(frames, slots, width)
        x = x_ref[...].reshape(frames * slots, width).astype(F32)
        shift_grad = column_sum(total)
        gain_grad = (column_sum(total * x) - shift_ref[...] * shift_grad) / gain_ref[...]
        norm_ref[...] = jnp.concatenate([gain_grad, shift_grad, jnp.zeros((6, width), F32)], axis=0)


def temporal_bwd(x, q, k, v, grad, weight, gain, shift):
    frames, slots, width = x.shape
    groups = width // WIDE
    w = lambda part: pl.BlockSpec((width, WIDE), lambda g: (0, part * groups + g))
    one = pl.BlockSpec((frames, slots, WIDE), lambda g: (0, 0, g))
    return pl.pallas_call(
        temporal_bwd_body,
        grid=(groups,),
        in_specs=[fixed(x.shape), one, one, one, one, w(0), w(1), w(2), fixed((1, width)), fixed((1, width))],
        out_specs=[one, one, one, fixed(x.shape), pl.BlockSpec((8, WIDE), lambda g: (0, g)), fixed((8, width))],
        out_shape=[jax.ShapeDtypeStruct(x.shape, BF16)] * 4 + [jax.ShapeDtypeStruct((8, width), F32)] * 2,
        scratch_shapes=[pltpu.VMEM((frames * slots, width), F32)],
        compiler_params=params(),
        name="temporal_bwd",
    )(x, q, k, v, grad, weight, weight, weight, gain, shift)


def middle_body(mixed_ref, video_ref, proj_ref, pb_ref, gain_ref, shift_ref, w_ref, bias_ref, first_ref, normed_ref, qkv_ref):
    slots, width = video_ref.shape
    first = video_ref[...].astype(F32) + (dot(mixed_ref[:slots, :], proj_ref[...]) + pb_ref[...])
    first_ref[...] = first
    unit, _ = norm_parts(first)
    normed_ref[...] = (unit * gain_ref[...] + shift_ref[...]).astype(BF16)
    normed = normed_ref[...]
    q = dot(normed, w_ref[:, :width]) + bias_ref[:, :width]
    qkv_ref[:, :width] = (q * HEAD_DIM**-0.5).astype(BF16)
    qkv_ref[:, width : 2 * width] = dot(normed, w_ref[:, width : 2 * width]).astype(BF16)
    qkv_ref[:, 2 * width :] = (dot(normed, w_ref[:, 2 * width :]) + bias_ref[:, width:]).astype(BF16)


def middle(mixed, video, proj, proj_bias, gain, shift, weight, bias):
    frames, slots, width = video.shape
    per = lambda rows, cols: pl.BlockSpec((None, rows, cols), lambda f: (f, 0, 0))
    return pl.pallas_call(
        middle_body,
        grid=(frames,),
        in_specs=[
            per(mixed.shape[1], width), per(slots, width), fixed(proj.shape), fixed((1, width)), fixed((1, width)),
            fixed((1, width)), fixed(weight.shape), fixed((1, 2 * width)),
        ],
        out_specs=[per(slots, width), per(slots, width), per(slots, 3 * width)],
        out_shape=[
            jax.ShapeDtypeStruct(video.shape, F32),
            jax.ShapeDtypeStruct(video.shape, BF16),
            jax.ShapeDtypeStruct((frames, slots, 3 * width), BF16),
        ],
        compiler_params=params(),
        name="middle",
    )(mixed, video, proj, proj_bias, gain, shift, weight, bias)


def gelu_both(value):
    half = 0.5 * (1.0 + lax.erf(value * 0.7071067811865476))
    density = jnp.exp(-0.5 * value * value) * 0.3989422804014327
    return value * half, half + value * density


def feed_body(
    first_ref, mixed_ref, cot_ref, proj_ref, pb_ref, gain_ref, shift_ref, fc1_ref, fb1_ref, fc2_ref, fb2_ref,
    out_ref, normed_ref, hidden_ref, gi_ref, gs_ref, gso_ref, gspace_ref, sums_ref, unitsum_ref,
    second, branch, gnorm, *, sub,
):
    frame, chunk = pl.program_id(0), pl.program_id(1)
    slots, width = first_ref.shape
    units = fc1_ref.shape[1]

    @pl.when(chunk == 0)
    def _():
        value = first_ref[...] + (dot(mixed_ref[...], proj_ref[...]) + pb_ref[...])
        second[...] = value
        unit, _ = norm_parts(value)
        normed_ref[...] = (unit * gain_ref[...] + shift_ref[...]).astype(BF16)
        branch[...] = jnp.zeros_like(branch)
        gnorm[...] = jnp.zeros_like(gnorm)

    @pl.when(jnp.logical_and(frame == 0, chunk == 0))
    def _():
        sums_ref[...] = jnp.zeros_like(sums_ref)
        unitsum_ref[...] = jnp.zeros_like(unitsum_ref)

    normed = normed_ref[...]
    cot = cot_ref[...]
    for start in range(0, units, sub):
        span = slice(start, start + sub)
        inner = dot(normed, fc1_ref[:, span]) + fb1_ref[0:1, span]
        grad_hidden = dot_nt(cot, fc2_ref[span, :])
        act, slope = gelu_both(inner)
        hidden_ref[:, span] = act.astype(BF16)
        gi_ref[:, span] = (grad_hidden * slope).astype(BF16)
    branch[...] += dot(hidden_ref[...], fc2_ref[...])
    gnorm[...] += dot_nt(gi_ref[...], fc1_ref[...])
    unitsum_ref[chunk, 0:1, :] += column_sum(gi_ref[...])

    @pl.when(chunk == pl.num_programs(1) - 1)
    def _():
        value = second[...]
        out_ref[...] = (value + (branch[...] + fb2_ref[...])).astype(BF16)
        unit, scale = norm_parts(value)
        grad = gnorm[...]
        cot_full = cot_ref[...].astype(F32)
        grad_second = cot_full + norm_grad(grad, unit, scale, gain_ref[...])
        gs_ref[...] = grad_second
        gso_ref[...] = grad_second.astype(BF16)
        gspace_ref[...] = dot_nt(gso_ref[...], proj_ref[...]).astype(BF16)
        sums_ref[0:1, :] += column_sum(grad * unit)
        sums_ref[1:2, :] += column_sum(grad)
        sums_ref[2:3, :] += column_sum(gso_ref[...])
        sums_ref[3:4, :] += column_sum(cot_full)


def feed(first, mixed, cot, proj, proj_bias, gain, shift, fc1, fc1_bias, fc2, fc2_bias, sub=256):
    frames, slots, width = first.shape
    chunks, _, units = fc1.shape
    sub = units if units % sub else sub
    per = pl.BlockSpec((None, slots, width), lambda f, c: (f, 0, 0))
    row = fixed((1, width))
    hid = pl.BlockSpec((None, None, slots, units), lambda f, c: (c, f, 0, 0))
    hid_shape = jax.ShapeDtypeStruct((chunks, frames, slots, units), BF16)
    tok = lambda dtype: jax.ShapeDtypeStruct(first.shape, dtype)
    return pl.pallas_call(
        functools.partial(feed_body, sub=sub),
        grid=(frames, chunks),
        in_specs=[
            per, per, per, fixed(proj.shape), row, row, row,
            pl.BlockSpec((None, width, units), lambda f, c: (c, 0, 0)),
            pl.BlockSpec((None, 1, units), lambda f, c: (c, 0, 0)),
            pl.BlockSpec((None, units, width), lambda f, c: (c, 0, 0)),
            row,
        ],
        out_specs=[per, per, hid, hid, per, per, per, fixed((8, width)), fixed((chunks, 8, units))],
        out_shape=[
            tok(BF16), tok(BF16), hid_shape, hid_shape, tok(F32), tok(BF16), tok(BF16),
            jax.ShapeDtypeStruct((8, width), F32), jax.ShapeDtypeStruct((chunks, 8, units), F32),
        ],
        scratch_shapes=[pltpu.VMEM((slots, width), F32)] * 3,
        compiler_params=params(60),
        name="feed",
    )(first, mixed, cot, proj, proj_bias, gain, shift, fc1, fc1_bias, fc2, fc2_bias)


def middle_bwd_body(
    dq_ref, dk_ref, dv_ref, w_ref, first_ref, gs_ref, gain_ref, proj_ref, gf_ref, gto_ref, gt_ref, sums_ref
):
    slots, width = first_ref.shape
    dq, dk, dv = dq_ref[...], dk_ref[...], dv_ref[...]
    grad = dot_nt(dq, w_ref[:, :width]) + dot_nt(dk, w_ref[:, width : 2 * width]) + dot_nt(dv, w_ref[:, 2 * width :])
    unit, scale = norm_parts(first_ref[...])
    grad_first = gs_ref[...] + norm_grad(grad, unit, scale, gain_ref[...])
    gf_ref[...] = grad_first
    gto_ref[...] = grad_first.astype(BF16)
    gt_ref[:slots, :] = dot_nt(gto_ref[...], proj_ref[...]).astype(BF16)
    if gt_ref.shape[0] > slots:
        gt_ref[slots:, :] = jnp.zeros((gt_ref.shape[0] - slots, width), BF16)

    @pl.when(pl.program_id(0) == 0)
    def _():
        sums_ref[...] = jnp.zeros_like(sums_ref)

    sums_ref[0:1, :] += column_sum(grad * unit)
    sums_ref[1:2, :] += column_sum(grad)
    sums_ref[2:3, :] += column_sum(dq)
    sums_ref[3:4, :] += column_sum(dv)
    sums_ref[4:5, :] += column_sum(gto_ref[...])


def middle_bwd(dq, dk, dv, weight, first, grad_second, gain, proj, padded):
    frames, slots, width = first.shape
    per = lambda rows: pl.BlockSpec((None, rows, width), lambda f: (f, 0, 0))
    return pl.pallas_call(
        middle_bwd_body,
        grid=(frames,),
        in_specs=[
            per(slots), per(slots), per(slots), fixed(weight.shape), per(slots), per(slots), fixed((1, width)), fixed(proj.shape)
        ],
        out_specs=[per(slots), per(slots), per(padded), fixed((8, width))],
        out_shape=[
            jax.ShapeDtypeStruct(first.shape, F32), jax.ShapeDtypeStruct(first.shape, BF16),
            jax.ShapeDtypeStruct((frames, padded, width), BF16), jax.ShapeDtypeStruct((8, width), F32),
        ],
        compiler_params=params(60),
        name="middle_bwd",
    )(dq, dk, dv, weight, first, grad_second, gain, proj)


def norm_out_body(grad_ref, video_ref, gf_ref, gain_ref, out_ref):
    slots = video_ref.shape[0]
    unit, scale = norm_parts(video_ref[...].astype(F32))
    out_ref[...] = gf_ref[...] + norm_grad(grad_ref[:slots, :].astype(F32), unit, scale, gain_ref[...])


def norm_out(grad, video, grad_first, gain):
    frames, slots, width = video.shape
    per = lambda rows: pl.BlockSpec((None, rows, width), lambda f: (f, 0, 0))
    return pl.pallas_call(
        norm_out_body,
        grid=(frames,),
        in_specs=[per(grad.shape[1]), per(slots), per(slots), fixed((1, width))],
        out_specs=per(slots),
        out_shape=jax.ShapeDtypeStruct(video.shape, F32),
        compiler_params=params(),
        name="norm_out",
    )(grad, video, grad_first, gain)


def tn_body(a_ref, b_ref, out_ref):
    out_ref[...] = dot_tn(a_ref[...], b_ref[...]).astype(out_ref.dtype)


def weight_grads(pairs):
    found = []
    for a, many in pairs:
        rows, width = a.shape
        for b in many:
            found.append(
                pl.pallas_call(
                    tn_body,
                    grid=(width // WIDE,),
                    in_specs=[fixed(a.shape), pl.BlockSpec((rows, WIDE), lambda i: (0, i))],
                    out_specs=pl.BlockSpec((width, WIDE), lambda i: (0, i)),
                    out_shape=jax.ShapeDtypeStruct((width, width), BF16),
                    cost_estimate=pl.CostEstimate(
                        flops=2 * rows * width * width, bytes_accessed=4 * rows * width, transcendentals=0
                    ),
                    compiler_params=params(),
                    name="weight_grad",
                )(a, b)
            )
    return jnp.stack(found)


def fc_grads_body(normed_ref, cot_ref, gi_ref, hid_ref, out_ref):
    units = gi_ref.shape[1]
    out_ref[:, :units] = dot_tn(normed_ref[...], gi_ref[...]).astype(BF16)
    out_ref[:, units:] = dot_tn(cot_ref[...], hid_ref[...]).astype(BF16)


def fc_grads(normed, cot, grad_inner, hidden):
    chunks, frames, slots, units = hidden.shape
    width = normed.shape[-1]
    rows = frames * slots
    hid = pl.BlockSpec((None, rows, units), lambda c: (c, 0, 0))
    flat = lambda value: value.reshape(chunks, rows, units)
    return pl.pallas_call(
        fc_grads_body,
        grid=(chunks,),
        in_specs=[fixed((rows, width)), fixed((rows, width)), hid, hid],
        out_specs=pl.BlockSpec((None, width, 2 * units), lambda c: (c, 0, 0)),
        out_shape=jax.ShapeDtypeStruct((chunks, width, 2 * units), BF16),
        cost_estimate=pl.CostEstimate(
            flops=4 * rows * width * units * chunks, bytes_accessed=4 * rows * units * chunks, transcendentals=0
        ),
        compiler_params=params(),
        name="fc_grads",
    )(normed.reshape(rows, width), cot.reshape(rows, width), flat(grad_inner), flat(hidden))


def shards(
    video,
    patch_width,
    temporal_gain,
    temporal_shift,
    temporal_qkv,
    temporal_qv_bias,
    temporal_proj,
    temporal_proj_bias,
    spatial_gain,
    spatial_shift,
    spatial_qkv,
    spatial_qv_bias,
    spatial_proj,
    spatial_proj_bias,
    mlp_gain,
    mlp_shift,
    fc1_weight,
    fc1_bias,
    fc2_weight,
    fc2_bias,
    cotangent,
):
    frames, sets, slots, width = video.shape
    units = fc1_weight.shape[1]
    parts, planes = lax.axis_size("mp"), lax.axis_size("dp")
    share = -(-slots // (parts * STEP)) * STEP
    padded = share * parts
    row = lambda value: value.astype(F32).reshape(1, -1)
    video = video.reshape(frames * sets, slots, width)
    cot = cotangent.reshape(frames * sets, slots, width)

    piece = width // planes
    mine = lax.axis_index("dp") * piece
    own = jnp.concatenate(
        [lax.dynamic_slice_in_dim(fc1_weight, mine, piece, 0), lax.dynamic_slice_in_dim(fc2_weight, mine, piece, 0)], axis=1
    ) if units == width else None
    if own is not None:
        both = lax.all_gather(own, ("mp", "dp"), axis=0, tiled=True).reshape(parts, width, 2 * units)
        fc1, fc2 = both[:, :, :units], both[:, :, units:]
    else:
        piece2 = units // planes
        fc1 = lax.all_gather(lax.dynamic_slice_in_dim(fc1_weight, mine, piece, 0), ("mp", "dp"), axis=0, tiled=True)
        fc1 = fc1.reshape(parts, width, units)
        fc2 = lax.all_gather(
            lax.dynamic_slice_in_dim(fc2_weight, lax.axis_index("dp") * piece2, piece2, 0), ("mp", "dp"), axis=0, tiled=True
        ).reshape(parts, units, width)
    fb1 = lax.all_gather(fc1_bias, "mp", axis=0, tiled=True).astype(F32).reshape(parts, 1, units)

    normed_in = norm_in(video, row(temporal_gain), row(temporal_shift), padded)
    x = lax.all_to_all(normed_in, "mp", split_axis=1, concat_axis=0, tiled=True)
    tq, tk, tv, time_mixed = temporal_fwd(x, temporal_qkv, row(temporal_qv_bias))
    time_back = lax.all_to_all(time_mixed, "mp", split_axis=0, concat_axis=1, tiled=True)

    first, normed_mid, space_qkv = middle(
        time_back, video, temporal_proj, row(temporal_proj_bias), row(spatial_gain), row(spatial_shift), spatial_qkv,
        row(spatial_qv_bias),
    )
    space_mixed, lse = spatial_fwd(patch_width, space_qkv, frames, slots)

    output, normed_out, hidden, grad_inner, grad_second, grad_space_out, grad_space, feed_sums, unit_sums = feed(
        first, space_mixed, cot, spatial_proj, row(spatial_proj_bias), row(mlp_gain), row(mlp_shift), fc1, fb1, fc2,
        row(fc2_bias),
    )
    fc_part = fc_grads(normed_out, cot, grad_inner, hidden)
    fc_part = lax.psum_scatter(fc_part, "dp", scatter_dimension=1, tiled=True)
    fc_part = lax.psum_scatter(fc_part, "mp", scatter_dimension=0, tiled=True)[0].astype(F32)
    fc1_weight_grad = fc_part[:, :units]
    fc2_weight_grad = fc_part[:, units:].T

    dq, dk, dv = spatial_bwd(patch_width, space_qkv, space_mixed, lse, grad_space, frames, slots)
    grad_first, grad_time_out, grad_time, mid_sums = middle_bwd(
        dq, dk, dv, spatial_qkv, first, grad_second, row(spatial_gain), temporal_proj, padded
    )
    flat = lambda value: value.reshape(-1, width)
    early = weight_grads(
        [
            (flat(normed_mid), [flat(dq), flat(dk), flat(dv)]),
            (flat(space_mixed), [flat(grad_space_out)]),
            (flat(time_back[:, :slots]), [flat(grad_time_out)]),
        ]
    )
    early = lax.psum(early, ("dp", "mp"))

    grad_slot = lax.all_to_all(grad_time, "mp", split_axis=1, concat_axis=0, tiled=True)
    gq, gk, gv, grad_x, bias_sums, norm_sums = temporal_bwd(
        x, tq, tk, tv, grad_slot, temporal_qkv, row(temporal_gain), row(temporal_shift)
    )
    grad_in = lax.all_to_all(grad_x, "mp", split_axis=0, concat_axis=1, tiled=True)
    late = weight_grads([(flat(x), [flat(gq), flat(gk), flat(gv)])])
    late = lax.psum(late, ("dp", "mp"))
    video_grad = norm_out(grad_in, video, grad_first, row(temporal_gain))

    small = jnp.concatenate(
        [unit_sums[:, 0, :].reshape(-1, width), feed_sums[:4], mid_sums[:5], bias_sums[:2], norm_sums[:2]], axis=0
    )
    small = lax.psum(small, ("dp", "mp"))
    count = parts * units // width
    fc1_bias_grad = small[:count].reshape(-1)
    (
        mlp_gain_grad, mlp_shift_grad, spatial_proj_bias_grad, fc2_bias_grad,
        spatial_gain_grad, spatial_shift_grad, space_q_sum, space_v_sum, temporal_proj_bias_grad,
        time_q_sum, time_v_sum, temporal_gain_grad, temporal_shift_grad,
    ) = [small[count + i] for i in range(13)]
    wide = lambda parts_: jnp.concatenate([part.astype(F32) for part in parts_], axis=1)
    return (
        output.reshape(frames, sets, slots, width),
        video_grad.reshape(frames, sets, slots, width),
        temporal_gain_grad,
        temporal_shift_grad,
        wide([late[0], late[1], late[2]]),
        jnp.concatenate([time_q_sum, time_v_sum]),
        early[4].astype(F32),
        temporal_proj_bias_grad,
        spatial_gain_grad,
        spatial_shift_grad,
        wide([early[0], early[1], early[2]]),
        jnp.concatenate([space_q_sum, space_v_sum]),
        early[3].astype(F32),
        spatial_proj_bias_grad,
        mlp_gain_grad,
        mlp_shift_grad,
        fc1_weight_grad,
        fc1_bias_grad,
        fc2_weight_grad,
        fc2_bias_grad,
    )


def solution(mesh):
    tokens = P("mp", "dp", None, None)
    return jax.shard_map(
        shards,
        mesh=mesh,
        in_specs=(tokens, P("dp")) + (P(),) * 14 + (P(None, "mp"), P("mp"), P("mp", None), P(), tokens),
        out_specs=(tokens, tokens) + (P(),) * 14 + (P("dp", "mp"), P(), P("mp", "dp"), P()),
        check_vma=False,
    )
```

```python
import functools
import jax
import jax.numpy as jnp
from jax import lax
from jax.experimental import pallas as pl
from jax.experimental.pallas import tpu as pltpu
from jax.sharding import PartitionSpec as P

HEADS = 12
HEAD_DIM = 64
GROUP = 4
WIDE = GROUP * HEAD_DIM
EPSILON = 1e-06
F32 = jnp.float32
BF16 = jnp.bfloat16
MIB = 1 << 20


def params(mib=56):
    return pltpu.CompilerParams(vmem_limit_bytes=mib * MIB)


def dot(a, b):
    return jnp.dot(a, b, preferred_element_type=F32)


def dot_nt(a, b):
    return lax.dot_general(a, b, (((1,), (1,)), ((), ())), preferred_element_type=F32)


def dot_tn(a, b):
    return lax.dot_general(a, b, (((0,), (0,)), ((), ())), preferred_element_type=F32)


def head_lanes(rows, head, dtype):
    lane = lax.broadcasted_iota(jnp.int32, (rows, WIDE), 1)
    return (lane // HEAD_DIM == head).astype(dtype)


def windows(slots, clips, rows):
    size = slots // clips
    found = []
    for start in range(0, slots, rows):
        stop = min(start + rows, slots)
        low = start // size * size // 16 * 16
        high = min(-(-(-(-stop // size) * size) // 16) * 16, slots)
        found.append((start, stop, low, high))
    return found


def spatial_fwd_body(width_ref, q_ref, k_ref, v_ref, o_ref, l_ref, *, slots, rows, narrow):
    def attend(chunks, size):
        stats = []
        for start, stop, low, high in chunks:
            count = stop - start
            q = q_ref[start:stop, :]
            k = k_ref[low:high, :]
            v = v_ref[low:high, :]
            if size < slots:
                query_clip = (lax.broadcasted_iota(jnp.int32, (count, high - low), 0) + start) // size
                key_clip = (lax.broadcasted_iota(jnp.int32, (count, high - low), 1) + low) // size
                same = query_clip == key_clip
            total = jnp.zeros((count, WIDE), F32)
            lse = jnp.zeros((count, 128), F32)
            lane = lax.broadcasted_iota(jnp.int32, (count, 128), 1)
            for head in range(GROUP):
                s = dot_nt(q * head_lanes(count, head, BF16), k)
                if size < slots:
                    s = jnp.where(same, s, -1e30)
                top = jnp.max(s, axis=1, keepdims=True)
                e = jnp.exp(s - top)
                norm = jnp.sum(e, axis=1, keepdims=True)
                o = dot(e.astype(BF16), v)
                total = total + o * (head_lanes(count, head, F32) / norm)
                lse = jnp.where(lane == head, top + jnp.log(norm), lse)
            o_ref[start:stop, :] = total.astype(BF16)
            stats.append(lse)
        l_ref[...] = jnp.concatenate(stats, axis=0).T[:8, :]

    wide = width_ref[0] == slots

    @pl.when(wide)
    def _():
        attend(windows(slots, 1, rows or slots), slots)

    @pl.when(jnp.logical_not(wide))
    def _():
        attend(windows(slots, 4, narrow), slots // 4)


def spatial_fwd(width, qkv, frames, slots, rows=None, narrow=256):
    groups = HEADS // GROUP
    qkv = qkv.reshape(frames, slots, -1)
    spec = lambda part: pl.BlockSpec((None, slots, WIDE), lambda f, g, w: (f, 0, part * groups + g))
    out = pl.pallas_call(
        functools.partial(spatial_fwd_body, slots=slots, rows=rows, narrow=narrow),
        grid_spec=pltpu.PrefetchScalarGridSpec(
            num_scalar_prefetch=1,
            grid=(frames, groups),
            in_specs=[spec(0), spec(1), spec(2)],
            out_specs=[
                pl.BlockSpec((None, slots, WIDE), lambda f, g, w: (f, 0, g)),
                pl.BlockSpec((None, None, 8, slots), lambda f, g, w: (f, g, 0, 0)),
            ],
        ),
        out_shape=[
            jax.ShapeDtypeStruct((frames, slots, HEADS * HEAD_DIM), BF16),
            jax.ShapeDtypeStruct((frames, groups, 8, slots), F32),
        ],
        compiler_params=params(),
        name="spatial_fwd",
    )(width, qkv, qkv, qkv)
    return out


def spatial_bwd_body(width_ref, q_ref, k_ref, v_ref, o_ref, l_ref, g_ref, dq_ref, dk_ref, dv_ref, dqt, *, slots, rows, narrow):
    prod = g_ref[...].astype(F32) * o_ref[...].astype(F32)
    high_part = prod.astype(BF16)
    low_part = (prod - high_part.astype(F32)).astype(BF16)
    lane = lax.broadcasted_iota(jnp.int32, (8, WIDE), 1)
    row = lax.broadcasted_iota(jnp.int32, (8, WIDE), 0)
    picks = (lane // HEAD_DIM == row).astype(BF16)
    delta = dot_nt(picks, high_part) + dot_nt(picks, low_part)

    def attend(chunks, size):
        dqt[...] = jnp.zeros_like(dqt)
        kt = k_ref[...].T
        for start, stop, low, high in chunks:
            count = stop - start
            k = k_ref[start:stop, :]
            v = v_ref[start:stop, :]
            q = q_ref[low:high, :]
            g = g_ref[low:high, :]
            if size < slots:
                key_clip = (lax.broadcasted_iota(jnp.int32, (count, high - low), 0) + start) // size
                query_clip = (lax.broadcasted_iota(jnp.int32, (count, high - low), 1) + low) // size
                same = query_clip == key_clip
            dk = jnp.zeros((count, WIDE), F32)
            dv = jnp.zeros((count, WIDE), F32)
            for head in range(GROUP):
                mask = head_lanes(count, head, BF16)
                s = dot_nt(k * mask, q)
                p = jnp.exp(s - l_ref[head : head + 1, low:high])
                if size < slots:
                    p = jnp.where(same, p, 0.0)
                dp = dot_nt(v * mask, g)
                ds = (p * (dp - delta[head : head + 1, low:high])).astype(BF16)
                keep = head_lanes(count, head, F32)
                dv = dv + dot(p.astype(BF16), g) * keep
                dk = dk + dot(ds, q) * keep
                span = slice(head * HEAD_DIM, (head + 1) * HEAD_DIM)
                dqt[span, low:high] += dot(kt[span, start:stop], ds)
            dk_ref[start:stop, :] = dk.astype(BF16)
            dv_ref[start:stop, :] = dv.astype(BF16)
        dq_ref[...] = (dqt[...] * HEAD_DIM**-0.5).T.astype(BF16)

    wide = width_ref[0] == slots

    @pl.when(wide)
    def _():
        attend(windows(slots, 1, rows or slots), slots)

    @pl.when(jnp.logical_not(wide))
    def _():
        attend(windows(slots, 4, narrow), slots // 4)


def spatial_bwd(width, qkv, mixed, lse, grad, frames, slots, rows=None, narrow=208):
    groups = HEADS // GROUP
    width_all = HEADS * HEAD_DIM
    qkv = qkv.reshape(frames, slots, -1)
    spec = lambda part: pl.BlockSpec((None, slots, WIDE), lambda f, g, w: (f, 0, part * groups + g))
    one = pl.BlockSpec((None, slots, WIDE), lambda f, g, w: (f, 0, g))
    out = pl.pallas_call(
        functools.partial(spatial_bwd_body, slots=slots, rows=rows, narrow=narrow),
        grid_spec=pltpu.PrefetchScalarGridSpec(
            num_scalar_prefetch=1,
            grid=(frames, groups),
            in_specs=[
                spec(0), spec(1), spec(2), one,
                pl.BlockSpec((None, None, 8, slots), lambda f, g, w: (f, g, 0, 0)), one,
            ],
            out_specs=[one, one, one],
            scratch_shapes=[pltpu.VMEM((WIDE, slots), F32)],
        ),
        out_shape=[jax.ShapeDtypeStruct((frames, slots, width_all), BF16)] * 3,
        compiler_params=params(),
        name="spatial_bwd",
    )(width, qkv, qkv, qkv, mixed, lse, grad)
    return out


def fixed(shape):
    return pl.BlockSpec(shape, lambda *_: (0,) * len(shape))


def norm_parts(value):
    centered = value - jnp.mean(value, axis=-1, keepdims=True)
    scale = lax.rsqrt(jnp.mean(centered * centered, axis=-1, keepdims=True) + EPSILON)
    return centered * scale, scale


def norm_grad(grad, unit, scale, gain):
    inner = grad * gain
    return scale * (
        inner
        - jnp.mean(inner, axis=-1, keepdims=True)
        - unit * jnp.mean(inner * unit, axis=-1, keepdims=True)
    )


def column_sum(value):
    return jnp.sum(value.astype(F32), axis=0, keepdims=True)


def by_part(parts, share, width):
    return pl.BlockSpec((parts, None, share, width), lambda f: (0, f, 0, 0))


def norm_in_body(video_ref, gain_ref, shift_ref, out_ref):
    unit, _ = norm_parts(video_ref[...].astype(F32))
    split_positions(out_ref, (unit * gain_ref[...] + shift_ref[...]).astype(BF16))


def split_positions(out_ref, value):
    parts, share, width = out_ref.shape
    slots = value.shape[0]
    for part in range(parts):
        start = part * share
        count = min(max(slots - start, 0), share)
        if count > 0:
            out_ref[part, :count, :] = value[start : start + count, :]
        if count < share:
            out_ref[part, count:, :] = jnp.zeros((share - count, width), value.dtype)


def joined_positions(ref, slots):
    parts, share, width = ref.shape
    return ref[...].reshape(parts * share, width)[:slots, :]


def norm_in(video, gain, shift, parts, share):
    frames, slots, width = video.shape
    return pl.pallas_call(
        norm_in_body,
        grid=(frames,),
        in_specs=[pl.BlockSpec((None, slots, width), lambda f: (f, 0, 0)), fixed((1, width)), fixed((1, width))],
        out_specs=by_part(parts, share, width),
        out_shape=jax.ShapeDtypeStruct((parts, frames, share, width), BF16),
        compiler_params=params(),
        name="norm_in",
    )(video, gain, shift)


STEP = 16


def stacked(block, rows):
    return jnp.concatenate([block * head_lanes(rows, head, BF16) for head in range(GROUP)], axis=0)


def temporal_fwd_body(x_ref, wq_ref, wk_ref, wv_ref, bq_ref, bv_ref, q_ref, k_ref, v_ref, o_ref):
    frames, slots, width = x_ref.shape
    x = x_ref[...].reshape(frames * slots, width)
    shape = (frames, slots, WIDE)
    q_ref[...] = ((dot(x, wq_ref[...]) + bq_ref[...]) * HEAD_DIM**-0.5).astype(BF16).reshape(shape)
    k_ref[...] = dot(x, wk_ref[...]).astype(BF16).reshape(shape)
    v_ref[...] = (dot(x, wv_ref[...]) + bv_ref[...]).astype(BF16).reshape(shape)
    rows = frames * STEP
    row = lax.broadcasted_iota(jnp.int32, (rows, rows), 0)
    col = lax.broadcasted_iota(jnp.int32, (rows, rows), 1)
    same = row % STEP == col % STEP
    for step in range(slots // STEP):
        part = slice(step * STEP, (step + 1) * STEP)
        q = q_ref[:, part, :].reshape(rows, WIDE)
        keys = stacked(k_ref[:, part, :].reshape(rows, WIDE), rows)
        values = stacked(v_ref[:, part, :].reshape(rows, WIDE), rows)
        scores = dot_nt(q, keys)
        mixing = []
        for head in range(GROUP):
            s = jnp.where(same, scores[:, head * rows : (head + 1) * rows], -1e30)
            e = jnp.exp(s - jnp.max(s, axis=1, keepdims=True))
            mixing.append((e / jnp.sum(e, axis=1, keepdims=True)).astype(BF16))
        o = dot(jnp.concatenate(mixing, axis=1), values)
        o_ref[:, part, :] = o.astype(BF16).reshape(frames, STEP, WIDE)


def temporal_fwd(x, weight, bias):
    frames, slots, width = x.shape
    groups = width // WIDE
    w = lambda part: pl.BlockSpec((width, WIDE), lambda g: (0, part * groups + g))
    b = lambda part: pl.BlockSpec((1, WIDE), lambda g: (0, part * groups + g))
    one = pl.BlockSpec((frames, slots, WIDE), lambda g: (0, 0, g))
    return pl.pallas_call(
        temporal_fwd_body,
        grid=(groups,),
        in_specs=[fixed(x.shape), w(0), w(1), w(2), b(0), b(1)],
        out_specs=[one] * 4,
        out_shape=[jax.ShapeDtypeStruct(x.shape, BF16)] * 4,
        compiler_params=params(),
        name="temporal_fwd",
    )(x, weight, weight, weight, bias, bias)


def temporal_bwd_body(
    x_ref, q_ref, k_ref, v_ref, g_ref, wq_ref, wk_ref, wv_ref, gain_ref, shift_ref,
    dq_ref, dk_ref, dv_ref, dx_ref, sums_ref, norm_ref, total_ref,
):
    frames, slots, width = x_ref.shape
    rows = frames * STEP
    row = lax.broadcasted_iota(jnp.int32, (rows, rows), 0)
    col = lax.broadcasted_iota(jnp.int32, (rows, rows), 1)
    same = row % STEP == col % STEP
    shape = (frames, STEP, WIDE)
    for step in range(slots // STEP):
        part = slice(step * STEP, (step + 1) * STEP)
        k = k_ref[:, part, :].reshape(rows, WIDE)
        v = v_ref[:, part, :].reshape(rows, WIDE)
        queries = stacked(q_ref[:, part, :].reshape(rows, WIDE), rows)
        grads = stacked(g_ref[:, part, :].reshape(rows, WIDE), rows)
        scores = dot_nt(k, queries)
        grad_mixing = dot_nt(v, grads)
        mixing, grad_scores = [], []
        for head in range(GROUP):
            span = slice(head * rows, (head + 1) * rows)
            s = jnp.where(same, scores[:, span], -1e30)
            e = jnp.exp(s - jnp.max(s, axis=0, keepdims=True))
            p = e / jnp.sum(e, axis=0, keepdims=True)
            gp = grad_mixing[:, span]
            ds = p * (gp - jnp.sum(p * gp, axis=0, keepdims=True))
            mixing.append(p.astype(BF16))
            grad_scores.append(ds.astype(BF16))
        grad_scores = jnp.concatenate(grad_scores, axis=1)
        dv_ref[:, part, :] = dot(jnp.concatenate(mixing, axis=1), grads).astype(BF16).reshape(shape)
        dk_ref[:, part, :] = dot(grad_scores, queries).astype(BF16).reshape(shape)
        spread = dot_tn(grad_scores, k)
        dq = jnp.zeros((rows, WIDE), F32)
        for head in range(GROUP):
            dq = dq + spread[head * rows : (head + 1) * rows] * head_lanes(rows, head, F32)
        dq_ref[:, part, :] = (dq * HEAD_DIM**-0.5).astype(BF16).reshape(shape)
    flat = (frames * slots, WIDE)
    dq, dk, dv = dq_ref[...].reshape(flat), dk_ref[...].reshape(flat), dv_ref[...].reshape(flat)
    sums_ref[...] = jnp.concatenate([column_sum(dq), column_sum(dv), jnp.zeros((6, WIDE), F32)], axis=0)
    update = dot_nt(dq, wq_ref[...]) + dot_nt(dk, wk_ref[...]) + dot_nt(dv, wv_ref[...])
    group = pl.program_id(0)

    @pl.when(group == 0)
    def _():
        total_ref[...] = update

    @pl.when(group > 0)
    def _():
        total_ref[...] += update

    @pl.when(group == pl.num_programs(0) - 1)
    def _():
        total = total_ref[...]
        dx_ref[...] = total.astype(BF16).reshape(frames, slots, width)
        x = x_ref[...].reshape(frames * slots, width).astype(F32)
        shift_grad = column_sum(total)
        gain_grad = (column_sum(total * x) - shift_ref[...] * shift_grad) / gain_ref[...]
        norm_ref[...] = jnp.concatenate([gain_grad, shift_grad, jnp.zeros((6, width), F32)], axis=0)


def temporal_bwd(x, q, k, v, grad, weight, gain, shift):
    frames, slots, width = x.shape
    groups = width // WIDE
    w = lambda part: pl.BlockSpec((width, WIDE), lambda g: (0, part * groups + g))
    one = pl.BlockSpec((frames, slots, WIDE), lambda g: (0, 0, g))
    return pl.pallas_call(
        temporal_bwd_body,
        grid=(groups,),
        in_specs=[fixed(x.shape), one, one, one, one, w(0), w(1), w(2), fixed((1, width)), fixed((1, width))],
        out_specs=[one, one, one, fixed(x.shape), pl.BlockSpec((8, WIDE), lambda g: (0, g)), fixed((8, width))],
        out_shape=[jax.ShapeDtypeStruct(x.shape, BF16)] * 4 + [jax.ShapeDtypeStruct((8, width), F32)] * 2,
        scratch_shapes=[pltpu.VMEM((frames * slots, width), F32)],
        compiler_params=params(),
        name="temporal_bwd",
    )(x, q, k, v, grad, weight, weight, weight, gain, shift)


def middle_body(mixed_ref, video_ref, proj_ref, pb_ref, gain_ref, shift_ref, w_ref, bias_ref, first_ref, normed_ref, qkv_ref):
    slots, width = video_ref.shape
    first = video_ref[...].astype(F32) + (dot(joined_positions(mixed_ref, slots), proj_ref[...]) + pb_ref[...])
    first_ref[...] = first
    unit, _ = norm_parts(first)
    normed_ref[...] = (unit * gain_ref[...] + shift_ref[...]).astype(BF16)
    normed = normed_ref[...]
    q = dot(normed, w_ref[:, :width]) + bias_ref[:, :width]
    qkv_ref[:, :width] = (q * HEAD_DIM**-0.5).astype(BF16)
    qkv_ref[:, width : 2 * width] = dot(normed, w_ref[:, width : 2 * width]).astype(BF16)
    qkv_ref[:, 2 * width :] = (dot(normed, w_ref[:, 2 * width :]) + bias_ref[:, width:]).astype(BF16)


def middle(mixed, video, proj, proj_bias, gain, shift, weight, bias):
    frames, slots, width = video.shape
    per = lambda rows, cols: pl.BlockSpec((None, rows, cols), lambda f: (f, 0, 0))
    return pl.pallas_call(
        middle_body,
        grid=(frames,),
        in_specs=[
            by_part(mixed.shape[0], mixed.shape[2], width), per(slots, width), fixed(proj.shape), fixed((1, width)), fixed((1, width)),
            fixed((1, width)), fixed(weight.shape), fixed((1, 2 * width)),
        ],
        out_specs=[per(slots, width), per(slots, width), per(slots, 3 * width)],
        out_shape=[
            jax.ShapeDtypeStruct(video.shape, F32),
            jax.ShapeDtypeStruct(video.shape, BF16),
            jax.ShapeDtypeStruct((frames, slots, 3 * width), BF16),
        ],
        compiler_params=params(),
        name="middle",
    )(mixed, video, proj, proj_bias, gain, shift, weight, bias)


def gelu_both(value):
    half = 0.5 * (1.0 + lax.erf(value * 0.7071067811865476))
    density = jnp.exp(-0.5 * value * value) * 0.3989422804014327
    return value * half, half + value * density


def feed_body(
    first_ref, mixed_ref, cot_ref, proj_ref, pb_ref, gain_ref, shift_ref, fc1_ref, fb1_ref, fc2_ref, fb2_ref,
    out_ref, normed_ref, hidden_ref, gi_ref, gs_ref, gso_ref, gspace_ref, sums_ref, unitsum_ref,
    second, branch, gnorm, *, sub,
):
    frame, chunk = pl.program_id(0), pl.program_id(1)
    slots, width = first_ref.shape
    units = fc1_ref.shape[1]

    @pl.when(chunk == 0)
    def _():
        value = first_ref[...] + (dot(mixed_ref[...], proj_ref[...]) + pb_ref[...])
        second[...] = value
        unit, _ = norm_parts(value)
        normed_ref[...] = (unit * gain_ref[...] + shift_ref[...]).astype(BF16)
        branch[...] = jnp.zeros_like(branch)
        gnorm[...] = jnp.zeros_like(gnorm)

    @pl.when(jnp.logical_and(frame == 0, chunk == 0))
    def _():
        sums_ref[...] = jnp.zeros_like(sums_ref)
        unitsum_ref[...] = jnp.zeros_like(unitsum_ref)

    normed = normed_ref[...]
    cot = cot_ref[...]
    for start in range(0, units, sub):
        span = slice(start, start + sub)
        inner = dot(normed, fc1_ref[:, span]) + fb1_ref[0:1, span]
        grad_hidden = dot(cot, fc2_ref[:, span])
        act, slope = gelu_both(inner)
        hidden_ref[:, span] = act.astype(BF16)
        gi_ref[:, span] = (grad_hidden * slope).astype(BF16)
    branch[...] += dot_nt(hidden_ref[...], fc2_ref[...])
    gnorm[...] += dot_nt(gi_ref[...], fc1_ref[...])
    unitsum_ref[chunk, 0:1, :] += column_sum(gi_ref[...])

    @pl.when(chunk == pl.num_programs(1) - 1)
    def _():
        value = second[...]
        out_ref[...] = (value + (branch[...] + fb2_ref[...])).astype(BF16)
        unit, scale = norm_parts(value)
        grad = gnorm[...]
        cot_full = cot_ref[...].astype(F32)
        grad_second = cot_full + norm_grad(grad, unit, scale, gain_ref[...])
        gs_ref[...] = grad_second
        gso_ref[...] = grad_second.astype(BF16)
        gspace_ref[...] = dot_nt(gso_ref[...], proj_ref[...]).astype(BF16)
        sums_ref[0:1, :] += column_sum(grad * unit)
        sums_ref[1:2, :] += column_sum(grad)
        sums_ref[2:3, :] += column_sum(gso_ref[...])
        sums_ref[3:4, :] += column_sum(cot_full)


def feed(first, mixed, cot, proj, proj_bias, gain, shift, joint, fc1_bias, fc2_bias, sub=None):
    frames, slots, width = first.shape
    chunks, _, units = fc1_bias.shape
    sub = sub or units
    per = pl.BlockSpec((None, slots, width), lambda f, c: (f, 0, 0))
    row = fixed((1, width))
    hid = pl.BlockSpec((None, None, slots, units), lambda f, c: (c, f, 0, 0))
    hid_shape = jax.ShapeDtypeStruct((chunks, frames, slots, units), BF16)
    tok = lambda dtype: jax.ShapeDtypeStruct(first.shape, dtype)
    return pl.pallas_call(
        functools.partial(feed_body, sub=sub),
        grid=(frames, chunks),
        in_specs=[
            per, per, per, fixed(proj.shape), row, row, row,
            pl.BlockSpec((None, width, units), lambda f, c: (c, 0, 0)),
            pl.BlockSpec((None, 1, units), lambda f, c: (c, 0, 0)),
            pl.BlockSpec((None, width, units), lambda f, c: (c, 0, 1)),
            row,
        ],
        out_specs=[per, per, hid, hid, per, per, per, fixed((8, width)), fixed((chunks, 8, units))],
        out_shape=[
            tok(BF16), tok(BF16), hid_shape, hid_shape, tok(F32), tok(BF16), tok(BF16),
            jax.ShapeDtypeStruct((8, width), F32), jax.ShapeDtypeStruct((chunks, 8, units), F32),
        ],
        scratch_shapes=[pltpu.VMEM((slots, width), F32)] * 3,
        compiler_params=params(60),
        name="feed",
    )(first, mixed, cot, proj, proj_bias, gain, shift, joint, fc1_bias, joint, fc2_bias)


def middle_bwd_body(
    dq_ref, dk_ref, dv_ref, w_ref, first_ref, gs_ref, gain_ref, proj_ref, gf_ref, gto_ref, gt_ref, sums_ref
):
    slots, width = first_ref.shape
    dq, dk, dv = dq_ref[...], dk_ref[...], dv_ref[...]
    grad = dot_nt(dq, w_ref[:, :width]) + dot_nt(dk, w_ref[:, width : 2 * width]) + dot_nt(dv, w_ref[:, 2 * width :])
    unit, scale = norm_parts(first_ref[...])
    grad_first = gs_ref[...] + norm_grad(grad, unit, scale, gain_ref[...])
    gf_ref[...] = grad_first
    gto_ref[...] = grad_first.astype(BF16)
    split_positions(gt_ref, dot_nt(gto_ref[...], proj_ref[...]).astype(BF16))

    @pl.when(pl.program_id(0) == 0)
    def _():
        sums_ref[...] = jnp.zeros_like(sums_ref)

    sums_ref[0:1, :] += column_sum(grad * unit)
    sums_ref[1:2, :] += column_sum(grad)
    sums_ref[2:3, :] += column_sum(dq)
    sums_ref[3:4, :] += column_sum(dv)
    sums_ref[4:5, :] += column_sum(gto_ref[...])


def middle_bwd(dq, dk, dv, weight, first, grad_second, gain, proj, parts, share):
    frames, slots, width = first.shape
    per = lambda rows: pl.BlockSpec((None, rows, width), lambda f: (f, 0, 0))
    return pl.pallas_call(
        middle_bwd_body,
        grid=(frames,),
        in_specs=[
            per(slots), per(slots), per(slots), fixed(weight.shape), per(slots), per(slots), fixed((1, width)), fixed(proj.shape)
        ],
        out_specs=[per(slots), per(slots), by_part(parts, share, width), fixed((8, width))],
        out_shape=[
            jax.ShapeDtypeStruct(first.shape, F32), jax.ShapeDtypeStruct(first.shape, BF16),
            jax.ShapeDtypeStruct((parts, frames, share, width), BF16), jax.ShapeDtypeStruct((8, width), F32),
        ],
        compiler_params=params(60),
        name="middle_bwd",
    )(dq, dk, dv, weight, first, grad_second, gain, proj)


def norm_out_body(grad_ref, video_ref, gf_ref, gain_ref, out_ref):
    slots = video_ref.shape[0]
    unit, scale = norm_parts(video_ref[...].astype(F32))
    out_ref[...] = gf_ref[...] + norm_grad(joined_positions(grad_ref, slots).astype(F32), unit, scale, gain_ref[...])


def norm_out(grad, video, grad_first, gain):
    frames, slots, width = video.shape
    per = lambda rows: pl.BlockSpec((None, rows, width), lambda f: (f, 0, 0))
    return pl.pallas_call(
        norm_out_body,
        grid=(frames,),
        in_specs=[by_part(grad.shape[0], grad.shape[2], width), per(slots), per(slots), fixed((1, width))],
        out_specs=per(slots),
        out_shape=jax.ShapeDtypeStruct(video.shape, F32),
        compiler_params=params(),
        name="norm_out",
    )(grad, video, grad_first, gain)


def tn_body(a_ref, b_ref, out_ref):
    out_ref[...] = dot_tn(a_ref[...], b_ref[...]).astype(out_ref.dtype)


def weight_grads(pairs):
    found = []
    for a, many in pairs:
        rows, width = a.shape
        for b in many:
            found.append(
                pl.pallas_call(
                    tn_body,
                    grid=(width // WIDE,),
                    in_specs=[fixed(a.shape), pl.BlockSpec((rows, WIDE), lambda i: (0, i))],
                    out_specs=pl.BlockSpec((width, WIDE), lambda i: (0, i)),
                    out_shape=jax.ShapeDtypeStruct((width, width), BF16),
                    cost_estimate=pl.CostEstimate(
                        flops=2 * rows * width * width, bytes_accessed=4 * rows * width, transcendentals=0
                    ),
                    compiler_params=params(),
                    name="weight_grad",
                )(a, b)
            )
    return jnp.stack(found)


def fc_grads_body(normed_ref, cot_ref, gi_ref, hid_ref, out_ref):
    units = gi_ref.shape[1]
    out_ref[:, :units] = dot_tn(normed_ref[...], gi_ref[...]).astype(BF16)
    out_ref[:, units:] = dot_tn(cot_ref[...], hid_ref[...]).astype(BF16)


def fc_grads(normed, cot, grad_inner, hidden):
    chunks, frames, slots, units = hidden.shape
    width = normed.shape[-1]
    rows = frames * slots
    hid = pl.BlockSpec((None, rows, units), lambda c: (c, 0, 0))
    flat = lambda value: value.reshape(chunks, rows, units)
    return pl.pallas_call(
        fc_grads_body,
        grid=(chunks,),
        in_specs=[fixed((rows, width)), fixed((rows, width)), hid, hid],
        out_specs=pl.BlockSpec((None, width, 2 * units), lambda c: (c, 0, 0)),
        out_shape=jax.ShapeDtypeStruct((chunks, width, 2 * units), BF16),
        cost_estimate=pl.CostEstimate(
            flops=4 * rows * width * units * chunks, bytes_accessed=4 * rows * units * chunks, transcendentals=0
        ),
        compiler_params=params(),
        name="fc_grads",
    )(normed.reshape(rows, width), cot.reshape(rows, width), flat(grad_inner), flat(hidden))


MESH = pl.DeviceIdType.MESH


def bits_of(count):
    return [1 << i for i in range(count.bit_length() - 1)]


def reducible(width, planes, parts):
    power = planes >= 4 and planes & (planes - 1) == 0 and parts & (parts - 1) == 0
    return power and width % (planes * 2 * 16) == 0


def reduce_body(*refs, counts, planes, parts, has_small):
    total = sum(counts)
    inputs, refs = refs[: len(counts) + total], refs[len(counts) + total :]
    if has_small:
        small_ref, refs = refs[0], refs[1:]
    out_ref, refs = refs[0], refs[1:]
    if has_small:
        small_out, refs = refs[0], refs[1:]
    own, final = refs[:2]
    bits, hops = bits_of(planes), bits_of(parts)
    deep, steps = len(bits), len(bits) + len(hops)
    got = refs[2 : 2 + steps]
    held = refs[2 + steps : 1 + 2 * steps]
    refs = refs[1 + 2 * steps :]
    send_sem, recv_sem, out_sem = refs[:3]
    if has_small:
        small_got, small_held, small_send, small_recv = refs[3:7]
    plane, part = lax.axis_index("dp"), lax.axis_index("mp")
    place = lambda bit: (plane // bit) % 2
    swap_plane = lambda bit: {"dp": plane + bit - 2 * bit * place(bit)}
    swap_part = lambda bit: {"mp": part + bit - 2 * bit * ((part // bit) % 2)}
    partners = [swap_plane(bit) for bit in bits] + [swap_part(bit) for bit in hops]

    barrier = pltpu.get_barrier_semaphore()
    for partner in partners:
        pl.semaphore_signal(barrier, inc=1, device_id=partner, device_id_type=MESH)
    pl.semaphore_wait(barrier, len(partners))

    width = own.shape[1]
    started = []
    waiting = {}

    def send(chain, step, source, target, partner):
        copy = pltpu.make_async_remote_copy(
            src_ref=source, dst_ref=target, send_sem=send_sem.at[chain, step], recv_sem=recv_sem.at[chain, step],
            device_id=partner, device_id_type=MESH,
        )
        copy.start()
        started.append(copy)
        waiting[chain] = copy

    def order(stream):
        return bits if stream == 0 else bits[:1] + bits[1:][::-1]

    def rows_at(offset, size):
        return pl.ds(pl.multiple_of(offset, 16), size)

    def advance(chain, step):
        matrix, stream = chain // 2, chain % 2
        mine = order(stream)
        size = width // 2
        if step > 0:
            waiting[chain].wait_recv()
        if step == 0:
            half = (1 - place(mine[0])) * size + stream * (size // 2)
            send(chain, 0, own.at[matrix, rows_at(half, size // 2)], got[0].at[chain], partners_of[mine[0]])
            return
        if step <= steps:
            before = step - 1
            count = got[before].shape[1]
            if before == 0:
                kept = own[matrix, rows_at(place(mine[0]) * size + stream * (size // 2), count), :]
            elif before < deep:
                kept = held[before - 1][chain, rows_at(place(mine[before]) * count, count), :]
            else:
                kept = held[before - 1][chain]
            value = (kept.astype(F32) + got[before][chain].astype(F32)).astype(BF16)
            if step < steps:
                held[before][chain] = value
                if step < deep:
                    half = count // 2
                    source = held[before].at[chain, rows_at((1 - place(mine[step])) * half, half)]
                    send(chain, step, source, got[step].at[chain], partners_of[mine[step]])
                else:
                    send(chain, step, held[before].at[chain], got[step].at[chain], swap_part(hops[step - deep]))
                return
            spot, length = offsets(chain, deep)
            final[matrix, rows_at(spot, length), :] = value
        back = step - steps
        if back < deep:
            level = deep - back
            spot, length = offsets(chain, level)
            region = final.at[matrix, rows_at(spot, length)]
            send(chain, step, region, region, partners_of[mine[level - 1]])
        elif stream == 1:
            write = pltpu.make_async_copy(final.at[matrix], out_ref.at[matrix], out_sem.at[matrix])
            write.start()
            written.append(write)

    def offsets(chain, level):
        stream = chain % 2
        mine = order(stream)
        size = width // 2
        spot, length = place(mine[0]) * size + stream * (size // 2), size // 2
        for bit in mine[1:level]:
            length //= 2
            spot = spot + place(bit) * length
        return spot, length

    partners_of = {bit: swap_plane(bit) for bit in bits}
    written = []
    pairs = []
    at = len(counts)
    for which, count in enumerate(counts):
        for _ in range(count):
            pairs.append((inputs[which], inputs[at]))
            at += 1

    def small_step(step):
        if step > 0:
            small_wait.pop().wait_recv()
            before = small_ref[...] if step == 1 else small_held[step - 2]
            value = before + small_got[step - 1]
            if step == steps:
                small_out[...] = value
                return
            small_held[step - 1] = value
        source = small_ref if step == 0 else small_held.at[step - 1]
        copy = pltpu.make_async_remote_copy(
            src_ref=source, dst_ref=small_got.at[step], send_sem=small_send.at[step], recv_sem=small_recv.at[step],
            device_id=partners[step], device_id_type=MESH,
        )
        copy.start()
        started.append(copy)
        small_wait.append(copy)

    small_wait = []
    last = steps + deep
    for tick in range(total + last):
        if tick < total:
            a_ref, b_ref = pairs[tick]
            own[tick] = dot_tn(a_ref[...], b_ref[...]).astype(BF16)
        for matrix in range(total):
            step = tick - matrix
            if 0 <= step <= last:
                advance(2 * matrix, step)
                advance(2 * matrix + 1, step)
        if has_small and tick <= steps:
            small_step(tick)
    for copy in started:
        copy.wait_send()
    for write in written:
        write.wait()


def reduced_weight_grads(pairs, small, number):
    planes, parts = lax.axis_size("dp"), lax.axis_size("mp")
    width = pairs[0][0].shape[1]
    counts = [len(many) for _, many in pairs]
    total = sum(counts)
    if not reducible(width, planes, parts):
        grads = lax.psum(weight_grads(pairs), ("dp", "mp"))
        return (grads,) if small is None else (grads, lax.psum(small, ("dp", "mp")))
    deep, hops = len(bits_of(planes)), len(bits_of(parts))
    steps = deep + hops
    sizes = [width // 4 // (1 << i) for i in range(deep)] + [width // 4 // (1 << (deep - 1))] * hops
    chains = 2 * total
    buffers = lambda sizes: [pltpu.VMEM((chains, size, width), BF16) for size in sizes]
    operands = [a for a, _ in pairs] + [b for _, many in pairs for b in many]
    whole = pl.BlockSpec(memory_space=pltpu.VMEM)
    out_shape = [jax.ShapeDtypeStruct((total, width, width), BF16)]
    out_specs = [pl.BlockSpec(memory_space=pl.ANY)]
    scratch = (
        [pltpu.VMEM((total, width, width), BF16)] * 2 + buffers(sizes) + buffers(sizes[:-1])
        + [pltpu.SemaphoreType.DMA((chains, steps + deep))] * 2 + [pltpu.SemaphoreType.DMA((total,))]
    )
    if small is not None:
        operands.append(small)
        out_shape.append(jax.ShapeDtypeStruct(small.shape, F32))
        out_specs.append(whole)
        scratch += [pltpu.VMEM((steps,) + small.shape, F32), pltpu.VMEM((steps - 1,) + small.shape, F32)]
        scratch += [pltpu.SemaphoreType.DMA((steps,))] * 2
    rows = pairs[0][0].shape[0]
    return pl.pallas_call(
        functools.partial(reduce_body, counts=counts, planes=planes, parts=parts, has_small=small is not None),
        in_specs=[whole] * len(operands),
        out_specs=out_specs,
        out_shape=out_shape,
        scratch_shapes=scratch,
        cost_estimate=pl.CostEstimate(
            flops=2 * rows * width * width * total * 8, bytes_accessed=4 * rows * width * total * 8, transcendentals=0
        ),
        compiler_params=pltpu.CompilerParams(
            vmem_limit_bytes=60 * MIB, collective_id=number, has_side_effects=True
        ),
        name="reduced_weight_grads",
    )(*operands)


def shards(
    video,
    patch_width,
    temporal_gain,
    temporal_shift,
    temporal_qkv,
    temporal_qv_bias,
    temporal_proj,
    temporal_proj_bias,
    spatial_gain,
    spatial_shift,
    spatial_qkv,
    spatial_qv_bias,
    spatial_proj,
    spatial_proj_bias,
    mlp_gain,
    mlp_shift,
    fc1_weight,
    fc1_bias,
    fc2_weight,
    fc2_bias,
    cotangent,
):
    frames, sets, slots, width = video.shape
    units = fc1_weight.shape[1]
    parts, planes = lax.axis_size("mp"), lax.axis_size("dp")
    share = -(-slots // (parts * STEP)) * STEP
    row = lambda value: value.astype(F32).reshape(1, -1)
    video = video.reshape(frames * sets, slots, width)
    cot = cotangent.reshape(frames * sets, slots, width)

    joint = jnp.concatenate([fc1_weight, fc2_weight.T], axis=1)
    piece = width // planes
    own = lax.dynamic_slice_in_dim(joint, lax.axis_index("dp") * piece, piece, 0)
    bias_rows = jnp.pad(fc1_bias.reshape(1, units), ((0, 15), (0, units)))
    own = jnp.concatenate([own, bias_rows], axis=0)[None]

    def exchange(value):
        return lax.all_to_all(value, "mp", split_axis=0, concat_axis=0, tiled=True)

    by_position = lambda value: value.reshape(parts * frames, share, width)
    by_device = lambda value: value.reshape(parts, frames, share, width)
    normed_in = norm_in(video, row(temporal_gain), row(temporal_shift), parts, share)
    x = by_position(exchange(normed_in))
    own, x = lax.optimization_barrier((own, x))
    column = lax.all_gather(own, "mp", axis=0, tiled=True)
    tq, tk, tv, time_mixed = temporal_fwd(x, temporal_qkv, row(temporal_qv_bias))
    column, time_mixed = lax.optimization_barrier((column, time_mixed))
    fb1 = column[:, piece : piece + 1, :units].astype(F32)
    joint = lax.all_gather(column[:, :piece], "dp", axis=1, tiled=True)
    time_back = exchange(by_device(time_mixed))

    first, normed_mid, space_qkv = middle(
        time_back, video, temporal_proj, row(temporal_proj_bias), row(spatial_gain), row(spatial_shift), spatial_qkv,
        row(spatial_qv_bias),
    )
    space_mixed, lse = spatial_fwd(patch_width, space_qkv, frames, slots)

    output, normed_out, hidden, grad_inner, grad_second, grad_space_out, grad_space, feed_sums, unit_sums = feed(
        first, space_mixed, cot, spatial_proj, row(spatial_proj_bias), row(mlp_gain), row(mlp_shift), joint, fb1,
        row(fc2_bias),
    )
    fc_part = fc_grads(normed_out, cot, grad_inner, hidden)
    fc_part = lax.psum_scatter(fc_part, "dp", scatter_dimension=1, tiled=True)
    fc_part = lax.psum_scatter(fc_part, "mp", scatter_dimension=0, tiled=True)[0].astype(F32)
    fc1_weight_grad = fc_part[:, :units]
    fc2_weight_grad = fc_part[:, units:].T

    dq, dk, dv = spatial_bwd(patch_width, space_qkv, space_mixed, lse, grad_space, frames, slots)
    grad_first, grad_time_out, grad_time, mid_sums = middle_bwd(
        dq, dk, dv, spatial_qkv, first, grad_second, row(spatial_gain), temporal_proj, parts, share
    )
    flat = lambda value: value.reshape(-1, width)
    grad_slot = exchange(grad_time)
    time_rows = jnp.swapaxes(time_back, 0, 1).reshape(frames, parts * share, width)[:, :slots]
    (early,) = reduced_weight_grads(
        [
            (flat(normed_mid), [flat(dq), flat(dk), flat(dv)]),
            (flat(space_mixed), [flat(grad_space_out)]),
            (flat(time_rows), [flat(grad_time_out)]),
        ],
        None,
        1,
    )

    gq, gk, gv, grad_x, bias_sums, norm_sums = temporal_bwd(
        x, tq, tk, tv, by_position(grad_slot), temporal_qkv, row(temporal_gain), row(temporal_shift)
    )
    grad_in = exchange(by_device(grad_x))
    small = jnp.concatenate(
        [unit_sums[:, 0, :].reshape(-1, width), feed_sums[:4], mid_sums[:5], bias_sums[:2], norm_sums[:2]], axis=0
    )
    small = jnp.pad(small, ((0, -small.shape[0] % 8), (0, 0)))
    late, small = reduced_weight_grads([(flat(x), [flat(gq), flat(gk), flat(gv)])], small, 2)
    video_grad = norm_out(grad_in, video, grad_first, row(temporal_gain))
    count = parts * units // width
    fc1_bias_grad = small[:count].reshape(-1)
    (
        mlp_gain_grad, mlp_shift_grad, spatial_proj_bias_grad, fc2_bias_grad,
        spatial_gain_grad, spatial_shift_grad, space_q_sum, space_v_sum, temporal_proj_bias_grad,
        time_q_sum, time_v_sum, temporal_gain_grad, temporal_shift_grad,
    ) = [small[count + i] for i in range(13)]
    wide = lambda parts_: jnp.concatenate([part.astype(F32) for part in parts_], axis=1)
    return (
        output.reshape(frames, sets, slots, width),
        video_grad.reshape(frames, sets, slots, width),
        temporal_gain_grad,
        temporal_shift_grad,
        wide([late[0], late[1], late[2]]),
        jnp.concatenate([time_q_sum, time_v_sum]),
        early[4].astype(F32),
        temporal_proj_bias_grad,
        spatial_gain_grad,
        spatial_shift_grad,
        wide([early[0], early[1], early[2]]),
        jnp.concatenate([space_q_sum, space_v_sum]),
        early[3].astype(F32),
        spatial_proj_bias_grad,
        mlp_gain_grad,
        mlp_shift_grad,
        fc1_weight_grad,
        fc1_bias_grad,
        fc2_weight_grad,
        fc2_bias_grad,
    )


def solution(mesh):
    tokens = P("mp", "dp", None, None)
    return jax.shard_map(
        shards,
        mesh=mesh,
        in_specs=(tokens, P("dp")) + (P(),) * 14 + (P(None, "mp"), P("mp"), P("mp", None), P(), tokens),
        out_specs=(tokens, tokens) + (P(),) * 14 + (P("dp", "mp"), P(), P("mp", "dp"), P()),
        check_vma=False,
    )
```

```python
import functools
import jax
import jax.numpy as jnp
from jax import lax
from jax.experimental import pallas as pl
from jax.experimental.pallas import tpu as pltpu
from jax.sharding import PartitionSpec as P

HEADS = 12
HEAD_DIM = 64
GROUP = 4
WIDE = GROUP * HEAD_DIM
EPSILON = 1e-06
F32 = jnp.float32
BF16 = jnp.bfloat16
MIB = 1 << 20


def params(mib=56):
    return pltpu.CompilerParams(vmem_limit_bytes=mib * MIB)


def dot(a, b):
    return jnp.dot(a, b, preferred_element_type=F32)


def dot_nt(a, b):
    return lax.dot_general(a, b, (((1,), (1,)), ((), ())), preferred_element_type=F32)


def dot_tn(a, b):
    return lax.dot_general(a, b, (((0,), (0,)), ((), ())), preferred_element_type=F32)


def head_lanes(rows, head, dtype):
    lane = lax.broadcasted_iota(jnp.int32, (rows, WIDE), 1)
    return (lane // HEAD_DIM == head).astype(dtype)


def windows(slots, clips, rows):
    size = slots // clips
    found = []
    for start in range(0, slots, rows):
        stop = min(start + rows, slots)
        low = start // size * size // 16 * 16
        high = min(-(-(-(-stop // size) * size) // 16) * 16, slots)
        found.append((start, stop, low, high))
    return found


def spatial_fwd_body(width_ref, q_ref, k_ref, v_ref, o_ref, l_ref, *, slots, rows, narrow):
    def attend(chunks, size):
        stats = []
        for start, stop, low, high in chunks:
            count = stop - start
            q = q_ref[start:stop, :]
            k = k_ref[low:high, :]
            v = v_ref[low:high, :]
            if size < slots:
                query_clip = (lax.broadcasted_iota(jnp.int32, (count, high - low), 0) + start) // size
                key_clip = (lax.broadcasted_iota(jnp.int32, (count, high - low), 1) + low) // size
                same = query_clip == key_clip
            total = jnp.zeros((count, WIDE), F32)
            lse = jnp.zeros((count, 128), F32)
            lane = lax.broadcasted_iota(jnp.int32, (count, 128), 1)
            for head in range(GROUP):
                s = dot_nt(q * head_lanes(count, head, BF16), k)
                if size < slots:
                    s = jnp.where(same, s, -1e30)
                top = jnp.max(s, axis=1, keepdims=True)
                e = jnp.exp(s - top)
                norm = jnp.sum(e, axis=1, keepdims=True)
                o = dot(e.astype(BF16), v)
                total = total + o * (head_lanes(count, head, F32) / norm)
                lse = jnp.where(lane == head, top + jnp.log(norm), lse)
            o_ref[start:stop, :] = total.astype(BF16)
            stats.append(lse)
        l_ref[...] = jnp.concatenate(stats, axis=0).T[:8, :]

    wide = width_ref[0] == slots

    @pl.when(wide)
    def _():
        attend(windows(slots, 1, rows or slots), slots)

    @pl.when(jnp.logical_not(wide))
    def _():
        attend(windows(slots, 4, narrow), slots // 4)


def spatial_fwd(width, qkv, frames, slots, rows=None, narrow=256):
    groups = HEADS // GROUP
    qkv = qkv.reshape(frames, slots, -1)
    spec = lambda part: pl.BlockSpec((None, slots, WIDE), lambda f, g, w: (f, 0, part * groups + g))
    out = pl.pallas_call(
        functools.partial(spatial_fwd_body, slots=slots, rows=rows, narrow=narrow),
        grid_spec=pltpu.PrefetchScalarGridSpec(
            num_scalar_prefetch=1,
            grid=(frames, groups),
            in_specs=[spec(0), spec(1), spec(2)],
            out_specs=[
                pl.BlockSpec((None, slots, WIDE), lambda f, g, w: (f, 0, g)),
                pl.BlockSpec((None, None, 8, slots), lambda f, g, w: (f, g, 0, 0)),
            ],
        ),
        out_shape=[
            jax.ShapeDtypeStruct((frames, slots, HEADS * HEAD_DIM), BF16),
            jax.ShapeDtypeStruct((frames, groups, 8, slots), F32),
        ],
        compiler_params=params(),
        name="spatial_fwd",
    )(width, qkv, qkv, qkv)
    return out


def spatial_bwd_body(width_ref, q_ref, k_ref, v_ref, o_ref, l_ref, g_ref, dq_ref, dk_ref, dv_ref, dqt, *, slots, rows, narrow):
    prod = g_ref[...].astype(F32) * o_ref[...].astype(F32)
    high_part = prod.astype(BF16)
    low_part = (prod - high_part.astype(F32)).astype(BF16)
    lane = lax.broadcasted_iota(jnp.int32, (8, WIDE), 1)
    row = lax.broadcasted_iota(jnp.int32, (8, WIDE), 0)
    picks = (lane // HEAD_DIM == row).astype(BF16)
    delta = dot_nt(picks, high_part) + dot_nt(picks, low_part)

    def attend(chunks, size):
        dqt[...] = jnp.zeros_like(dqt)
        kt = k_ref[...].T
        for start, stop, low, high in chunks:
            count = stop - start
            k = k_ref[start:stop, :]
            v = v_ref[start:stop, :]
            q = q_ref[low:high, :]
            g = g_ref[low:high, :]
            if size < slots:
                key_clip = (lax.broadcasted_iota(jnp.int32, (count, high - low), 0) + start) // size
                query_clip = (lax.broadcasted_iota(jnp.int32, (count, high - low), 1) + low) // size
                same = query_clip == key_clip
            dk = jnp.zeros((count, WIDE), F32)
            dv = jnp.zeros((count, WIDE), F32)
            for head in range(GROUP):
                mask = head_lanes(count, head, BF16)
                s = dot_nt(k * mask, q)
                p = jnp.exp(s - l_ref[head : head + 1, low:high])
                if size < slots:
                    p = jnp.where(same, p, 0.0)
                dp = dot_nt(v * mask, g)
                ds = (p * (dp - delta[head : head + 1, low:high])).astype(BF16)
                keep = head_lanes(count, head, F32)
                dv = dv + dot(p.astype(BF16), g) * keep
                dk = dk + dot(ds, q) * keep
                span = slice(head * HEAD_DIM, (head + 1) * HEAD_DIM)
                dqt[span, low:high] += dot(kt[span, start:stop], ds)
            dk_ref[start:stop, :] = dk.astype(BF16)
            dv_ref[start:stop, :] = dv.astype(BF16)
        dq_ref[...] = (dqt[...] * HEAD_DIM**-0.5).T.astype(BF16)

    wide = width_ref[0] == slots

    @pl.when(wide)
    def _():
        attend(windows(slots, 1, rows or slots), slots)

    @pl.when(jnp.logical_not(wide))
    def _():
        attend(windows(slots, 4, narrow), slots // 4)


def spatial_bwd(width, qkv, mixed, lse, grad, frames, slots, rows=None, narrow=208):
    groups = HEADS // GROUP
    width_all = HEADS * HEAD_DIM
    qkv = qkv.reshape(frames, slots, -1)
    spec = lambda part: pl.BlockSpec((None, slots, WIDE), lambda f, g, w: (f, 0, part * groups + g))
    one = pl.BlockSpec((None, slots, WIDE), lambda f, g, w: (f, 0, g))
    out = pl.pallas_call(
        functools.partial(spatial_bwd_body, slots=slots, rows=rows, narrow=narrow),
        grid_spec=pltpu.PrefetchScalarGridSpec(
            num_scalar_prefetch=1,
            grid=(frames, groups),
            in_specs=[
                spec(0), spec(1), spec(2), one,
                pl.BlockSpec((None, None, 8, slots), lambda f, g, w: (f, g, 0, 0)), one,
            ],
            out_specs=[one, one, one],
            scratch_shapes=[pltpu.VMEM((WIDE, slots), F32)],
        ),
        out_shape=[jax.ShapeDtypeStruct((frames, slots, width_all), BF16)] * 3,
        compiler_params=params(),
        name="spatial_bwd",
    )(width, qkv, qkv, qkv, mixed, lse, grad)
    return out


def fixed(shape):
    return pl.BlockSpec(shape, lambda *_: (0,) * len(shape))


def norm_parts(value):
    centered = value - jnp.mean(value, axis=-1, keepdims=True)
    scale = lax.rsqrt(jnp.mean(centered * centered, axis=-1, keepdims=True) + EPSILON)
    return centered * scale, scale


def norm_grad(grad, unit, scale, gain):
    inner = grad * gain
    return scale * (
        inner
        - jnp.mean(inner, axis=-1, keepdims=True)
        - unit * jnp.mean(inner * unit, axis=-1, keepdims=True)
    )


def column_sum(value):
    return jnp.sum(value.astype(F32), axis=0, keepdims=True)


def by_part(parts, share, width):
    return pl.BlockSpec((parts, None, share, width), lambda f: (0, f, 0, 0))


def norm_in_body(video_ref, gain_ref, shift_ref, out_ref):
    unit, _ = norm_parts(video_ref[...].astype(F32))
    split_positions(out_ref, (unit * gain_ref[...] + shift_ref[...]).astype(BF16))


def split_positions(out_ref, value):
    parts, share, width = out_ref.shape
    slots = value.shape[0]
    for part in range(parts):
        start = part * share
        count = min(max(slots - start, 0), share)
        if count > 0:
            out_ref[part, :count, :] = value[start : start + count, :]
        if count < share:
            out_ref[part, count:, :] = jnp.zeros((share - count, width), value.dtype)


def joined_positions(ref, slots):
    parts, share, width = ref.shape
    return ref[...].reshape(parts * share, width)[:slots, :]


def norm_in(video, gain, shift, parts, share):
    frames, slots, width = video.shape
    return pl.pallas_call(
        norm_in_body,
        grid=(frames,),
        in_specs=[pl.BlockSpec((None, slots, width), lambda f: (f, 0, 0)), fixed((1, width)), fixed((1, width))],
        out_specs=by_part(parts, share, width),
        out_shape=jax.ShapeDtypeStruct((parts, frames, share, width), BF16),
        compiler_params=params(),
        name="norm_in",
    )(video, gain, shift)


STEP = 16


def stacked(block, rows):
    return jnp.concatenate([block * head_lanes(rows, head, BF16) for head in range(GROUP)], axis=0)


def temporal_fwd_body(x_ref, wq_ref, wk_ref, wv_ref, bq_ref, bv_ref, q_ref, k_ref, v_ref, o_ref):
    frames, slots, width = x_ref.shape
    x = x_ref[...].reshape(frames * slots, width)
    shape = (frames, slots, WIDE)
    q_ref[...] = ((dot(x, wq_ref[...]) + bq_ref[...]) * HEAD_DIM**-0.5).astype(BF16).reshape(shape)
    k_ref[...] = dot(x, wk_ref[...]).astype(BF16).reshape(shape)
    v_ref[...] = (dot(x, wv_ref[...]) + bv_ref[...]).astype(BF16).reshape(shape)
    rows = frames * STEP
    row = lax.broadcasted_iota(jnp.int32, (rows, rows), 0)
    col = lax.broadcasted_iota(jnp.int32, (rows, rows), 1)
    same = row % STEP == col % STEP
    for step in range(slots // STEP):
        part = slice(step * STEP, (step + 1) * STEP)
        q = q_ref[:, part, :].reshape(rows, WIDE)
        keys = stacked(k_ref[:, part, :].reshape(rows, WIDE), rows)
        values = stacked(v_ref[:, part, :].reshape(rows, WIDE), rows)
        scores = dot_nt(q, keys)
        mixing = []
        for head in range(GROUP):
            s = jnp.where(same, scores[:, head * rows : (head + 1) * rows], -1e30)
            e = jnp.exp(s - jnp.max(s, axis=1, keepdims=True))
            mixing.append((e / jnp.sum(e, axis=1, keepdims=True)).astype(BF16))
        o = dot(jnp.concatenate(mixing, axis=1), values)
        o_ref[:, part, :] = o.astype(BF16).reshape(frames, STEP, WIDE)


def temporal_fwd(x, weight, bias):
    frames, slots, width = x.shape
    groups = width // WIDE
    w = lambda part: pl.BlockSpec((width, WIDE), lambda g: (0, part * groups + g))
    b = lambda part: pl.BlockSpec((1, WIDE), lambda g: (0, part * groups + g))
    one = pl.BlockSpec((frames, slots, WIDE), lambda g: (0, 0, g))
    return pl.pallas_call(
        temporal_fwd_body,
        grid=(groups,),
        in_specs=[fixed(x.shape), w(0), w(1), w(2), b(0), b(1)],
        out_specs=[one] * 4,
        out_shape=[jax.ShapeDtypeStruct(x.shape, BF16)] * 4,
        compiler_params=params(),
        name="temporal_fwd",
    )(x, weight, weight, weight, bias, bias)


def temporal_bwd_body(
    x_ref, q_ref, k_ref, v_ref, g_ref, wq_ref, wk_ref, wv_ref, gain_ref, shift_ref,
    dq_ref, dk_ref, dv_ref, dx_ref, sums_ref, norm_ref, total_ref,
):
    frames, slots, width = x_ref.shape
    rows = frames * STEP
    row = lax.broadcasted_iota(jnp.int32, (rows, rows), 0)
    col = lax.broadcasted_iota(jnp.int32, (rows, rows), 1)
    same = row % STEP == col % STEP
    shape = (frames, STEP, WIDE)
    for step in range(slots // STEP):
        part = slice(step * STEP, (step + 1) * STEP)
        k = k_ref[:, part, :].reshape(rows, WIDE)
        v = v_ref[:, part, :].reshape(rows, WIDE)
        queries = stacked(q_ref[:, part, :].reshape(rows, WIDE), rows)
        grads = stacked(g_ref[:, part, :].reshape(rows, WIDE), rows)
        scores = dot_nt(k, queries)
        grad_mixing = dot_nt(v, grads)
        mixing, grad_scores = [], []
        for head in range(GROUP):
            span = slice(head * rows, (head + 1) * rows)
            s = jnp.where(same, scores[:, span], -1e30)
            e = jnp.exp(s - jnp.max(s, axis=0, keepdims=True))
            p = e / jnp.sum(e, axis=0, keepdims=True)
            gp = grad_mixing[:, span]
            ds = p * (gp - jnp.sum(p * gp, axis=0, keepdims=True))
            mixing.append(p.astype(BF16))
            grad_scores.append(ds.astype(BF16))
        grad_scores = jnp.concatenate(grad_scores, axis=1)
        dv_ref[:, part, :] = dot(jnp.concatenate(mixing, axis=1), grads).astype(BF16).reshape(shape)
        dk_ref[:, part, :] = dot(grad_scores, queries).astype(BF16).reshape(shape)
        spread = dot_tn(grad_scores, k)
        dq = jnp.zeros((rows, WIDE), F32)
        for head in range(GROUP):
            dq = dq + spread[head * rows : (head + 1) * rows] * head_lanes(rows, head, F32)
        dq_ref[:, part, :] = (dq * HEAD_DIM**-0.5).astype(BF16).reshape(shape)
    flat = (frames * slots, WIDE)
    dq, dk, dv = dq_ref[...].reshape(flat), dk_ref[...].reshape(flat), dv_ref[...].reshape(flat)
    sums_ref[...] = jnp.concatenate([column_sum(dq), column_sum(dv), jnp.zeros((6, WIDE), F32)], axis=0)
    update = dot_nt(dq, wq_ref[...]) + dot_nt(dk, wk_ref[...]) + dot_nt(dv, wv_ref[...])
    group = pl.program_id(0)

    @pl.when(group == 0)
    def _():
        total_ref[...] = update

    @pl.when(group > 0)
    def _():
        total_ref[...] += update

    @pl.when(group == pl.num_programs(0) - 1)
    def _():
        total = total_ref[...]
        dx_ref[...] = total.astype(BF16).reshape(frames, slots, width)
        x = x_ref[...].reshape(frames * slots, width).astype(F32)
        shift_grad = column_sum(total)
        gain_grad = (column_sum(total * x) - shift_ref[...] * shift_grad) / gain_ref[...]
        norm_ref[...] = jnp.concatenate([gain_grad, shift_grad, jnp.zeros((6, width), F32)], axis=0)


def temporal_bwd(x, q, k, v, grad, weight, gain, shift):
    frames, slots, width = x.shape
    groups = width // WIDE
    w = lambda part: pl.BlockSpec((width, WIDE), lambda g: (0, part * groups + g))
    one = pl.BlockSpec((frames, slots, WIDE), lambda g: (0, 0, g))
    return pl.pallas_call(
        temporal_bwd_body,
        grid=(groups,),
        in_specs=[fixed(x.shape), one, one, one, one, w(0), w(1), w(2), fixed((1, width)), fixed((1, width))],
        out_specs=[one, one, one, fixed(x.shape), pl.BlockSpec((8, WIDE), lambda g: (0, g)), fixed((8, width))],
        out_shape=[jax.ShapeDtypeStruct(x.shape, BF16)] * 4 + [jax.ShapeDtypeStruct((8, width), F32)] * 2,
        scratch_shapes=[pltpu.VMEM((frames * slots, width), F32)],
        compiler_params=params(),
        name="temporal_bwd",
    )(x, q, k, v, grad, weight, weight, weight, gain, shift)


def middle_body(mixed_ref, video_ref, proj_ref, pb_ref, gain_ref, shift_ref, w_ref, bias_ref, first_ref, normed_ref, qkv_ref):
    slots, width = video_ref.shape
    first = video_ref[...].astype(F32) + (dot(joined_positions(mixed_ref, slots), proj_ref[...]) + pb_ref[...])
    first_ref[...] = first
    unit, _ = norm_parts(first)
    normed_ref[...] = (unit * gain_ref[...] + shift_ref[...]).astype(BF16)
    normed = normed_ref[...]
    q = dot(normed, w_ref[:, :width]) + bias_ref[:, :width]
    qkv_ref[:, :width] = (q * HEAD_DIM**-0.5).astype(BF16)
    qkv_ref[:, width : 2 * width] = dot(normed, w_ref[:, width : 2 * width]).astype(BF16)
    qkv_ref[:, 2 * width :] = (dot(normed, w_ref[:, 2 * width :]) + bias_ref[:, width:]).astype(BF16)


def middle(mixed, video, proj, proj_bias, gain, shift, weight, bias):
    frames, slots, width = video.shape
    per = lambda rows, cols: pl.BlockSpec((None, rows, cols), lambda f: (f, 0, 0))
    return pl.pallas_call(
        middle_body,
        grid=(frames,),
        in_specs=[
            by_part(mixed.shape[0], mixed.shape[2], width), per(slots, width), fixed(proj.shape), fixed((1, width)), fixed((1, width)),
            fixed((1, width)), fixed(weight.shape), fixed((1, 2 * width)),
        ],
        out_specs=[per(slots, width), per(slots, width), per(slots, 3 * width)],
        out_shape=[
            jax.ShapeDtypeStruct(video.shape, F32),
            jax.ShapeDtypeStruct(video.shape, BF16),
            jax.ShapeDtypeStruct((frames, slots, 3 * width), BF16),
        ],
        compiler_params=params(),
        name="middle",
    )(mixed, video, proj, proj_bias, gain, shift, weight, bias)


def gelu_both(value):
    half = 0.5 * (1.0 + lax.erf(value * 0.7071067811865476))
    density = jnp.exp(-0.5 * value * value) * 0.3989422804014327
    return value * half, half + value * density


def feed_body(
    first_ref, mixed_ref, cot_ref, proj_ref, pb_ref, gain_ref, shift_ref, fc1_ref, fb1_ref, fc2_ref, fb2_ref,
    out_ref, normed_ref, hidden_ref, gi_ref, gs_ref, gso_ref, gspace_ref, sums_ref, unitsum_ref,
    second, branch, gnorm, *, sub,
):
    frame, chunk = pl.program_id(0), pl.program_id(1)
    slots, width = first_ref.shape
    units = fc1_ref.shape[1]

    @pl.when(chunk == 0)
    def _():
        value = first_ref[...] + (dot(mixed_ref[...], proj_ref[...]) + pb_ref[...])
        second[...] = value
        unit, _ = norm_parts(value)
        normed_ref[...] = (unit * gain_ref[...] + shift_ref[...]).astype(BF16)
        branch[...] = jnp.zeros_like(branch)
        gnorm[...] = jnp.zeros_like(gnorm)

    @pl.when(jnp.logical_and(frame == 0, chunk == 0))
    def _():
        sums_ref[...] = jnp.zeros_like(sums_ref)
        unitsum_ref[...] = jnp.zeros_like(unitsum_ref)

    normed = normed_ref[...]
    cot = cot_ref[...]
    for start in range(0, units, sub):
        span = slice(start, start + sub)
        inner = dot(normed, fc1_ref[:, span]) + fb1_ref[0:1, span]
        grad_hidden = dot(cot, fc2_ref[:, span])
        act, slope = gelu_both(inner)
        hidden_ref[:, span] = act.astype(BF16)
        gi_ref[:, span] = (grad_hidden * slope).astype(BF16)
    branch[...] += dot_nt(hidden_ref[...], fc2_ref[...])
    gnorm[...] += dot_nt(gi_ref[...], fc1_ref[...])
    unitsum_ref[chunk, 0:1, :] += column_sum(gi_ref[...])

    @pl.when(chunk == pl.num_programs(1) - 1)
    def _():
        value = second[...]
        out_ref[...] = (value + (branch[...] + fb2_ref[...])).astype(BF16)
        unit, scale = norm_parts(value)
        grad = gnorm[...]
        cot_full = cot_ref[...].astype(F32)
        grad_second = cot_full + norm_grad(grad, unit, scale, gain_ref[...])
        gs_ref[...] = grad_second
        gso_ref[...] = grad_second.astype(BF16)
        gspace_ref[...] = dot_nt(gso_ref[...], proj_ref[...]).astype(BF16)
        sums_ref[0:1, :] += column_sum(grad * unit)
        sums_ref[1:2, :] += column_sum(grad)
        sums_ref[2:3, :] += column_sum(gso_ref[...])
        sums_ref[3:4, :] += column_sum(cot_full)


def feed(first, mixed, cot, proj, proj_bias, gain, shift, joint, fc1_bias, fc2_bias, sub=None):
    frames, slots, width = first.shape
    chunks, _, units = fc1_bias.shape
    sub = sub or units
    per = pl.BlockSpec((None, slots, width), lambda f, c: (f, 0, 0))
    row = fixed((1, width))
    hid = pl.BlockSpec((None, None, slots, units), lambda f, c: (c, f, 0, 0))
    hid_shape = jax.ShapeDtypeStruct((chunks, frames, slots, units), BF16)
    tok = lambda dtype: jax.ShapeDtypeStruct(first.shape, dtype)
    return pl.pallas_call(
        functools.partial(feed_body, sub=sub),
        grid=(frames, chunks),
        in_specs=[
            per, per, per, fixed(proj.shape), row, row, row,
            pl.BlockSpec((None, width, units), lambda f, c: (c, 0, 0)),
            pl.BlockSpec((None, 1, units), lambda f, c: (c, 0, 0)),
            pl.BlockSpec((None, width, units), lambda f, c: (c, 0, 1)),
            row,
        ],
        out_specs=[per, per, hid, hid, per, per, per, fixed((8, width)), fixed((chunks, 8, units))],
        out_shape=[
            tok(BF16), tok(BF16), hid_shape, hid_shape, tok(F32), tok(BF16), tok(BF16),
            jax.ShapeDtypeStruct((8, width), F32), jax.ShapeDtypeStruct((chunks, 8, units), F32),
        ],
        scratch_shapes=[pltpu.VMEM((slots, width), F32)] * 3,
        compiler_params=params(60),
        name="feed",
    )(first, mixed, cot, proj, proj_bias, gain, shift, joint, fc1_bias, joint, fc2_bias)


def middle_bwd_body(
    dq_ref, dk_ref, dv_ref, w_ref, first_ref, gs_ref, gain_ref, proj_ref, gf_ref, gto_ref, gt_ref, sums_ref
):
    slots, width = first_ref.shape
    dq, dk, dv = dq_ref[...], dk_ref[...], dv_ref[...]
    grad = dot_nt(dq, w_ref[:, :width]) + dot_nt(dk, w_ref[:, width : 2 * width]) + dot_nt(dv, w_ref[:, 2 * width :])
    unit, scale = norm_parts(first_ref[...])
    grad_first = gs_ref[...] + norm_grad(grad, unit, scale, gain_ref[...])
    gf_ref[...] = grad_first
    gto_ref[...] = grad_first.astype(BF16)
    split_positions(gt_ref, dot_nt(gto_ref[...], proj_ref[...]).astype(BF16))

    @pl.when(pl.program_id(0) == 0)
    def _():
        sums_ref[...] = jnp.zeros_like(sums_ref)

    sums_ref[0:1, :] += column_sum(grad * unit)
    sums_ref[1:2, :] += column_sum(grad)
    sums_ref[2:3, :] += column_sum(dq)
    sums_ref[3:4, :] += column_sum(dv)
    sums_ref[4:5, :] += column_sum(gto_ref[...])


def middle_bwd(dq, dk, dv, weight, first, grad_second, gain, proj, parts, share):
    frames, slots, width = first.shape
    per = lambda rows: pl.BlockSpec((None, rows, width), lambda f: (f, 0, 0))
    return pl.pallas_call(
        middle_bwd_body,
        grid=(frames,),
        in_specs=[
            per(slots), per(slots), per(slots), fixed(weight.shape), per(slots), per(slots), fixed((1, width)), fixed(proj.shape)
        ],
        out_specs=[per(slots), per(slots), by_part(parts, share, width), fixed((8, width))],
        out_shape=[
            jax.ShapeDtypeStruct(first.shape, F32), jax.ShapeDtypeStruct(first.shape, BF16),
            jax.ShapeDtypeStruct((parts, frames, share, width), BF16), jax.ShapeDtypeStruct((8, width), F32),
        ],
        compiler_params=params(60),
        name="middle_bwd",
    )(dq, dk, dv, weight, first, grad_second, gain, proj)


def norm_out_body(grad_ref, video_ref, gf_ref, gain_ref, out_ref):
    slots = video_ref.shape[0]
    unit, scale = norm_parts(video_ref[...].astype(F32))
    out_ref[...] = gf_ref[...] + norm_grad(joined_positions(grad_ref, slots).astype(F32), unit, scale, gain_ref[...])


def norm_out(grad, video, grad_first, gain):
    frames, slots, width = video.shape
    per = lambda rows: pl.BlockSpec((None, rows, width), lambda f: (f, 0, 0))
    return pl.pallas_call(
        norm_out_body,
        grid=(frames,),
        in_specs=[by_part(grad.shape[0], grad.shape[2], width), per(slots), per(slots), fixed((1, width))],
        out_specs=per(slots),
        out_shape=jax.ShapeDtypeStruct(video.shape, F32),
        compiler_params=params(),
        name="norm_out",
    )(grad, video, grad_first, gain)


def tn_body(a_ref, b_ref, out_ref):
    out_ref[...] = dot_tn(a_ref[...], b_ref[...]).astype(out_ref.dtype)


def weight_grads(pairs):
    found = []
    for a, many in pairs:
        rows, width = a.shape
        for b in many:
            found.append(
                pl.pallas_call(
                    tn_body,
                    grid=(width // WIDE,),
                    in_specs=[fixed(a.shape), pl.BlockSpec((rows, WIDE), lambda i: (0, i))],
                    out_specs=pl.BlockSpec((width, WIDE), lambda i: (0, i)),
                    out_shape=jax.ShapeDtypeStruct((width, width), BF16),
                    cost_estimate=pl.CostEstimate(
                        flops=2 * rows * width * width, bytes_accessed=4 * rows * width, transcendentals=0
                    ),
                    compiler_params=params(),
                    name="weight_grad",
                )(a, b)
            )
    return found


def fc_grads_body(normed_ref, cot_ref, gi_ref, hid_ref, out_ref):
    units = gi_ref.shape[1]
    out_ref[:, :units] = dot_tn(normed_ref[...], gi_ref[...]).astype(BF16)
    out_ref[:, units:] = dot_tn(cot_ref[...], hid_ref[...]).astype(BF16)


def fc_grads(normed, cot, grad_inner, hidden):
    chunks, frames, slots, units = hidden.shape
    width = normed.shape[-1]
    rows = frames * slots
    hid = pl.BlockSpec((None, rows, units), lambda c: (c, 0, 0))
    flat = lambda value: value.reshape(chunks, rows, units)
    return pl.pallas_call(
        fc_grads_body,
        grid=(chunks,),
        in_specs=[fixed((rows, width)), fixed((rows, width)), hid, hid],
        out_specs=pl.BlockSpec((None, width, 2 * units), lambda c: (c, 0, 0)),
        out_shape=jax.ShapeDtypeStruct((chunks, width, 2 * units), BF16),
        cost_estimate=pl.CostEstimate(
            flops=4 * rows * width * units * chunks, bytes_accessed=4 * rows * units * chunks, transcendentals=0
        ),
        compiler_params=params(),
        name="fc_grads",
    )(normed.reshape(rows, width), cot.reshape(rows, width), flat(grad_inner), flat(hidden))


MESH = pl.DeviceIdType.MESH
EARLY_GAP = 3.0
HOP = 4.0


def bits_of(count):
    return [1 << i for i in range(count.bit_length() - 1)]


def reducible(width, planes, parts):
    return parts == 4 and planes >= 4 and planes & (planes - 1) == 0 and width % (planes * 2 * 16) == 0


class Ring:
    def __init__(self, planes):
        self.bits = bits_of(planes)
        self.deep = len(self.bits)
        self.plane, self.part = lax.axis_index("dp"), lax.axis_index("mp")
        self.by_bit = {bit: {"dp": self.plane + bit - 2 * bit * self.place(bit)} for bit in self.bits}
        self.beside = {"mp": self.part + 1 - 2 * (self.part % 2)}
        self.across = {"mp": 3 - self.part}
        self.third = {"mp": (self.part + 2) % 4}
        self.inner = ((self.part + 1) // 2) % 2 == 1
        self.outer = ((self.part + 1) // 2) % 2 == 0
        self.started = []

    def place(self, bit):
        return (self.plane // bit) % 2

    def greet(self):
        partners = [self.by_bit[bit] for bit in self.bits] + [self.beside, self.across, self.third]
        barrier = pltpu.get_barrier_semaphore()
        for partner in partners:
            pl.semaphore_signal(barrier, inc=1, device_id=partner, device_id_type=MESH)
        pl.semaphore_wait(barrier, len(partners))

    def order(self, stream):
        return self.bits if stream == 0 else self.bits[:1] + self.bits[1:][::-1]

    def send(self, source, target, sems, at, partner, when=None):
        send_sem, recv_sem = sems
        copy = pltpu.make_async_remote_copy(
            src_ref=source, dst_ref=target, send_sem=send_sem.at[at], recv_sem=recv_sem.at[at],
            device_id=partner, device_id_type=MESH,
        )
        if when is None:
            copy.start()
        else:
            pl.when(when)(copy.start)
        self.started.append((when, copy))
        return copy

    def finish(self):
        for when, copy in self.started:
            if when is None:
                copy.wait_send()
            else:
                pl.when(when)(copy.wait_send)

    def rows(self, chain, level, width):
        stream = chain % 2
        mine = self.order(stream)
        size = width // 2
        spot, length = self.place(mine[0]) * size + stream * (size // 2), size // 2
        for bit in mine[1:level]:
            length //= 2
            spot = spot + self.place(bit) * length
        return spot, length


def rows_at(offset, size):
    return pl.ds(pl.multiple_of(offset, 16), size)


class Reduction:
    def __init__(self, ring, own, got, line, piece, out, sems, back_sems, out_sem):
        self.ring, self.own, self.got, self.line, self.piece, self.sems = ring, own, got, line, piece, sems
        self.out, self.back_sems, self.out_sem = out, back_sems, out_sem
        self.width = own.shape[1]
        self.waiting = {}
        self.local = {}
        self.steps = 2 * ring.deep + 4

    def back(self, chain, step):
        ring, matrix = self.ring, chain // 2
        level = ring.deep - step
        if step == 0:
            spot, length = ring.rows(chain, level, self.width)
            source, region = self.piece.at[chain], self.out.at[matrix, rows_at(spot, length)]
            self.local[chain] = pltpu.make_async_copy(source, region, self.out_sem.at[chain])
            self.local[chain].start()
        else:
            if step == 1:
                self.local[chain].wait()
            self.waiting[chain].wait_recv()
            if step == ring.deep:
                return
            spot, length = ring.rows(chain, level, self.width)
            source = region = self.out.at[matrix, rows_at(spot, length)]
        partner = ring.by_bit[ring.order(chain % 2)[level - 1]]
        self.waiting[chain] = ring.send(source, region, self.back_sems, (chain, step), partner)

    def advance(self, chain, step):
        ring, deep = self.ring, self.ring.deep
        matrix, stream = chain // 2, chain % 2
        mine = ring.order(stream)
        size = self.width // 2
        got = self.got
        if step < deep or step == deep:
            if step == 0:
                spot = (1 - ring.place(mine[0])) * size + stream * (size // 2)
                source = self.own.at[matrix, rows_at(spot, size // 2)]
            else:
                self.waiting[chain].wait_recv()
                count = got[step - 1].shape[1]
                if step == 1:
                    kept = self.own[matrix, rows_at(ring.place(mine[0]) * size + stream * (size // 2), count), :]
                else:
                    kept = got[step - 2][chain, rows_at(ring.place(mine[step - 1]) * count, count), :]
                got[step - 1][chain] = (kept.astype(F32) + got[step - 1][chain].astype(F32)).astype(BF16)
                if step < deep:
                    half = count // 2
                    source = got[step - 1].at[chain, rows_at((1 - ring.place(mine[step])) * half, half)]
            if step < deep:
                self.waiting[chain] = ring.send(
                    source, got[step].at[chain], self.sems, (chain, step), ring.by_bit[mine[step]]
                )
                return
        if step <= deep + 3:
            self.line.advance(chain, step - deep, got[deep - 1].at[chain])
        if step >= deep + 3:
            self.back(chain, step - deep - 3)


class Line:
    def __init__(self, ring, lines, piece, sems, first=0):
        self.ring, self.lines, self.piece, self.sems, self.first = ring, lines, piece, sems, first
        self.waiting = {}

    def advance(self, chain, step, source):
        ring, lines, at = self.ring, self.lines, chain - self.first
        if step == 0:
            self.waiting[chain] = ring.send(source, lines[0].at[at], self.sems, (at, 0), ring.beside, ring.outer)
        elif step == 1:
            first = self.waiting[chain]

            @pl.when(ring.inner)
            def _():
                first.wait_recv()
                lines[0][at] = (source[...].astype(F32) + lines[0][at].astype(F32)).astype(BF16)

            self.waiting[chain] = ring.send(lines[0].at[at], lines[1].at[at], self.sems, (at, 1), ring.across, ring.inner)
        elif step == 2:
            second = self.waiting[chain]

            @pl.when(ring.inner)
            def _():
                second.wait_recv()
                both = (lines[0][at].astype(F32) + lines[1][at].astype(F32)).astype(BF16)
                self.piece[chain - self.first] = both
                lines[2][at] = both

            self.waiting[chain] = ring.send(lines[2].at[at], lines[3].at[at], self.sems, (at, 2), ring.beside, ring.inner)
        else:
            third = self.waiting[chain]

            @pl.when(ring.outer)
            def _():
                third.wait_recv()
                self.piece[chain - self.first] = lines[3][at]


def reduction_scratch(chains, width, deep):
    length = width // 4
    sizes = [length >> i for i in range(deep)]
    shapes = [pltpu.VMEM((chains, size, width), BF16) for size in sizes + [sizes[-1]] * 4]
    return shapes + [pltpu.SemaphoreType.DMA((chains, deep))] * 2 + [pltpu.SemaphoreType.DMA((chains, 3))] * 2 + [
        pltpu.SemaphoreType.DMA((chains, deep))
    ] * 2 + [pltpu.SemaphoreType.DMA((chains,)), pltpu.VMEM((chains, sizes[-1], width), BF16)]


def temporal_tail_body(
    g_ref, gain_ref, shift_ref, small_in, x_hbm, q_hbm, k_hbm, v_hbm, w_hbm, *refs, planes, early, taken,
):
    early_hbm, refs = refs[:early], refs[early:]
    moved_ref, out_ref, small_out, refs = refs[0], refs[1], refs[2], refs[3:]
    x_ref, qkv_ref, w_ref, d_ref, dx_ref, own, load_sem, refs = *refs[:7], refs[7:]
    move_send, move_recv, move_local, small_ref, small_got, small_held, small_send, small_recv, refs = *refs[:8], refs[8:]
    ring = Ring(planes)
    deep = ring.deep
    got, lines, refs = refs[:deep], refs[deep : deep + 4], refs[deep + 4 :]
    sems, line_sems, back_sems, out_sem, piece_ref = refs[:2], refs[2:4], refs[4:6], refs[6], refs[7]
    frames, slots, width = g_ref.shape
    groups = width // WIDE
    rows = frames * STEP
    loads = {}

    def load(name, source, target, at):
        copy = pltpu.make_async_copy(source, target, load_sem.at[at])
        copy.start()
        loads[name] = copy

    def load_group(group):
        for place, ref in enumerate((q_hbm, k_hbm, v_hbm)):
            source = ref.at[:, :, pl.ds(group * WIDE, WIDE)]
            load(("qkv", group, place), source, qkv_ref.at[group % 2, place], early + 2 + 3 * group + place)

    load_group(0)
    for matrix in range(early):
        load(("own", matrix), early_hbm[matrix], own.at[matrix], matrix)
    load("x", x_hbm, x_ref, early)
    load("w", w_hbm, w_ref, early + 1)
    ring.greet()
    matrices = early + groups
    line = Line(ring, lines, piece_ref, line_sems)
    sums = Reduction(ring, own, got, line, piece_ref, out_ref, sems, back_sems, out_sem)
    small_ref[...] = small_in[...]

    row = lax.broadcasted_iota(jnp.int32, (rows, rows), 0)
    col = lax.broadcasted_iota(jnp.int32, (rows, rows), 1)
    same = row % STEP == col % STEP
    shape = (frames, STEP, WIDE)
    starts = {}
    ready = {}

    def compute():
        for group in range(groups):
            if group + 1 < groups:
                load_group(group + 1)
            for place in range(3):
                loads[("qkv", group, place)].wait()
            slot = group % 2
            lanes = slice(group * WIDE, (group + 1) * WIDE)
            for step in range(slots // STEP):
                part = slice(step * STEP, (step + 1) * STEP)
                k = qkv_ref[slot, 1, :, part, :].reshape(rows, WIDE)
                v = qkv_ref[slot, 2, :, part, :].reshape(rows, WIDE)
                queries = stacked(qkv_ref[slot, 0, :, part, :].reshape(rows, WIDE), rows)
                grads = stacked(g_ref[:, part, lanes].reshape(rows, WIDE), rows)
                scores = dot_nt(k, queries)
                grad_mixing = dot_nt(v, grads)
                mixing, grad_scores = [], []
                for head in range(GROUP):
                    span = slice(head * rows, (head + 1) * rows)
                    s = jnp.where(same, scores[:, span], -1e30)
                    e = jnp.exp(s - jnp.max(s, axis=0, keepdims=True))
                    p = e / jnp.sum(e, axis=0, keepdims=True)
                    gp = grad_mixing[:, span]
                    ds = p * (gp - jnp.sum(p * gp, axis=0, keepdims=True))
                    mixing.append(p.astype(BF16))
                    grad_scores.append(ds.astype(BF16))
                grad_scores = jnp.concatenate(grad_scores, axis=1)
                dv = dot(jnp.concatenate(mixing, axis=1), grads)
                dk = dot(grad_scores, queries)
                spread = dot_tn(grad_scores, k)
                dq = jnp.zeros((rows, WIDE), F32)
                for head in range(GROUP):
                    dq = dq + spread[head * rows : (head + 1) * rows] * head_lanes(rows, head, F32)
                d_ref[group, :, part, :WIDE] = (dq * HEAD_DIM**-0.5).astype(BF16).reshape(shape)
                d_ref[group, :, part, WIDE : 2 * WIDE] = dk.astype(BF16).reshape(shape)
                d_ref[group, :, part, 2 * WIDE :] = dv.astype(BF16).reshape(shape)
                if step % 4 == 3:
                    yield 2.0
            if group == 0:
                loads["x"].wait()
            d = d_ref[group].reshape(frames * slots, 3 * WIDE)
            x = x_ref[...].reshape(frames * slots, width)
            own[early + group] = dot_tn(x, d).astype(BF16)
            ready[early + group] = True
            yield 4.5
            small_ref[taken : taken + 1, lanes] = column_sum(d[:, :WIDE])
            small_ref[taken + 1 : taken + 2, lanes] = column_sum(d[:, 2 * WIDE :])
        loads["w"].wait()
        quarter = frames // 4
        shift_grad, product = jnp.zeros((1, width), F32), jnp.zeros((1, width), F32)
        for distance in (2, 3, 1, 0):
            part = (ring.part + distance) % 4
            some = pl.ds(part * quarter, quarter)
            total = jnp.zeros((quarter * slots, width), F32)
            for group in range(groups):
                d = d_ref[group, some].reshape(quarter * slots, 3 * WIDE)
                for place in range(3):
                    weight = w_ref[:, pl.ds(place * width + group * WIDE, WIDE)]
                    total = total + dot_nt(d[:, place * WIDE : (place + 1) * WIDE], weight)
            dx_ref[some] = total.astype(BF16).reshape(quarter, slots, width)
            if distance:
                moves.append(move(distance))
                moves[-1].start()
            else:
                keep = pltpu.make_async_copy(dx_ref.at[some], moved_ref.at[ring.part], move_local.at[0])
                keep.start()
                kept.append(keep)
            x = x_ref[some].reshape(quarter * slots, width)
            shift_grad += column_sum(total)
            product += column_sum(total * x.astype(F32))
            yield 3.5
        small_ref[taken + 2 : taken + 3, :] = (product - shift_ref[...] * shift_grad) / gain_ref[...]
        small_ref[taken + 3 : taken + 4, :] = shift_grad

    moves, kept = [], []

    def move(distance, arriving=False):
        target = (ring.part + distance) % 4
        source = (ring.part + 4 - distance) % 4 if arriving else ring.part
        return pltpu.make_async_remote_copy(
            src_ref=dx_ref.at[pl.ds(target * (frames // 4), frames // 4)], dst_ref=moved_ref.at[source],
            send_sem=move_send.at[distance], recv_sem=move_recv.at[source], device_id={"mp": target}, device_id_type=MESH,
        )

    partners = [ring.by_bit[bit] for bit in ring.bits] + [ring.beside, ring.third]
    small_wait = []

    def small_step(step):
        if step > 0:
            small_wait.pop().wait_recv()
            before = small_ref[...] if step == 1 else small_held[step - 2]
            value = before + small_got[step - 1]
            if step == len(partners):
                small_out[...] = value
                return
            small_held[step - 1] = value
        source = small_ref if step == 0 else small_held.at[step - 1]
        small_wait.append(ring.send(source, small_got.at[step], (small_send, small_recv), step, partners[step]))

    following = [0] * matrices
    due = [EARLY_GAP * matrix for matrix in range(matrices)]
    clock = 0.0

    def advance_all():
        for matrix in range(matrices):
            step = following[matrix]
            if step < sums.steps and clock >= due[matrix] and (matrix < early or matrix in ready):
                if step == 0 and matrix < early:
                    loads[("own", matrix)].wait()
                for chain in (2 * matrix, 2 * matrix + 1):
                    sums.advance(chain, step)
                following[matrix] += 1
                due[matrix] = clock + HOP

    advance_all()
    for spent in compute():
        clock += spent
        advance_all()
    small_at = 0
    while any(step < sums.steps for step in following) or small_at <= len(partners):
        clock += HOP
        advance_all()
        if small_at <= len(partners):
            small_step(small_at)
            small_at += 1
    for distance in (1, 2, 3):
        move(distance, True).wait_recv()
    for copy in moves:
        copy.wait_send()
    kept[0].wait()
    ring.finish()


def temporal_tail(x, q, k, v, grad, weight, gain, shift, early, small, taken, planes, number):
    frames, slots, width = x.shape
    groups = width // WIDE
    deep = len(bits_of(planes))
    chains = 2 * (len(early) + groups)
    anywhere = pl.BlockSpec(memory_space=pl.ANY)
    whole = pl.BlockSpec(memory_space=pltpu.VMEM)
    flops = 2 * frames * slots * width * width * 12
    return pl.pallas_call(
        functools.partial(temporal_tail_body, planes=planes, early=len(early), taken=taken),
        in_specs=[whole] * 4 + [anywhere] * (5 + len(early)),
        out_specs=[anywhere, anywhere, whole],
        out_shape=[
            jax.ShapeDtypeStruct((4, frames // 4, slots, width), BF16),
            jax.ShapeDtypeStruct((len(early) + groups, width, width), BF16),
            jax.ShapeDtypeStruct(small.shape, F32),
        ],
        scratch_shapes=[
            pltpu.VMEM(x.shape, BF16), pltpu.VMEM((2, 3, frames, slots, WIDE), BF16), pltpu.VMEM(weight.shape, BF16),
            pltpu.VMEM((groups, frames, slots, 3 * WIDE), BF16), pltpu.VMEM(x.shape, BF16),
            pltpu.VMEM((len(early) + groups, width, width), BF16),
            pltpu.SemaphoreType.DMA((len(early) + 2 + 3 * groups,)),
            pltpu.SemaphoreType.DMA((4,)), pltpu.SemaphoreType.DMA((4,)), pltpu.SemaphoreType.DMA((1,)),
            pltpu.VMEM(small.shape, F32), pltpu.VMEM((deep + 2,) + small.shape, F32), pltpu.VMEM((deep + 1,) + small.shape, F32),
            pltpu.SemaphoreType.DMA((deep + 2,)), pltpu.SemaphoreType.DMA((deep + 2,)),
        ] + reduction_scratch(chains, width, deep),
        cost_estimate=pl.CostEstimate(flops=flops, bytes_accessed=60 * MIB, transcendentals=0),
        compiler_params=pltpu.CompilerParams(vmem_limit_bytes=62 * MIB, collective_id=number, has_side_effects=True),
        name="temporal_tail",
    )(grad, gain, shift, small, x, q, k, v, weight, *early)


def shards(
    video,
    patch_width,
    temporal_gain,
    temporal_shift,
    temporal_qkv,
    temporal_qv_bias,
    temporal_proj,
    temporal_proj_bias,
    spatial_gain,
    spatial_shift,
    spatial_qkv,
    spatial_qv_bias,
    spatial_proj,
    spatial_proj_bias,
    mlp_gain,
    mlp_shift,
    fc1_weight,
    fc1_bias,
    fc2_weight,
    fc2_bias,
    cotangent,
):
    frames, sets, slots, width = video.shape
    units = fc1_weight.shape[1]
    parts, planes = lax.axis_size("mp"), lax.axis_size("dp")
    share = -(-slots // (parts * STEP)) * STEP
    row = lambda value: value.astype(F32).reshape(1, -1)
    video = video.reshape(frames * sets, slots, width)
    cot = cotangent.reshape(frames * sets, slots, width)

    joint = jnp.concatenate([fc1_weight, fc2_weight.T], axis=1)
    piece = width // planes
    own = lax.dynamic_slice_in_dim(joint, lax.axis_index("dp") * piece, piece, 0)
    bias_rows = jnp.pad(fc1_bias.reshape(1, units), ((0, 15), (0, units)))
    own = jnp.concatenate([own, bias_rows], axis=0)[None]

    def exchange(value):
        return lax.all_to_all(value, "mp", split_axis=0, concat_axis=0, tiled=True)

    by_position = lambda value: value.reshape(parts * frames, share, width)
    by_device = lambda value: value.reshape(parts, frames, share, width)
    normed_in = norm_in(video, row(temporal_gain), row(temporal_shift), parts, share)
    x = by_position(exchange(normed_in))
    own, x = lax.optimization_barrier((own, x))
    column = lax.all_gather(own, "mp", axis=0, tiled=True)
    tq, tk, tv, time_mixed = temporal_fwd(x, temporal_qkv, row(temporal_qv_bias))
    column, time_mixed = lax.optimization_barrier((column, time_mixed))
    fb1 = column[:, piece : piece + 1, :units].astype(F32)
    joint = lax.all_gather(column[:, :piece], "dp", axis=1, tiled=True)
    time_back = exchange(by_device(time_mixed))

    first, normed_mid, space_qkv = middle(
        time_back, video, temporal_proj, row(temporal_proj_bias), row(spatial_gain), row(spatial_shift), spatial_qkv,
        row(spatial_qv_bias),
    )
    space_mixed, lse = spatial_fwd(patch_width, space_qkv, frames, slots)

    output, normed_out, hidden, grad_inner, grad_second, grad_space_out, grad_space, feed_sums, unit_sums = feed(
        first, space_mixed, cot, spatial_proj, row(spatial_proj_bias), row(mlp_gain), row(mlp_shift), joint, fb1,
        row(fc2_bias),
    )
    fc_part = fc_grads(normed_out, cot, grad_inner, hidden)
    fc_part = lax.psum_scatter(fc_part, "dp", scatter_dimension=1, tiled=True)

    dq, dk, dv = spatial_bwd(patch_width, space_qkv, space_mixed, lse, grad_space, frames, slots)
    grad_first, grad_time_out, grad_time, mid_sums = middle_bwd(
        dq, dk, dv, spatial_qkv, first, grad_second, row(spatial_gain), temporal_proj, parts, share
    )
    flat = lambda value: value.reshape(-1, width)
    grad_slot = exchange(grad_time)
    time_rows = jnp.swapaxes(time_back, 0, 1).reshape(frames, parts * share, width)[:, :slots]
    early = weight_grads(
        [
            (flat(normed_mid), [flat(dq), flat(dk), flat(dv)]),
            (flat(space_mixed), [flat(grad_space_out)]),
            (flat(time_rows), [flat(grad_time_out)]),
        ]
    )
    fc_part, early[4] = lax.optimization_barrier((fc_part, early[4]))
    fc_part = lax.psum_scatter(fc_part, "mp", scatter_dimension=0, tiled=True)[0].astype(F32)
    fc1_weight_grad = fc_part[:, :units]
    fc2_weight_grad = fc_part[:, units:].T

    own_sums = [unit_sums[:, 0, :].reshape(-1, width), feed_sums[:4], mid_sums[:5]]
    time_inputs = (x, tq, tk, tv, by_position(grad_slot), temporal_qkv, row(temporal_gain), row(temporal_shift))
    wide = lambda blocks: jnp.concatenate([block.astype(F32) for block in blocks], axis=1)
    if reducible(width, planes, parts):
        taken = sum(rows.shape[0] for rows in own_sums)
        small = jnp.concatenate(own_sums + [jnp.zeros((4 + -(taken + 4) % 8, width), F32)], axis=0)
        grad_in, matrices, small = temporal_tail(*time_inputs, early, small, taken, planes, 1)
        groups = width // WIDE
        temporal_qkv_grad = wide(
            [matrices[5 + g][:, p * WIDE : (p + 1) * WIDE] for p in range(3) for g in range(groups)]
        )
    else:
        gq, gk, gv, grad_x, bias_sums, norm_sums = temporal_bwd(*time_inputs)
        grad_in = exchange(by_device(grad_x))
        small = jnp.concatenate(own_sums + [bias_sums[:2], norm_sums[:2]], axis=0)
        late = weight_grads([(flat(x), [flat(gq), flat(gk), flat(gv)])])
        matrices, small = lax.psum((jnp.stack(early + late), small), ("dp", "mp"))
        temporal_qkv_grad = wide([matrices[5 + p] for p in range(3)])
    video_grad = norm_out(grad_in, video, grad_first, row(temporal_gain))
    count = parts * units // width
    fc1_bias_grad = small[:count].reshape(-1)
    (
        mlp_gain_grad, mlp_shift_grad, spatial_proj_bias_grad, fc2_bias_grad,
        spatial_gain_grad, spatial_shift_grad, space_q_sum, space_v_sum, temporal_proj_bias_grad,
        time_q_sum, time_v_sum, temporal_gain_grad, temporal_shift_grad,
    ) = [small[count + i] for i in range(13)]
    return (
        output.reshape(frames, sets, slots, width),
        video_grad.reshape(frames, sets, slots, width),
        temporal_gain_grad,
        temporal_shift_grad,
        temporal_qkv_grad,
        jnp.concatenate([time_q_sum, time_v_sum]),
        matrices[4].astype(F32),
        temporal_proj_bias_grad,
        spatial_gain_grad,
        spatial_shift_grad,
        wide([matrices[0], matrices[1], matrices[2]]),
        jnp.concatenate([space_q_sum, space_v_sum]),
        matrices[3].astype(F32),
        spatial_proj_bias_grad,
        mlp_gain_grad,
        mlp_shift_grad,
        fc1_weight_grad,
        fc1_bias_grad,
        fc2_weight_grad,
        fc2_bias_grad,
    )


def solution(mesh):
    tokens = P("mp", "dp", None, None)
    return jax.shard_map(
        shards,
        mesh=mesh,
        in_specs=(tokens, P("dp")) + (P(),) * 14 + (P(None, "mp"), P("mp"), P("mp", None), P(), tokens),
        out_specs=(tokens, tokens) + (P(),) * 14 + (P("dp", "mp"), P(), P("mp", "dp"), P()),
        check_vma=False,
    )
```

```python
import functools
import jax
import jax.numpy as jnp
from jax import lax
from jax.experimental import pallas as pl
from jax.experimental.pallas import tpu as pltpu
from jax.sharding import PartitionSpec as P

HEADS = 12
HEAD_DIM = 64
GROUP = 4
WIDE = GROUP * HEAD_DIM
EPSILON = 1e-06
F32 = jnp.float32
BF16 = jnp.bfloat16
MIB = 1 << 20


def params(mib=56):
    return pltpu.CompilerParams(vmem_limit_bytes=mib * MIB)


def dot(a, b):
    return jnp.dot(a, b, preferred_element_type=F32)


def dot_nt(a, b):
    return lax.dot_general(a, b, (((1,), (1,)), ((), ())), preferred_element_type=F32)


def dot_tn(a, b):
    return lax.dot_general(a, b, (((0,), (0,)), ((), ())), preferred_element_type=F32)


def head_lanes(rows, head, dtype):
    lane = lax.broadcasted_iota(jnp.int32, (rows, WIDE), 1)
    return (lane // HEAD_DIM == head).astype(dtype)


def windows(slots, clips, rows):
    size = slots // clips
    found = []
    for start in range(0, slots, rows):
        stop = min(start + rows, slots)
        low = start // size * size // 16 * 16
        high = min(-(-(-(-stop // size) * size) // 16) * 16, slots)
        found.append((start, stop, low, high))
    return found


def spatial_fwd_body(width_ref, q_ref, k_ref, v_ref, o_ref, l_ref, *, slots, rows, narrow):
    def attend(chunks, size):
        stats = []
        for start, stop, low, high in chunks:
            count = stop - start
            q = q_ref[start:stop, :]
            k = k_ref[low:high, :]
            v = v_ref[low:high, :]
            if size < slots:
                query_clip = (lax.broadcasted_iota(jnp.int32, (count, high - low), 0) + start) // size
                key_clip = (lax.broadcasted_iota(jnp.int32, (count, high - low), 1) + low) // size
                same = query_clip == key_clip
            total = jnp.zeros((count, WIDE), F32)
            lse = jnp.zeros((count, 128), F32)
            lane = lax.broadcasted_iota(jnp.int32, (count, 128), 1)
            for head in range(GROUP):
                s = dot_nt(q * head_lanes(count, head, BF16), k)
                if size < slots:
                    s = jnp.where(same, s, -1e30)
                top = jnp.max(s, axis=1, keepdims=True)
                e = jnp.exp(s - top)
                norm = jnp.sum(e, axis=1, keepdims=True)
                o = dot(e.astype(BF16), v)
                total = total + o * (head_lanes(count, head, F32) / norm)
                lse = jnp.where(lane == head, top + jnp.log(norm), lse)
            o_ref[start:stop, :] = total.astype(BF16)
            stats.append(lse)
        l_ref[...] = jnp.concatenate(stats, axis=0).T[:8, :]

    wide = width_ref[0] == slots

    @pl.when(wide)
    def _():
        attend(windows(slots, 1, rows or slots), slots)

    @pl.when(jnp.logical_not(wide))
    def _():
        attend(windows(slots, 4, narrow), slots // 4)


def spatial_fwd(width, qkv, frames, slots, rows=None, narrow=256):
    groups = HEADS // GROUP
    qkv = qkv.reshape(frames, slots, -1)
    spec = lambda part: pl.BlockSpec((None, slots, WIDE), lambda f, g, w: (f, 0, part * groups + g))
    out = pl.pallas_call(
        functools.partial(spatial_fwd_body, slots=slots, rows=rows, narrow=narrow),
        grid_spec=pltpu.PrefetchScalarGridSpec(
            num_scalar_prefetch=1,
            grid=(frames, groups),
            in_specs=[spec(0), spec(1), spec(2)],
            out_specs=[
                pl.BlockSpec((None, slots, WIDE), lambda f, g, w: (f, 0, g)),
                pl.BlockSpec((None, None, 8, slots), lambda f, g, w: (f, g, 0, 0)),
            ],
        ),
        out_shape=[
            jax.ShapeDtypeStruct((frames, slots, HEADS * HEAD_DIM), BF16),
            jax.ShapeDtypeStruct((frames, groups, 8, slots), F32),
        ],
        cost_estimate=pl.CostEstimate(flops=20 * 10**9, bytes_accessed=5 * MIB, transcendentals=0),
        compiler_params=params(),
        name="spatial_fwd",
    )(width, qkv, qkv, qkv)
    return out


def spatial_bwd_body(width_ref, q_ref, k_ref, v_ref, o_ref, l_ref, g_ref, dq_ref, dk_ref, dv_ref, dqt, *, slots, rows, narrow):
    prod = g_ref[...].astype(F32) * o_ref[...].astype(F32)
    high_part = prod.astype(BF16)
    low_part = (prod - high_part.astype(F32)).astype(BF16)
    lane = lax.broadcasted_iota(jnp.int32, (8, WIDE), 1)
    row = lax.broadcasted_iota(jnp.int32, (8, WIDE), 0)
    picks = (lane // HEAD_DIM == row).astype(BF16)
    delta = dot_nt(picks, high_part) + dot_nt(picks, low_part)

    def attend(chunks, size):
        dqt[...] = jnp.zeros_like(dqt)
        kt = k_ref[...].T
        for start, stop, low, high in chunks:
            count = stop - start
            k = k_ref[start:stop, :]
            v = v_ref[start:stop, :]
            q = q_ref[low:high, :]
            g = g_ref[low:high, :]
            if size < slots:
                key_clip = (lax.broadcasted_iota(jnp.int32, (count, high - low), 0) + start) // size
                query_clip = (lax.broadcasted_iota(jnp.int32, (count, high - low), 1) + low) // size
                same = query_clip == key_clip
            dk = jnp.zeros((count, WIDE), F32)
            dv = jnp.zeros((count, WIDE), F32)
            for head in range(GROUP):
                mask = head_lanes(count, head, BF16)
                s = dot_nt(k * mask, q)
                p = jnp.exp(s - l_ref[head : head + 1, low:high])
                if size < slots:
                    p = jnp.where(same, p, 0.0)
                dp = dot_nt(v * mask, g)
                ds = (p * (dp - delta[head : head + 1, low:high])).astype(BF16)
                keep = head_lanes(count, head, F32)
                dv = dv + dot(p.astype(BF16), g) * keep
                dk = dk + dot(ds, q) * keep
                span = slice(head * HEAD_DIM, (head + 1) * HEAD_DIM)
                dqt[span, low:high] += dot(kt[span, start:stop], ds)
            dk_ref[start:stop, :] = dk.astype(BF16)
            dv_ref[start:stop, :] = dv.astype(BF16)
        dq_ref[...] = (dqt[...] * HEAD_DIM**-0.5).T.astype(BF16)

    wide = width_ref[0] == slots

    @pl.when(wide)
    def _():
        attend(windows(slots, 1, rows or slots), slots)

    @pl.when(jnp.logical_not(wide))
    def _():
        attend(windows(slots, 4, narrow), slots // 4)


def spatial_bwd(frame, width, qkv, mixed, lse, grad, frames, slots, rows=None, narrow=208):
    groups = HEADS // GROUP
    width_all = HEADS * HEAD_DIM
    qkv = qkv.reshape(frames, slots, -1)
    spec = lambda part: pl.BlockSpec((None, slots, WIDE), lambda f, g, w: (f, 0, part * groups + g))
    one = pl.BlockSpec((None, slots, WIDE), lambda f, g, w: (f, 0, g))
    out = pl.pallas_call(
        functools.partial(spatial_bwd_body, slots=slots, rows=rows, narrow=narrow),
        grid_spec=pltpu.PrefetchScalarGridSpec(
            num_scalar_prefetch=1,
            grid=(frames, groups),
            in_specs=[
                spec(0), spec(1), spec(2), one,
                pl.BlockSpec((None, None, 8, slots), lambda f, g, w: (f, g, 0, 0)),
                pl.BlockSpec((None, slots, WIDE), lambda f, g, w: (frame + f, 0, g)),
            ],
            out_specs=[one, one, one],
            scratch_shapes=[pltpu.VMEM((WIDE, slots), F32)],
        ),
        out_shape=[jax.ShapeDtypeStruct((frames, slots, width_all), BF16)] * 3,
        cost_estimate=pl.CostEstimate(flops=32 * 10**9, bytes_accessed=9 * MIB, transcendentals=0),
        compiler_params=params(),
        name="spatial_bwd",
    )(width, qkv, qkv, qkv, mixed, lse, grad)
    return out


def fixed(shape):
    return pl.BlockSpec(shape, lambda *_: (0,) * len(shape))


def norm_parts(value):
    centered = value - jnp.mean(value, axis=-1, keepdims=True)
    scale = lax.rsqrt(jnp.mean(centered * centered, axis=-1, keepdims=True) + EPSILON)
    return centered * scale, scale


def norm_grad(grad, unit, scale, gain):
    inner = grad * gain
    return scale * (
        inner
        - jnp.mean(inner, axis=-1, keepdims=True)
        - unit * jnp.mean(inner * unit, axis=-1, keepdims=True)
    )


def column_sum(value):
    return jnp.sum(value.astype(F32), axis=0, keepdims=True)


def by_part(parts, share, width):
    return pl.BlockSpec((parts, None, share, width), lambda f: (0, f, 0, 0))


def norm_in_body(video_ref, gain_ref, shift_ref, out_ref):
    unit, _ = norm_parts(video_ref[...].astype(F32))
    split_positions(out_ref, (unit * gain_ref[...] + shift_ref[...]).astype(BF16))


def split_positions(out_ref, value):
    parts, share, width = out_ref.shape
    slots = value.shape[0]
    for part in range(parts):
        start = part * share
        count = min(max(slots - start, 0), share)
        if count > 0:
            out_ref[part, :count, :] = value[start : start + count, :]
        if count < share:
            out_ref[part, count:, :] = jnp.zeros((share - count, width), value.dtype)


def joined_positions(ref, slots):
    parts, share, width = ref.shape
    return ref[...].reshape(parts * share, width)[:slots, :]


def norm_in(video, gain, shift, parts, share):
    frames, slots, width = video.shape
    return pl.pallas_call(
        norm_in_body,
        grid=(frames,),
        in_specs=[pl.BlockSpec((None, slots, width), lambda f: (f, 0, 0)), fixed((width,)), fixed((width,))],
        out_specs=by_part(parts, share, width),
        out_shape=jax.ShapeDtypeStruct((parts, frames, share, width), BF16),
        cost_estimate=pl.CostEstimate(flops=1 * 10**9, bytes_accessed=10 * MIB, transcendentals=0),
        compiler_params=params(),
        name="norm_in",
    )(video, gain, shift)


STEP = 16


def stacked(block, rows):
    return jnp.concatenate([block * head_lanes(rows, head, BF16) for head in range(GROUP)], axis=0)


def temporal_fwd_body(x_ref, wq_ref, wk_ref, wv_ref, bq_ref, bv_ref, q_ref, k_ref, v_ref, *o_refs):
    frames, slots, width = x_ref.shape
    x = x_ref[...].reshape(frames * slots, width)
    shape = (frames, slots, WIDE)
    q_ref[...] = ((dot(x, wq_ref[...]) + bq_ref[...]) * HEAD_DIM**-0.5).astype(BF16).reshape(shape)
    k_ref[...] = dot(x, wk_ref[...]).astype(BF16).reshape(shape)
    v_ref[...] = (dot(x, wv_ref[...]) + bv_ref[...]).astype(BF16).reshape(shape)
    rows = frames * STEP
    row = lax.broadcasted_iota(jnp.int32, (rows, rows), 0)
    col = lax.broadcasted_iota(jnp.int32, (rows, rows), 1)
    same = row % STEP == col % STEP
    for step in range(slots // STEP):
        part = slice(step * STEP, (step + 1) * STEP)
        q = q_ref[:, part, :].reshape(rows, WIDE)
        keys = stacked(k_ref[:, part, :].reshape(rows, WIDE), rows)
        values = stacked(v_ref[:, part, :].reshape(rows, WIDE), rows)
        scores = dot_nt(q, keys)
        mixing = []
        for head in range(GROUP):
            s = jnp.where(same, scores[:, head * rows : (head + 1) * rows], -1e30)
            e = jnp.exp(s - jnp.max(s, axis=1, keepdims=True))
            mixing.append((e / jnp.sum(e, axis=1, keepdims=True)).astype(BF16))
        o = dot(jnp.concatenate(mixing, axis=1), values)
        o = o.astype(BF16).reshape(frames // len(o_refs), len(o_refs), STEP, WIDE)
        for place, o_ref in enumerate(o_refs):
            o_ref[:, part, :] = o[:, place]


def temporal_fwd(x, weight, bias, local):
    frames, slots, width = x.shape
    groups = width // WIDE
    w = lambda part: pl.BlockSpec((width, WIDE), lambda g: (0, part * groups + g))
    b = lambda part: pl.BlockSpec((1, WIDE), lambda g: (0, part * groups + g))
    one = pl.BlockSpec((frames, slots, WIDE), lambda g: (0, 0, g))
    return pl.pallas_call(
        temporal_fwd_body,
        grid=(groups,),
        in_specs=[fixed(x.shape), w(0), w(1), w(2), b(0), b(1)],
        out_specs=[one] * 3 + [pl.BlockSpec((frames // local, slots, WIDE), lambda g: (0, 0, g))] * local,
        out_shape=[jax.ShapeDtypeStruct(x.shape, BF16)] * 3
        + [jax.ShapeDtypeStruct((frames // local, slots, width), BF16)] * local,
        cost_estimate=pl.CostEstimate(flops=30 * 10**9, bytes_accessed=16 * MIB, transcendentals=0),
        compiler_params=params(),
        name="temporal_fwd",
    )(x, weight, weight, weight, bias, bias)


def temporal_bwd_body(
    x_ref, q_ref, k_ref, v_ref, g_ref, wq_ref, wk_ref, wv_ref, gain_ref, shift_ref,
    dq_ref, dk_ref, dv_ref, dx_ref, sums_ref, norm_ref, total_ref,
):
    frames, slots, width = x_ref.shape
    rows = frames * STEP
    row = lax.broadcasted_iota(jnp.int32, (rows, rows), 0)
    col = lax.broadcasted_iota(jnp.int32, (rows, rows), 1)
    same = row % STEP == col % STEP
    shape = (frames, STEP, WIDE)
    for step in range(slots // STEP):
        part = slice(step * STEP, (step + 1) * STEP)
        k = k_ref[:, part, :].reshape(rows, WIDE)
        v = v_ref[:, part, :].reshape(rows, WIDE)
        queries = stacked(q_ref[:, part, :].reshape(rows, WIDE), rows)
        grads = stacked(g_ref[:, part, :].reshape(rows, WIDE), rows)
        scores = dot_nt(k, queries)
        grad_mixing = dot_nt(v, grads)
        mixing, grad_scores = [], []
        for head in range(GROUP):
            span = slice(head * rows, (head + 1) * rows)
            s = jnp.where(same, scores[:, span], -1e30)
            e = jnp.exp(s - jnp.max(s, axis=0, keepdims=True))
            p = e / jnp.sum(e, axis=0, keepdims=True)
            gp = grad_mixing[:, span]
            ds = p * (gp - jnp.sum(p * gp, axis=0, keepdims=True))
            mixing.append(p.astype(BF16))
            grad_scores.append(ds.astype(BF16))
        grad_scores = jnp.concatenate(grad_scores, axis=1)
        dv_ref[:, part, :] = dot(jnp.concatenate(mixing, axis=1), grads).astype(BF16).reshape(shape)
        dk_ref[:, part, :] = dot(grad_scores, queries).astype(BF16).reshape(shape)
        spread = dot_tn(grad_scores, k)
        dq = jnp.zeros((rows, WIDE), F32)
        for head in range(GROUP):
            dq = dq + spread[head * rows : (head + 1) * rows] * head_lanes(rows, head, F32)
        dq_ref[:, part, :] = (dq * HEAD_DIM**-0.5).astype(BF16).reshape(shape)
    flat = (frames * slots, WIDE)
    dq, dk, dv = dq_ref[...].reshape(flat), dk_ref[...].reshape(flat), dv_ref[...].reshape(flat)
    sums_ref[...] = jnp.concatenate([column_sum(dq), column_sum(dv), jnp.zeros((6, WIDE), F32)], axis=0)
    update = dot_nt(dq, wq_ref[...]) + dot_nt(dk, wk_ref[...]) + dot_nt(dv, wv_ref[...])
    group = pl.program_id(0)

    @pl.when(group == 0)
    def _():
        total_ref[...] = update

    @pl.when(group > 0)
    def _():
        total_ref[...] += update

    @pl.when(group == pl.num_programs(0) - 1)
    def _():
        total = total_ref[...]
        dx_ref[...] = total.astype(BF16).reshape(frames, slots, width)
        x = x_ref[...].reshape(frames * slots, width).astype(F32)
        shift_grad = column_sum(total)
        gain_grad = (column_sum(total * x) - shift_ref[...][None] * shift_grad) / gain_ref[...][None]
        norm_ref[...] = jnp.concatenate([gain_grad, shift_grad, jnp.zeros((6, width), F32)], axis=0)


def temporal_bwd(x, q, k, v, grad, weight, gain, shift):
    frames, slots, width = x.shape
    groups = width // WIDE
    w = lambda part: pl.BlockSpec((width, WIDE), lambda g: (0, part * groups + g))
    one = pl.BlockSpec((frames, slots, WIDE), lambda g: (0, 0, g))
    return pl.pallas_call(
        temporal_bwd_body,
        grid=(groups,),
        in_specs=[fixed(x.shape), one, one, one, one, w(0), w(1), w(2), fixed((width,)), fixed((width,))],
        out_specs=[one, one, one, fixed(x.shape), pl.BlockSpec((8, WIDE), lambda g: (0, g)), fixed((8, width))],
        out_shape=[jax.ShapeDtypeStruct(x.shape, BF16)] * 4 + [jax.ShapeDtypeStruct((8, width), F32)] * 2,
        scratch_shapes=[pltpu.VMEM((frames * slots, width), F32)],
        cost_estimate=pl.CostEstimate(flops=35 * 10**9, bytes_accessed=30 * MIB, transcendentals=0),
        compiler_params=params(),
        name="temporal_bwd",
    )(x, q, k, v, grad, weight, weight, weight, gain, shift)


def middle_body(mixed_ref, video_ref, proj_ref, pb_ref, gain_ref, shift_ref, w_ref, bias_ref, first_ref, normed_ref, qkv_ref):
    slots, width = video_ref.shape
    first = video_ref[...].astype(F32) + (dot(joined_positions(mixed_ref, slots), proj_ref[...]) + pb_ref[...])
    first_ref[...] = first
    unit, _ = norm_parts(first)
    normed_ref[...] = (unit * gain_ref[...] + shift_ref[...]).astype(BF16)
    normed = normed_ref[...]
    q = dot(normed, w_ref[:, :width]) + bias_ref[:, :width]
    qkv_ref[:, :width] = (q * HEAD_DIM**-0.5).astype(BF16)
    qkv_ref[:, width : 2 * width] = dot(normed, w_ref[:, width : 2 * width]).astype(BF16)
    qkv_ref[:, 2 * width :] = (dot(normed, w_ref[:, 2 * width :]) + bias_ref[:, width:]).astype(BF16)


def middle(frame, mixed, video, proj, proj_bias, gain, shift, weight, bias):
    _, slots, width = video.shape
    return pl.pallas_call(
        middle_body,
        grid=(1,),
        in_specs=[
            fixed(mixed.shape), pl.BlockSpec((None, slots, width), lambda i: (frame, 0, 0)), fixed(proj.shape), fixed((width,)),
            fixed((width,)), fixed((width,)), fixed(weight.shape), fixed((1, 2 * width)),
        ],
        out_specs=[fixed((slots, width)), fixed((slots, width)), fixed((slots, 3 * width))],
        out_shape=[
            jax.ShapeDtypeStruct((slots, width), F32),
            jax.ShapeDtypeStruct((slots, width), BF16),
            jax.ShapeDtypeStruct((slots, 3 * width), BF16),
        ],
        cost_estimate=pl.CostEstimate(flops=11 * 10**9, bytes_accessed=14 * MIB, transcendentals=0),
        compiler_params=params(),
        name="middle",
    )(mixed, video, proj, proj_bias, gain, shift, weight, bias)


def gelu_both(value):
    half = 0.5 * (1.0 + lax.erf(value * 0.7071067811865476))
    density = jnp.exp(-0.5 * value * value) * 0.3989422804014327
    return value * half, half + value * density


def feed_body(
    cot_ref, proj_ref, pb_ref, gain_ref, shift_ref, fc1_ref, fb1_ref, fc2_ref, fb2_ref, *refs, sub, frames,
):
    firsts, mixeds, refs = refs[:frames], refs[frames : 2 * frames], refs[2 * frames :]
    out_ref, normed_ref, hidden_ref, gi_ref, gs_ref, gso_ref, gspace_ref, sums_ref, unitsum_ref, second, branch, gnorm = refs
    frame, chunk = pl.program_id(0), pl.program_id(1)
    slots, width = cot_ref.shape
    units = fc1_ref.shape[1]
    for place in range(frames):

        @pl.when(jnp.logical_and(chunk == 0, frame == place))
        def _(place=place):
            second[...] = firsts[place][...] + (dot(mixeds[place][...], proj_ref[...]) + pb_ref[...])

    @pl.when(chunk == 0)
    def _():
        value = second[...]
        unit, _ = norm_parts(value)
        normed_ref[...] = (unit * gain_ref[...] + shift_ref[...]).astype(BF16)
        branch[...] = jnp.zeros_like(branch)
        gnorm[...] = jnp.zeros_like(gnorm)

    @pl.when(jnp.logical_and(frame == 0, chunk == 0))
    def _():
        sums_ref[...] = jnp.zeros_like(sums_ref)
        unitsum_ref[...] = jnp.zeros_like(unitsum_ref)

    normed = normed_ref[...]
    cot = cot_ref[...]
    for start in range(0, units, sub):
        span = slice(start, start + sub)
        inner = dot(normed, fc1_ref[:, span]) + fb1_ref[0:1, span]
        grad_hidden = dot(cot, fc2_ref[:, span])
        act, slope = gelu_both(inner)
        hidden_ref[:, span] = act.astype(BF16)
        gi_ref[:, span] = (grad_hidden * slope).astype(BF16)
    branch[...] += dot_nt(hidden_ref[...], fc2_ref[...])
    gnorm[...] += dot_nt(gi_ref[...], fc1_ref[...])
    unitsum_ref[chunk, 0:1, :] += column_sum(gi_ref[...])

    @pl.when(chunk == pl.num_programs(1) - 1)
    def _():
        value = second[...]
        out_ref[...] = (value + (branch[...] + fb2_ref[...])).astype(BF16)
        unit, scale = norm_parts(value)
        grad = gnorm[...]
        cot_full = cot_ref[...].astype(F32)
        grad_second = cot_full + norm_grad(grad, unit, scale, gain_ref[...])
        gs_ref[...] = grad_second
        gso_ref[...] = grad_second.astype(BF16)
        gspace_ref[...] = dot_nt(gso_ref[...], proj_ref[...]).astype(BF16)
        sums_ref[0:1, :] += column_sum(grad * unit)
        sums_ref[1:2, :] += column_sum(grad)
        sums_ref[2:3, :] += column_sum(gso_ref[...])
        sums_ref[3:4, :] += column_sum(cot_full)


def feed(first, mixed, cot, proj, proj_bias, gain, shift, joint, fc1_bias, fc2_bias, sub=None):
    frames, slots, width = cot.shape
    chunks, _, units = fc1_bias.shape
    sub = sub or units
    per = pl.BlockSpec((None, slots, width), lambda f, c: (f, 0, 0))
    row = fixed((width,))
    hid = pl.BlockSpec((None, None, slots, units), lambda f, c: (c, f, 0, 0))
    hid_shape = jax.ShapeDtypeStruct((chunks, frames, slots, units), BF16)
    tok = lambda dtype: jax.ShapeDtypeStruct(cot.shape, dtype)
    return pl.pallas_call(
        functools.partial(feed_body, sub=sub, frames=frames),
        grid=(frames, chunks),
        in_specs=[
            per, fixed(proj.shape), row, row, row,
            pl.BlockSpec((None, width, units), lambda f, c: (c, 0, 0)),
            pl.BlockSpec((None, 1, units), lambda f, c: (c, 0, 0)),
            pl.BlockSpec((None, width, units), lambda f, c: (c, 0, 1)),
            row,
        ] + [fixed((slots, width))] * (2 * frames),
        out_specs=[per, per, hid, hid, per, per, per, fixed((8, width)), fixed((chunks, 8, units))],
        out_shape=[
            tok(BF16), tok(BF16), hid_shape, hid_shape, tok(F32), tok(BF16), tok(BF16),
            jax.ShapeDtypeStruct((8, width), F32), jax.ShapeDtypeStruct((chunks, 8, units), F32),
        ],
        scratch_shapes=[pltpu.VMEM((slots, width), F32)] * 3,
        cost_estimate=pl.CostEstimate(flops=56 * 10**9, bytes_accessed=60 * MIB, transcendentals=0),
        compiler_params=params(60),
        name="feed",
    )(cot, proj, proj_bias, gain, shift, joint, fc1_bias, joint, fc2_bias, *first, *mixed)


def middle_bwd_body(
    dq_ref, dk_ref, dv_ref, w_ref, first_ref, gs_ref, gain_ref, proj_ref, gf_ref, gto_ref, gt_ref, sums_ref
):
    slots, width = first_ref.shape
    dq, dk, dv = dq_ref[...], dk_ref[...], dv_ref[...]
    grad = dot_nt(dq, w_ref[:, :width]) + dot_nt(dk, w_ref[:, width : 2 * width]) + dot_nt(dv, w_ref[:, 2 * width :])
    unit, scale = norm_parts(first_ref[...])
    grad_first = gs_ref[...] + norm_grad(grad, unit, scale, gain_ref[...])
    gf_ref[...] = grad_first
    gto_ref[...] = grad_first.astype(BF16)
    split_positions(gt_ref, dot_nt(gto_ref[...], proj_ref[...]).astype(BF16))

    rows = [grad * unit, grad, dq, dv, gto_ref[...]]
    sums_ref[...] = jnp.concatenate([column_sum(value) for value in rows] + [jnp.zeros((3, width), F32)], axis=0)


def middle_bwd(frame, dq, dk, dv, weight, first, grad_second, gain, proj, parts, share):
    slots, width = first.shape
    return pl.pallas_call(
        middle_bwd_body,
        grid=(1,),
        in_specs=[
            fixed((slots, width)), fixed((slots, width)), fixed((slots, width)), fixed(weight.shape), fixed((slots, width)),
            pl.BlockSpec((None, slots, width), lambda i: (frame, 0, 0)), fixed((width,)), fixed(proj.shape),
        ],
        out_specs=[fixed((slots, width)), fixed((slots, width)), fixed((parts, share, width)), fixed((8, width))],
        out_shape=[
            jax.ShapeDtypeStruct(first.shape, F32), jax.ShapeDtypeStruct(first.shape, BF16),
            jax.ShapeDtypeStruct((parts, share, width), BF16), jax.ShapeDtypeStruct((8, width), F32),
        ],
        cost_estimate=pl.CostEstimate(flops=14 * 10**9, bytes_accessed=16 * MIB, transcendentals=0),
        compiler_params=params(60),
        name="middle_bwd",
    )(dq, dk, dv, weight, first, grad_second, gain, proj)


def norm_out_body(grad_ref, video_ref, gain_ref, *refs):
    *gf_refs, out_ref = refs
    slots = video_ref.shape[0]
    frame = pl.program_id(0)
    unit, scale = norm_parts(video_ref[...].astype(F32))
    result = norm_grad(joined_positions(grad_ref, slots).astype(F32), unit, scale, gain_ref[...])
    for place, gf_ref in enumerate(gf_refs):

        @pl.when(frame == place)
        def _(gf_ref=gf_ref):
            out_ref[...] = gf_ref[...] + result


def norm_out(grad, video, grad_first, gain):
    frames, slots, width = video.shape
    per = lambda rows: pl.BlockSpec((None, rows, width), lambda f: (f, 0, 0))
    return pl.pallas_call(
        norm_out_body,
        grid=(frames,),
        in_specs=[by_part(grad.shape[0], grad.shape[2], width), per(slots), fixed((width,))]
        + [fixed((slots, width))] * frames,
        out_specs=per(slots),
        out_shape=jax.ShapeDtypeStruct(video.shape, F32),
        cost_estimate=pl.CostEstimate(flops=1 * 10**9, bytes_accessed=25 * MIB, transcendentals=0),
        compiler_params=params(),
        name="norm_out",
    )(grad, video, gain, *grad_first)


def tn_body(*refs):
    *refs, out_ref = refs
    count = len(refs) // 2
    total = None
    for a_ref, b_ref in zip(refs[:count], refs[count:]):
        rows, width = b_ref.shape[0], a_ref.shape[-1]
        part = dot_tn(a_ref[...].reshape(-1, width)[:rows], b_ref[...])
        total = part if total is None else total + part
    out_ref[...] = total.astype(out_ref.dtype)


def weight_grad(a, b):
    if isinstance(b, list):
        rows, width = b[0].shape
        places = [0] * len(b)
    else:
        rows, width = b.shape[0] // len(a), b.shape[1]
        places, b = range(len(a)), [b] * len(a)
    return pl.pallas_call(
        tn_body,
        grid=(width // WIDE,),
        in_specs=[fixed(value.shape) for value in a] + [pl.BlockSpec((rows, WIDE), lambda i, p=p: (p, i)) for p in places],
        out_specs=pl.BlockSpec((width, WIDE), lambda i: (0, i)),
        out_shape=jax.ShapeDtypeStruct((width, width), BF16),
        cost_estimate=pl.CostEstimate(
            flops=2 * len(b) * rows * width * width, bytes_accessed=4 * len(b) * rows * width, transcendentals=0
        ),
        compiler_params=params(),
        name="weight_grad",
    )(*a, *b)


def fc_grads_body(normed_ref, cot_ref, gi_ref, hid_ref, out_ref):
    units = gi_ref.shape[1]
    out_ref[:, :units] = dot_tn(normed_ref[...], gi_ref[...]).astype(BF16)
    out_ref[:, units:] = dot_tn(cot_ref[...], hid_ref[...]).astype(BF16)


def fc_grads(normed, cot, grad_inner, hidden):
    chunks, frames, slots, units = hidden.shape
    width = normed.shape[-1]
    rows = frames * slots
    hid = pl.BlockSpec((None, rows, units), lambda c: (c, 0, 0))
    flat = lambda value: value.reshape(chunks, rows, units)
    return pl.pallas_call(
        fc_grads_body,
        grid=(chunks,),
        in_specs=[fixed((rows, width)), fixed((rows, width)), hid, hid],
        out_specs=pl.BlockSpec((None, width, 2 * units), lambda c: (c, 0, 0)),
        out_shape=jax.ShapeDtypeStruct((chunks, width, 2 * units), BF16),
        cost_estimate=pl.CostEstimate(
            flops=4 * rows * width * units * chunks, bytes_accessed=4 * rows * units * chunks, transcendentals=0
        ),
        compiler_params=params(),
        name="fc_grads",
    )(normed.reshape(rows, width), cot.reshape(rows, width), flat(grad_inner), flat(hidden))


def finish_body(time_ref, space_ref, space_proj_ref, time_proj_ref, time_out, space_out, space_proj_out, time_proj_out):
    for group in range(time_ref.shape[0]):
        time_out[:, group * WIDE : (group + 1) * WIDE] = time_ref[group].astype(F32)
    space_out[...] = space_ref[...].astype(F32)

    @pl.when(pl.program_id(0) == 0)
    def _():
        space_proj_out[...] = space_proj_ref[...].astype(F32)
        time_proj_out[...] = time_proj_ref[...].astype(F32)


def finish(matrices):
    width = matrices.shape[1]
    groups = width // WIDE
    one = lambda at: pl.BlockSpec((None, width, width), lambda i: (at, 0, 0))
    block = pl.BlockSpec((width, width), lambda i: (0, i))
    full = jax.ShapeDtypeStruct((width, 3 * width), F32)
    square = jax.ShapeDtypeStruct((width, width), F32)
    return pl.pallas_call(
        finish_body,
        grid=(3,),
        in_specs=[
            pl.BlockSpec((groups, width, WIDE), lambda i: (0, 0, i)),
            pl.BlockSpec((None, width, width), lambda i: (groups + i, 0, 0)), one(groups + 3), one(groups + 4),
        ],
        out_specs=[block, block, fixed((width, width)), fixed((width, width))],
        out_shape=[full, full, square, square],
        cost_estimate=pl.CostEstimate(flops=1 * 10**9, bytes_accessed=30 * MIB, transcendentals=0),
        compiler_params=params(),
        name="finish",
    )(matrices, matrices, matrices, matrices)


MESH = pl.DeviceIdType.MESH
EARLY_GAP = 3.0
HOP = 4.0


def bits_of(count):
    return [1 << i for i in range(count.bit_length() - 1)]


def reducible(width, planes, parts):
    return parts == 4 and planes >= 4 and planes & (planes - 1) == 0 and width % (planes * 2 * 16) == 0


class Ring:
    def __init__(self, planes):
        self.bits = bits_of(planes)
        self.deep = len(self.bits)
        self.plane, self.part = lax.axis_index("dp"), lax.axis_index("mp")
        self.by_bit = {bit: {"dp": self.plane + bit - 2 * bit * self.place(bit)} for bit in self.bits}
        self.beside = {"mp": self.part + 1 - 2 * (self.part % 2)}
        self.across = {"mp": 3 - self.part}
        self.third = {"mp": (self.part + 2) % 4}
        self.inner = ((self.part + 1) // 2) % 2 == 1
        self.outer = ((self.part + 1) // 2) % 2 == 0
        self.started = []

    def place(self, bit):
        return (self.plane // bit) % 2

    def greet(self):
        partners = [self.by_bit[bit] for bit in self.bits] + [self.beside, self.across, self.third]
        barrier = pltpu.get_barrier_semaphore()
        for partner in partners:
            pl.semaphore_signal(barrier, inc=1, device_id=partner, device_id_type=MESH)
        pl.semaphore_wait(barrier, len(partners))

    def order(self, stream):
        return self.bits if stream == 0 else self.bits[:1] + self.bits[1:][::-1]

    def send(self, source, target, sems, at, partner, when=None):
        send_sem, recv_sem = sems
        copy = pltpu.make_async_remote_copy(
            src_ref=source, dst_ref=target, send_sem=send_sem.at[at], recv_sem=recv_sem.at[at],
            device_id=partner, device_id_type=MESH,
        )
        if when is None:
            copy.start()
        else:
            pl.when(when)(copy.start)
        self.started.append((when, copy))
        return copy

    def finish(self):
        for when, copy in self.started:
            if when is None:
                copy.wait_send()
            else:
                pl.when(when)(copy.wait_send)

    def rows(self, chain, level, width):
        stream = chain % 2
        mine = self.order(stream)
        size = width // 2
        spot, length = self.place(mine[0]) * size + stream * (size // 2), size // 2
        for bit in mine[1:level]:
            length //= 2
            spot = spot + self.place(bit) * length
        return spot, length


def rows_at(offset, size):
    return pl.ds(pl.multiple_of(offset, 16), size)


class Reduction:
    def __init__(self, ring, own, got, line, piece, out, spots, sems, back_sems, out_sem):
        self.ring, self.own, self.got, self.line, self.piece, self.sems = ring, own, got, line, piece, sems
        self.out, self.spots, self.back_sems, self.out_sem = out, spots, back_sems, out_sem
        self.width = own.shape[1]
        self.waiting = {}
        self.local = {}
        self.steps = 2 * ring.deep + 4

    def back(self, chain, step):
        ring, matrix = self.ring, chain // 2
        level = ring.deep - step
        if step == 0:
            spot, length = ring.rows(chain, level, self.width)
            source, region = self.piece.at[chain], self.out.at[self.spots[matrix], rows_at(spot, length)]
            self.local[chain] = pltpu.make_async_copy(source, region, self.out_sem.at[chain])
            self.local[chain].start()
        else:
            if step == 1:
                self.local[chain].wait()
            self.waiting[chain].wait_recv()
            if step == ring.deep:
                return
            spot, length = ring.rows(chain, level, self.width)
            source = region = self.out.at[self.spots[matrix], rows_at(spot, length)]
        partner = ring.by_bit[ring.order(chain % 2)[level - 1]]
        self.waiting[chain] = ring.send(source, region, self.back_sems, (chain, step), partner)

    def advance(self, chain, step):
        ring, deep = self.ring, self.ring.deep
        matrix, stream = chain // 2, chain % 2
        mine = ring.order(stream)
        size = self.width // 2
        got = self.got
        if step < deep or step == deep:
            if step == 0:
                spot = (1 - ring.place(mine[0])) * size + stream * (size // 2)
                source = self.own.at[matrix, rows_at(spot, size // 2)]
            else:
                self.waiting[chain].wait_recv()
                count = got[step - 1].shape[1]
                if step == 1:
                    kept = self.own[matrix, rows_at(ring.place(mine[0]) * size + stream * (size // 2), count), :]
                else:
                    kept = got[step - 2][chain, rows_at(ring.place(mine[step - 1]) * count, count), :]
                got[step - 1][chain] = (kept.astype(F32) + got[step - 1][chain].astype(F32)).astype(BF16)
                if step < deep:
                    half = count // 2
                    source = got[step - 1].at[chain, rows_at((1 - ring.place(mine[step])) * half, half)]
            if step < deep:
                self.waiting[chain] = ring.send(
                    source, got[step].at[chain], self.sems, (chain, step), ring.by_bit[mine[step]]
                )
                return
        if step <= deep + 3:
            self.line.advance(chain, step - deep, got[deep - 1].at[chain])
        if step >= deep + 3:
            self.back(chain, step - deep - 3)


class Line:
    def __init__(self, ring, lines, piece, sems, first=0):
        self.ring, self.lines, self.piece, self.sems, self.first = ring, lines, piece, sems, first
        self.waiting = {}

    def advance(self, chain, step, source):
        ring, lines, at = self.ring, self.lines, chain - self.first
        if step == 0:
            self.waiting[chain] = ring.send(source, lines[0].at[at], self.sems, (at, 0), ring.beside, ring.outer)
        elif step == 1:
            first = self.waiting[chain]

            @pl.when(ring.inner)
            def _():
                first.wait_recv()
                lines[0][at] = (source[...].astype(F32) + lines[0][at].astype(F32)).astype(BF16)

            self.waiting[chain] = ring.send(lines[0].at[at], lines[1].at[at], self.sems, (at, 1), ring.across, ring.inner)
        elif step == 2:
            second = self.waiting[chain]

            @pl.when(ring.inner)
            def _():
                second.wait_recv()
                both = (lines[0][at].astype(F32) + lines[1][at].astype(F32)).astype(BF16)
                self.piece[chain - self.first] = both
                lines[2][at] = both

            self.waiting[chain] = ring.send(lines[2].at[at], lines[3].at[at], self.sems, (at, 2), ring.beside, ring.inner)
        else:
            third = self.waiting[chain]

            @pl.when(ring.outer)
            def _():
                third.wait_recv()
                self.piece[chain - self.first] = lines[3][at]


def reduction_scratch(chains, width, deep):
    length = width // 4
    sizes = [length >> i for i in range(deep)]
    shapes = [pltpu.VMEM((chains, size, width), BF16) for size in sizes + [sizes[-1]] * 4]
    return shapes + [pltpu.SemaphoreType.DMA((chains, deep))] * 2 + [pltpu.SemaphoreType.DMA((chains, 3))] * 2 + [
        pltpu.SemaphoreType.DMA((chains, deep))
    ] * 2 + [pltpu.SemaphoreType.DMA((chains,)), pltpu.VMEM((chains, sizes[-1], width), BF16)]


def temporal_tail_body(
    gain_ref, shift_ref, small_in, *refs, planes, early, taken, local,
):
    g_refs, (x_hbm, q_hbm, k_hbm, v_hbm, w_hbm), refs = refs[:local], refs[local : local + 5], refs[local + 5 :]
    early_hbm, refs = refs[:early], refs[early:]
    moved_ref, out_ref, small_out, refs = refs[0], refs[1], refs[2], refs[3:]
    x_ref, qkv_ref, w_ref, d_ref, dx_ref, own, load_sem, refs = *refs[:7], refs[7:]
    move_send, move_recv, move_local, small_ref, small_got, small_held, small_send, small_recv, refs = *refs[:8], refs[8:]
    ring = Ring(planes)
    deep = ring.deep
    got, lines, refs = refs[:deep], refs[deep : deep + 4], refs[deep + 4 :]
    sems, line_sems, back_sems, out_sem, piece_ref = refs[:2], refs[2:4], refs[4:6], refs[6], refs[7]
    frames, slots, width = x_ref.shape
    groups = width // WIDE
    rows = frames * STEP
    loads = {}

    def load(name, source, target, at):
        copy = pltpu.make_async_copy(source, target, load_sem.at[at])
        copy.start()
        loads[name] = copy

    def load_group(group):
        for place, ref in enumerate((q_hbm, k_hbm, v_hbm)):
            source = ref.at[:, :, pl.ds(group * WIDE, WIDE)]
            load(("qkv", group, place), source, qkv_ref.at[group % 2, place], early + 2 + 3 * group + place)

    load_group(0)
    for matrix in range(early):
        load(("own", matrix), early_hbm[matrix], own.at[matrix], matrix)
    load("x", x_hbm, x_ref, early)
    load("w", w_hbm, w_ref, early + 1)
    ring.greet()
    matrices = early + groups
    line = Line(ring, lines, piece_ref, line_sems)
    spots = [groups + matrix for matrix in range(early)] + list(range(groups))
    sums = Reduction(ring, own, got, line, piece_ref, out_ref, spots, sems, back_sems, out_sem)
    small_ref[...] = small_in[...]

    row = lax.broadcasted_iota(jnp.int32, (rows, rows), 0)
    col = lax.broadcasted_iota(jnp.int32, (rows, rows), 1)
    same = row % STEP == col % STEP
    shape = (frames, STEP, WIDE)
    starts = {}
    ready = {}

    def compute():
        for group in range(groups):
            if group + 1 < groups:
                load_group(group + 1)
            for place in range(3):
                loads[("qkv", group, place)].wait()
            slot = group % 2
            lanes = slice(group * WIDE, (group + 1) * WIDE)
            for step in range(slots // STEP):
                part = slice(step * STEP, (step + 1) * STEP)
                k = qkv_ref[slot, 1, :, part, :].reshape(rows, WIDE)
                v = qkv_ref[slot, 2, :, part, :].reshape(rows, WIDE)
                queries = stacked(qkv_ref[slot, 0, :, part, :].reshape(rows, WIDE), rows)
                grads = jnp.stack([g_ref[:, part, lanes] for g_ref in g_refs], axis=1)
                grads = stacked(grads.reshape(rows, WIDE), rows)
                scores = dot_nt(k, queries)
                grad_mixing = dot_nt(v, grads)
                mixing, grad_scores = [], []
                for head in range(GROUP):
                    span = slice(head * rows, (head + 1) * rows)
                    s = jnp.where(same, scores[:, span], -1e30)
                    e = jnp.exp(s - jnp.max(s, axis=0, keepdims=True))
                    p = e / jnp.sum(e, axis=0, keepdims=True)
                    gp = grad_mixing[:, span]
                    ds = p * (gp - jnp.sum(p * gp, axis=0, keepdims=True))
                    mixing.append(p.astype(BF16))
                    grad_scores.append(ds.astype(BF16))
                grad_scores = jnp.concatenate(grad_scores, axis=1)
                dv = dot(jnp.concatenate(mixing, axis=1), grads)
                dk = dot(grad_scores, queries)
                spread = dot_tn(grad_scores, k)
                dq = jnp.zeros((rows, WIDE), F32)
                for head in range(GROUP):
                    dq = dq + spread[head * rows : (head + 1) * rows] * head_lanes(rows, head, F32)
                d_ref[group, :, part, :WIDE] = (dq * HEAD_DIM**-0.5).astype(BF16).reshape(shape)
                d_ref[group, :, part, WIDE : 2 * WIDE] = dk.astype(BF16).reshape(shape)
                d_ref[group, :, part, 2 * WIDE :] = dv.astype(BF16).reshape(shape)
                if step % 4 == 3:
                    yield 2.0
            if group == 0:
                loads["x"].wait()
            d = d_ref[group].reshape(frames * slots, 3 * WIDE)
            x = x_ref[...].reshape(frames * slots, width)
            own[early + group] = dot_tn(x, d).astype(BF16)
            ready[early + group] = True
            yield 4.5
            small_ref[taken : taken + 1, lanes] = column_sum(d[:, :WIDE])
            small_ref[taken + 1 : taken + 2, lanes] = column_sum(d[:, 2 * WIDE :])
        loads["w"].wait()
        quarter = frames // 4
        shift_grad, product = jnp.zeros((1, width), F32), jnp.zeros((1, width), F32)
        for distance in (2, 3, 1, 0):
            part = (ring.part + distance) % 4
            some = pl.ds(part * quarter, quarter)
            total = jnp.zeros((quarter * slots, width), F32)
            for group in range(groups):
                d = d_ref[group, some].reshape(quarter * slots, 3 * WIDE)
                for place in range(3):
                    weight = w_ref[:, pl.ds(place * width + group * WIDE, WIDE)]
                    total = total + dot_nt(d[:, place * WIDE : (place + 1) * WIDE], weight)
            dx_ref[some] = total.astype(BF16).reshape(quarter, slots, width)
            if distance:
                moves.append(move(distance))
                moves[-1].start()
            else:
                keep = pltpu.make_async_copy(dx_ref.at[some], moved_ref.at[ring.part], move_local.at[0])
                keep.start()
                kept.append(keep)
            x = x_ref[some].reshape(quarter * slots, width)
            shift_grad += column_sum(total)
            product += column_sum(total * x.astype(F32))
            yield 3.5
        small_ref[taken + 2 : taken + 3, :] = (product - shift_ref[...][None] * shift_grad) / gain_ref[...][None]
        small_ref[taken + 3 : taken + 4, :] = shift_grad

    moves, kept = [], []

    def move(distance, arriving=False):
        target = (ring.part + distance) % 4
        source = (ring.part + 4 - distance) % 4 if arriving else ring.part
        return pltpu.make_async_remote_copy(
            src_ref=dx_ref.at[pl.ds(target * (frames // 4), frames // 4)], dst_ref=moved_ref.at[source],
            send_sem=move_send.at[distance], recv_sem=move_recv.at[source], device_id={"mp": target}, device_id_type=MESH,
        )

    partners = [ring.by_bit[bit] for bit in ring.bits] + [ring.beside, ring.third]
    small_wait = []

    def small_step(step):
        if step > 0:
            small_wait.pop().wait_recv()
            before = small_ref[...] if step == 1 else small_held[step - 2]
            value = before + small_got[step - 1]
            if step == len(partners):
                small_out[...] = value
                return
            small_held[step - 1] = value
        source = small_ref if step == 0 else small_held.at[step - 1]
        small_wait.append(ring.send(source, small_got.at[step], (small_send, small_recv), step, partners[step]))

    following = [0] * matrices
    due = [EARLY_GAP * matrix for matrix in range(matrices)]
    clock = 0.0

    def advance_all():
        for matrix in range(matrices):
            step = following[matrix]
            if step < sums.steps and clock >= due[matrix] and (matrix < early or matrix in ready):
                if step == 0 and matrix < early:
                    loads[("own", matrix)].wait()
                for chain in (2 * matrix, 2 * matrix + 1):
                    sums.advance(chain, step)
                following[matrix] += 1
                due[matrix] = clock + HOP

    advance_all()
    for spent in compute():
        clock += spent
        advance_all()
    small_at = 0
    while any(step < sums.steps for step in following) or small_at <= len(partners):
        clock += HOP
        advance_all()
        if small_at <= len(partners):
            small_step(small_at)
            small_at += 1
    for distance in (1, 2, 3):
        move(distance, True).wait_recv()
    for copy in moves:
        copy.wait_send()
    kept[0].wait()
    ring.finish()


def temporal_tail(x, q, k, v, grad, weight, gain, shift, early, small, taken, planes, number):
    frames, slots, width = x.shape
    groups = width // WIDE
    deep = len(bits_of(planes))
    chains = 2 * (len(early) + groups)
    anywhere = pl.BlockSpec(memory_space=pl.ANY)
    whole = pl.BlockSpec(memory_space=pltpu.VMEM)
    flops = 2 * frames * slots * width * width * 12
    return pl.pallas_call(
        functools.partial(temporal_tail_body, planes=planes, early=len(early), taken=taken, local=len(grad)),
        in_specs=[whole] * (3 + len(grad)) + [anywhere] * (5 + len(early)),
        out_specs=[anywhere, anywhere, whole],
        out_shape=[
            jax.ShapeDtypeStruct((4, frames // 4, slots, width), BF16),
            jax.ShapeDtypeStruct((len(early) + groups, width, width), BF16),
            jax.ShapeDtypeStruct(small.shape, F32),
        ],
        scratch_shapes=[
            pltpu.VMEM(x.shape, BF16), pltpu.VMEM((2, 3, frames, slots, WIDE), BF16), pltpu.VMEM(weight.shape, BF16),
            pltpu.VMEM((groups, frames, slots, 3 * WIDE), BF16), pltpu.VMEM(x.shape, BF16),
            pltpu.VMEM((len(early) + groups, width, width), BF16),
            pltpu.SemaphoreType.DMA((len(early) + 2 + 3 * groups,)),
            pltpu.SemaphoreType.DMA((4,)), pltpu.SemaphoreType.DMA((4,)), pltpu.SemaphoreType.DMA((1,)),
            pltpu.VMEM(small.shape, F32), pltpu.VMEM((deep + 2,) + small.shape, F32), pltpu.VMEM((deep + 1,) + small.shape, F32),
            pltpu.SemaphoreType.DMA((deep + 2,)), pltpu.SemaphoreType.DMA((deep + 2,)),
        ] + reduction_scratch(chains, width, deep),
        cost_estimate=pl.CostEstimate(flops=flops, bytes_accessed=60 * MIB, transcendentals=0),
        compiler_params=pltpu.CompilerParams(vmem_limit_bytes=62 * MIB, collective_id=number, has_side_effects=True),
        name="temporal_tail",
    )(gain, shift, small, *grad, x, q, k, v, weight, *early)


def middle_and_space(frame, mixed, video, proj, proj_bias, gain, shift, weight, bias, patch_width):
    first, normed, qkv = middle(frame, mixed, video, proj, proj_bias, gain, shift, weight, bias)
    space_mixed, lse = spatial_fwd(patch_width, qkv, 1, video.shape[1])
    return first, normed, qkv, space_mixed, lse


def shards(
    video,
    patch_width,
    temporal_gain,
    temporal_shift,
    temporal_qkv,
    temporal_qv_bias,
    temporal_proj,
    temporal_proj_bias,
    spatial_gain,
    spatial_shift,
    spatial_qkv,
    spatial_qv_bias,
    spatial_proj,
    spatial_proj_bias,
    mlp_gain,
    mlp_shift,
    fc1_weight,
    fc1_bias,
    fc2_weight,
    fc2_bias,
    cotangent,
):
    frames, sets, slots, width = video.shape
    units = fc1_weight.shape[1]
    parts, planes = lax.axis_size("mp"), lax.axis_size("dp")
    share = -(-slots // (parts * STEP)) * STEP
    row = lambda value: value.astype(F32).reshape(1, -1)
    video = video.reshape(frames * sets, slots, width)
    cot = cotangent.reshape(frames * sets, slots, width)

    joint = jnp.concatenate([fc1_weight, fc2_weight.T], axis=1)
    piece = width // planes
    own = lax.dynamic_slice_in_dim(joint, lax.axis_index("dp") * piece, piece, 0)
    bias_rows = jnp.pad(fc1_bias.reshape(1, units), ((0, 15), (0, units)))
    own = jnp.concatenate([own, bias_rows], axis=0)[None]

    def exchange(value):
        return lax.all_to_all(value, "mp", split_axis=0, concat_axis=0, tiled=True)

    by_position = lambda value: value.reshape(parts * frames, share, width)
    by_device = lambda value: value.reshape(parts, frames, share, width)
    normed_in = norm_in(video, temporal_gain, temporal_shift, parts, share)
    x = by_position(exchange(normed_in))
    own, x = lax.optimization_barrier((own, x))
    column = lax.all_gather(own, "mp", axis=0, tiled=True)
    tq, tk, tv, *time_mixed = temporal_fwd(x, temporal_qkv, row(temporal_qv_bias), frames)
    column, *time_mixed = lax.optimization_barrier((column, *time_mixed))
    fb1 = column[:, piece : piece + 1, :units].astype(F32)
    joint = lax.all_gather(column[:, :piece], "dp", axis=1, tiled=True)
    time_back = [exchange(value) for value in time_mixed]

    several = lambda results: [list(values) for values in zip(*results)]
    spatial = []
    for f in range(frames):
        if f > 0:
            time_back[f], lse_before = lax.optimization_barrier((time_back[f], spatial[-1][-1]))
            spatial[-1] = spatial[-1][:-1] + (lse_before,)
        spatial.append(
            middle_and_space(
                f, time_back[f], video, temporal_proj, temporal_proj_bias, spatial_gain, spatial_shift, spatial_qkv,
                row(spatial_qv_bias), patch_width,
            )
        )
    first, normed_mid, space_qkv, space_mixed, lse = several(spatial)

    output, normed_out, hidden, grad_inner, grad_second, grad_space_out, grad_space, feed_sums, unit_sums = feed(
        first, [value[0] for value in space_mixed], cot, spatial_proj, spatial_proj_bias, mlp_gain, mlp_shift, joint, fb1, fc2_bias
    )
    fc_part = fc_grads(normed_out, cot, grad_inner, hidden)
    fc_part = lax.psum_scatter(fc_part, "dp", scatter_dimension=1, tiled=True)

    dq, dk, dv, grad_first, grad_time_out, mid_sums, grad_slot = [], [], [], [], [], [], []
    for f in range(frames):
        q_f, k_f, v_f = spatial_bwd(f, patch_width, space_qkv[f], space_mixed[f], lse[f], grad_space, 1, slots)
        if f > 0:
            grad_slot[-1], q_f = lax.optimization_barrier((grad_slot[-1], q_f))
        first_f, out_f, time_f, sums_f = middle_bwd(
            f, q_f[0], k_f[0], v_f[0], spatial_qkv, first[f], grad_second, spatial_gain, temporal_proj, parts, share
        )
        if f + 1 < frames:
            time_f, grad_space = lax.optimization_barrier((time_f, grad_space))
        grad_slot.append(exchange(time_f))
        for kept, value in zip(
            (dq, dk, dv, grad_first, grad_time_out, mid_sums), (q_f[0], k_f[0], v_f[0], first_f, out_f, sums_f)
        ):
            kept.append(value)
    early = [
        weight_grad(normed_mid, dq),
        weight_grad(normed_mid, dk),
        weight_grad(normed_mid, dv),
        weight_grad([value[0] for value in space_mixed], grad_space_out.reshape(-1, width)),
        weight_grad(time_back, grad_time_out),
    ]
    fc_part, grad_first[-1] = lax.optimization_barrier((fc_part, grad_first[-1]))
    fc_part = lax.psum_scatter(fc_part, "mp", scatter_dimension=0, tiled=True)[0].astype(F32)
    fc1_weight_grad = fc_part[:, :units]
    fc2_weight_grad = fc_part[:, units:].T

    own_sums = [unit_sums[:, 0, :].reshape(-1, width), feed_sums[:4], sum(mid_sums)[:5]]
    weights = (temporal_qkv, temporal_gain, temporal_shift)
    wide = lambda blocks: jnp.concatenate([block.astype(F32) for block in blocks], axis=1)
    if reducible(width, planes, parts):
        taken = sum(rows.shape[0] for rows in own_sums)
        small = jnp.concatenate(own_sums + [jnp.zeros((4 + -(taken + 4) % 8, width), F32)], axis=0)
        grad_in, matrices, small = temporal_tail(x, tq, tk, tv, grad_slot, *weights, early, small, taken, planes, 1)
        temporal_qkv_grad, spatial_qkv_grad, spatial_proj_grad, temporal_proj_grad = finish(matrices)
    else:
        gq, gk, gv, grad_x, bias_sums, norm_sums = temporal_bwd(x, tq, tk, tv, by_position(jnp.stack(grad_slot, axis=1)), *weights)
        grad_in = exchange(by_device(grad_x))
        small = jnp.concatenate(own_sums + [bias_sums[:2], norm_sums[:2]], axis=0)
        flat = lambda value: value.reshape(-1, width)
        late = [weight_grad([flat(x)], [flat(value)]) for value in (gq, gk, gv)]
        matrices, small = lax.psum((jnp.stack(early + late), small), ("dp", "mp"))
        temporal_qkv_grad = wide([matrices[5 + p] for p in range(3)])
        spatial_qkv_grad = wide([matrices[p] for p in range(3)])
        spatial_proj_grad, temporal_proj_grad = matrices[3].astype(F32), matrices[4].astype(F32)
    video_grad = norm_out(grad_in, video, grad_first, temporal_gain)
    count = parts * units // width
    fc1_bias_grad = small[:count].reshape(-1)
    (
        mlp_gain_grad, mlp_shift_grad, spatial_proj_bias_grad, fc2_bias_grad,
        spatial_gain_grad, spatial_shift_grad, space_q_sum, space_v_sum, temporal_proj_bias_grad,
        time_q_sum, time_v_sum, temporal_gain_grad, temporal_shift_grad,
    ) = [small[count + i] for i in range(13)]
    return (
        output.reshape(frames, sets, slots, width),
        video_grad.reshape(frames, sets, slots, width),
        temporal_gain_grad,
        temporal_shift_grad,
        temporal_qkv_grad,
        jnp.concatenate([time_q_sum, time_v_sum]),
        temporal_proj_grad,
        temporal_proj_bias_grad,
        spatial_gain_grad,
        spatial_shift_grad,
        spatial_qkv_grad,
        jnp.concatenate([space_q_sum, space_v_sum]),
        spatial_proj_grad,
        spatial_proj_bias_grad,
        mlp_gain_grad,
        mlp_shift_grad,
        fc1_weight_grad,
        fc1_bias_grad,
        fc2_weight_grad,
        fc2_bias_grad,
    )


def solution(mesh):
    tokens = P("mp", "dp", None, None)
    return jax.shard_map(
        shards,
        mesh=mesh,
        in_specs=(tokens, P("dp")) + (P(),) * 14 + (P(None, "mp"), P("mp"), P("mp", None), P(), tokens),
        out_specs=(tokens, tokens) + (P(),) * 14 + (P("dp", "mp"), P(), P("mp", "dp"), P()),
        check_vma=False,
    )
```

```python
import functools
import jax
import jax.numpy as jnp
from jax import lax
from jax.experimental import pallas as pl
from jax.experimental.pallas import tpu as pltpu
from jax.sharding import PartitionSpec as P

HEADS = 12
HEAD_DIM = 64
GROUP = 4
WIDE = GROUP * HEAD_DIM
EPSILON = 1e-06
F32 = jnp.float32
BF16 = jnp.bfloat16
MIB = 1 << 20


def params(mib=56):
    return pltpu.CompilerParams(vmem_limit_bytes=mib * MIB)


def dot(a, b):
    return jnp.dot(a, b, preferred_element_type=F32)


def dot_nt(a, b):
    return lax.dot_general(a, b, (((1,), (1,)), ((), ())), preferred_element_type=F32)


def dot_tn(a, b):
    return lax.dot_general(a, b, (((0,), (0,)), ((), ())), preferred_element_type=F32)


def head_lanes(rows, head, dtype):
    lane = lax.broadcasted_iota(jnp.int32, (rows, WIDE), 1)
    return (lane // HEAD_DIM == head).astype(dtype)


def windows(slots, clips, rows):
    size = slots // clips
    found = []
    for start in range(0, slots, rows):
        stop = min(start + rows, slots)
        low = start // size * size // 16 * 16
        high = min(-(-(-(-stop // size) * size) // 16) * 16, slots)
        found.append((start, stop, low, high))
    return found


def spatial_fwd_body(width_ref, q_ref, k_ref, v_ref, o_ref, l_ref, *, slots, rows, narrow):
    def attend(chunks, size):
        stats = []
        for start, stop, low, high in chunks:
            count = stop - start
            q = q_ref[start:stop, :]
            k = k_ref[low:high, :]
            v = v_ref[low:high, :]
            if size < slots:
                query_clip = (lax.broadcasted_iota(jnp.int32, (count, high - low), 0) + start) // size
                key_clip = (lax.broadcasted_iota(jnp.int32, (count, high - low), 1) + low) // size
                same = query_clip == key_clip
            total = jnp.zeros((count, WIDE), F32)
            lse = jnp.zeros((count, 128), F32)
            lane = lax.broadcasted_iota(jnp.int32, (count, 128), 1)
            for head in range(GROUP):
                s = dot_nt(q * head_lanes(count, head, BF16), k)
                if size < slots:
                    s = jnp.where(same, s, -1e30)
                top = jnp.max(s, axis=1, keepdims=True)
                e = jnp.exp(s - top)
                norm = jnp.sum(e, axis=1, keepdims=True)
                o = dot(e.astype(BF16), v)
                total = total + o * (head_lanes(count, head, F32) / norm)
                lse = jnp.where(lane == head, top + jnp.log(norm), lse)
            o_ref[start:stop, :] = total.astype(BF16)
            stats.append(lse)
        l_ref[...] = jnp.concatenate(stats, axis=0).T[:8, :]

    wide = width_ref[0] == slots

    @pl.when(wide)
    def _():
        attend(windows(slots, 1, rows or slots), slots)

    @pl.when(jnp.logical_not(wide))
    def _():
        attend(windows(slots, 4, narrow), slots // 4)


def spatial_fwd(width, qkv, frames, slots, rows=None, narrow=256):
    groups = HEADS // GROUP
    qkv = qkv.reshape(frames, slots, -1)
    spec = lambda part: pl.BlockSpec((None, slots, WIDE), lambda f, g, w: (f, 0, part * groups + g))
    out = pl.pallas_call(
        functools.partial(spatial_fwd_body, slots=slots, rows=rows, narrow=narrow),
        grid_spec=pltpu.PrefetchScalarGridSpec(
            num_scalar_prefetch=1,
            grid=(frames, groups),
            in_specs=[spec(0), spec(1), spec(2)],
            out_specs=[
                pl.BlockSpec((None, slots, WIDE), lambda f, g, w: (f, 0, g)),
                pl.BlockSpec((None, None, 8, slots), lambda f, g, w: (f, g, 0, 0)),
            ],
        ),
        out_shape=[
            jax.ShapeDtypeStruct((frames, slots, HEADS * HEAD_DIM), BF16),
            jax.ShapeDtypeStruct((frames, groups, 8, slots), F32),
        ],
        cost_estimate=pl.CostEstimate(flops=20 * 10**9, bytes_accessed=5 * MIB, transcendentals=0),
        compiler_params=params(),
        name="spatial_fwd",
    )(width, qkv, qkv, qkv)
    return out


def spatial_bwd_body(width_ref, q_ref, k_ref, v_ref, o_ref, l_ref, g_ref, dq_ref, dk_ref, dv_ref, dqt, *, slots, rows, narrow):
    prod = g_ref[...].astype(F32) * o_ref[...].astype(F32)
    high_part = prod.astype(BF16)
    low_part = (prod - high_part.astype(F32)).astype(BF16)
    lane = lax.broadcasted_iota(jnp.int32, (8, WIDE), 1)
    row = lax.broadcasted_iota(jnp.int32, (8, WIDE), 0)
    picks = (lane // HEAD_DIM == row).astype(BF16)
    delta = dot_nt(picks, high_part) + dot_nt(picks, low_part)

    def attend(chunks, size):
        dqt[...] = jnp.zeros_like(dqt)
        kt = k_ref[...].T
        for start, stop, low, high in chunks:
            count = stop - start
            k = k_ref[start:stop, :]
            v = v_ref[start:stop, :]
            q = q_ref[low:high, :]
            g = g_ref[low:high, :]
            if size < slots:
                key_clip = (lax.broadcasted_iota(jnp.int32, (count, high - low), 0) + start) // size
                query_clip = (lax.broadcasted_iota(jnp.int32, (count, high - low), 1) + low) // size
                same = query_clip == key_clip
            dk = jnp.zeros((count, WIDE), F32)
            dv = jnp.zeros((count, WIDE), F32)
            for head in range(GROUP):
                mask = head_lanes(count, head, BF16)
                s = dot_nt(k * mask, q)
                p = jnp.exp(s - l_ref[head : head + 1, low:high])
                if size < slots:
                    p = jnp.where(same, p, 0.0)
                dp = dot_nt(v * mask, g)
                ds = (p * (dp - delta[head : head + 1, low:high])).astype(BF16)
                keep = head_lanes(count, head, F32)
                dv = dv + dot(p.astype(BF16), g) * keep
                dk = dk + dot(ds, q) * keep
                span = slice(head * HEAD_DIM, (head + 1) * HEAD_DIM)
                dqt[span, low:high] += dot(kt[span, start:stop], ds)
            dk_ref[start:stop, :] = dk.astype(BF16)
            dv_ref[start:stop, :] = dv.astype(BF16)
        dq_ref[...] = (dqt[...] * HEAD_DIM**-0.5).T.astype(BF16)

    wide = width_ref[0] == slots

    @pl.when(wide)
    def _():
        attend(windows(slots, 1, rows or slots), slots)

    @pl.when(jnp.logical_not(wide))
    def _():
        attend(windows(slots, 4, narrow), slots // 4)


def spatial_bwd(frame, width, qkv, mixed, lse, grad, frames, slots, rows=None, narrow=208):
    groups = HEADS // GROUP
    width_all = HEADS * HEAD_DIM
    qkv = qkv.reshape(frames, slots, -1)
    spec = lambda part: pl.BlockSpec((None, slots, WIDE), lambda f, g, w: (f, 0, part * groups + g))
    one = pl.BlockSpec((None, slots, WIDE), lambda f, g, w: (f, 0, g))
    out = pl.pallas_call(
        functools.partial(spatial_bwd_body, slots=slots, rows=rows, narrow=narrow),
        grid_spec=pltpu.PrefetchScalarGridSpec(
            num_scalar_prefetch=1,
            grid=(frames, groups),
            in_specs=[
                spec(0), spec(1), spec(2), one,
                pl.BlockSpec((None, None, 8, slots), lambda f, g, w: (f, g, 0, 0)),
                pl.BlockSpec((None, slots, WIDE), lambda f, g, w: (frame + f, 0, g)),
            ],
            out_specs=[one, one, one],
            scratch_shapes=[pltpu.VMEM((WIDE, slots), F32)],
        ),
        out_shape=[jax.ShapeDtypeStruct((frames, slots, width_all), BF16)] * 3,
        cost_estimate=pl.CostEstimate(flops=32 * 10**9, bytes_accessed=9 * MIB, transcendentals=0),
        compiler_params=params(),
        name="spatial_bwd",
    )(width, qkv, qkv, qkv, mixed, lse, grad)
    return out


def fixed(shape):
    return pl.BlockSpec(shape, lambda *_: (0,) * len(shape))


def norm_parts(value):
    centered = value - jnp.mean(value, axis=-1, keepdims=True)
    scale = lax.rsqrt(jnp.mean(centered * centered, axis=-1, keepdims=True) + EPSILON)
    return centered * scale, scale


def norm_grad(grad, unit, scale, gain):
    inner = grad * gain
    return scale * (
        inner
        - jnp.mean(inner, axis=-1, keepdims=True)
        - unit * jnp.mean(inner * unit, axis=-1, keepdims=True)
    )


def column_sum(value):
    return jnp.sum(value.astype(F32), axis=0, keepdims=True)


def by_part(parts, share, width):
    return pl.BlockSpec((parts, None, share, width), lambda f: (0, f, 0, 0))


def norm_in_body(video_ref, gain_ref, shift_ref, out_ref):
    unit, _ = norm_parts(video_ref[...].astype(F32))
    split_positions(out_ref, (unit * gain_ref[...] + shift_ref[...]).astype(BF16))


def split_positions(out_ref, value):
    parts, share, width = out_ref.shape
    slots = value.shape[0]
    for part in range(parts):
        start = part * share
        count = min(max(slots - start, 0), share)
        if count > 0:
            out_ref[part, :count, :] = value[start : start + count, :]
        if count < share:
            out_ref[part, count:, :] = jnp.zeros((share - count, width), value.dtype)


def joined_positions(ref, slots):
    parts, share, width = ref.shape
    return ref[...].reshape(parts * share, width)[:slots, :]


def norm_in(video, gain, shift, parts, share):
    frames, slots, width = video.shape
    return pl.pallas_call(
        norm_in_body,
        grid=(frames,),
        in_specs=[pl.BlockSpec((None, slots, width), lambda f: (f, 0, 0)), fixed((width,)), fixed((width,))],
        out_specs=by_part(parts, share, width),
        out_shape=jax.ShapeDtypeStruct((parts, frames, share, width), BF16),
        cost_estimate=pl.CostEstimate(flops=1 * 10**9, bytes_accessed=10 * MIB, transcendentals=0),
        compiler_params=params(),
        name="norm_in",
    )(video, gain, shift)


STEP = 16


def stacked(block, rows):
    return jnp.concatenate([block * head_lanes(rows, head, BF16) for head in range(GROUP)], axis=0)


def temporal_fwd_body(x_ref, wq_ref, wk_ref, wv_ref, bq_ref, bv_ref, q_ref, k_ref, v_ref, *o_refs):
    frames, slots, width = x_ref.shape
    x = x_ref[...].reshape(frames * slots, width)
    shape = (frames, slots, WIDE)
    q_ref[...] = ((dot(x, wq_ref[...]) + bq_ref[...]) * HEAD_DIM**-0.5).astype(BF16).reshape(shape)
    k_ref[...] = dot(x, wk_ref[...]).astype(BF16).reshape(shape)
    v_ref[...] = (dot(x, wv_ref[...]) + bv_ref[...]).astype(BF16).reshape(shape)
    rows = frames * STEP
    row = lax.broadcasted_iota(jnp.int32, (rows, rows), 0)
    col = lax.broadcasted_iota(jnp.int32, (rows, rows), 1)
    same = row % STEP == col % STEP
    for step in range(slots // STEP):
        part = slice(step * STEP, (step + 1) * STEP)
        q = q_ref[:, part, :].reshape(rows, WIDE)
        keys = stacked(k_ref[:, part, :].reshape(rows, WIDE), rows)
        values = stacked(v_ref[:, part, :].reshape(rows, WIDE), rows)
        scores = dot_nt(q, keys)
        mixing = []
        for head in range(GROUP):
            s = jnp.where(same, scores[:, head * rows : (head + 1) * rows], -1e30)
            e = jnp.exp(s - jnp.max(s, axis=1, keepdims=True))
            mixing.append((e / jnp.sum(e, axis=1, keepdims=True)).astype(BF16))
        o = dot(jnp.concatenate(mixing, axis=1), values)
        o = o.astype(BF16).reshape(frames // len(o_refs), len(o_refs), STEP, WIDE)
        for place, o_ref in enumerate(o_refs):
            o_ref[:, part, :] = o[:, place]


def temporal_fwd(x, weight, bias, local):
    frames, slots, width = x.shape
    groups = width // WIDE
    w = lambda part: pl.BlockSpec((width, WIDE), lambda g: (0, part * groups + g))
    b = lambda part: pl.BlockSpec((1, WIDE), lambda g: (0, part * groups + g))
    one = pl.BlockSpec((frames, slots, WIDE), lambda g: (0, 0, g))
    return pl.pallas_call(
        temporal_fwd_body,
        grid=(groups,),
        in_specs=[fixed(x.shape), w(0), w(1), w(2), b(0), b(1)],
        out_specs=[one] * 3 + [pl.BlockSpec((frames // local, slots, WIDE), lambda g: (0, 0, g))] * local,
        out_shape=[jax.ShapeDtypeStruct(x.shape, BF16)] * 3
        + [jax.ShapeDtypeStruct((frames // local, slots, width), BF16)] * local,
        cost_estimate=pl.CostEstimate(flops=30 * 10**9, bytes_accessed=16 * MIB, transcendentals=0),
        compiler_params=params(),
        name="temporal_fwd",
    )(x, weight, weight, weight, bias, bias)


def temporal_bwd_body(
    x_ref, q_ref, k_ref, v_ref, g_ref, wq_ref, wk_ref, wv_ref, gain_ref, shift_ref,
    dq_ref, dk_ref, dv_ref, dx_ref, sums_ref, norm_ref, total_ref,
):
    frames, slots, width = x_ref.shape
    rows = frames * STEP
    row = lax.broadcasted_iota(jnp.int32, (rows, rows), 0)
    col = lax.broadcasted_iota(jnp.int32, (rows, rows), 1)
    same = row % STEP == col % STEP
    shape = (frames, STEP, WIDE)
    for step in range(slots // STEP):
        part = slice(step * STEP, (step + 1) * STEP)
        k = k_ref[:, part, :].reshape(rows, WIDE)
        v = v_ref[:, part, :].reshape(rows, WIDE)
        queries = stacked(q_ref[:, part, :].reshape(rows, WIDE), rows)
        grads = stacked(g_ref[:, part, :].reshape(rows, WIDE), rows)
        scores = dot_nt(k, queries)
        grad_mixing = dot_nt(v, grads)
        mixing, grad_scores = [], []
        for head in range(GROUP):
            span = slice(head * rows, (head + 1) * rows)
            s = jnp.where(same, scores[:, span], -1e30)
            e = jnp.exp(s - jnp.max(s, axis=0, keepdims=True))
            p = e / jnp.sum(e, axis=0, keepdims=True)
            gp = grad_mixing[:, span]
            ds = p * (gp - jnp.sum(p * gp, axis=0, keepdims=True))
            mixing.append(p.astype(BF16))
            grad_scores.append(ds.astype(BF16))
        grad_scores = jnp.concatenate(grad_scores, axis=1)
        dv_ref[:, part, :] = dot(jnp.concatenate(mixing, axis=1), grads).astype(BF16).reshape(shape)
        dk_ref[:, part, :] = dot(grad_scores, queries).astype(BF16).reshape(shape)
        spread = dot_tn(grad_scores, k)
        dq = jnp.zeros((rows, WIDE), F32)
        for head in range(GROUP):
            dq = dq + spread[head * rows : (head + 1) * rows] * head_lanes(rows, head, F32)
        dq_ref[:, part, :] = (dq * HEAD_DIM**-0.5).astype(BF16).reshape(shape)
    flat = (frames * slots, WIDE)
    dq, dk, dv = dq_ref[...].reshape(flat), dk_ref[...].reshape(flat), dv_ref[...].reshape(flat)
    sums_ref[...] = jnp.concatenate([column_sum(dq), column_sum(dv), jnp.zeros((6, WIDE), F32)], axis=0)
    update = dot_nt(dq, wq_ref[...]) + dot_nt(dk, wk_ref[...]) + dot_nt(dv, wv_ref[...])
    group = pl.program_id(0)

    @pl.when(group == 0)
    def _():
        total_ref[...] = update

    @pl.when(group > 0)
    def _():
        total_ref[...] += update

    @pl.when(group == pl.num_programs(0) - 1)
    def _():
        total = total_ref[...]
        dx_ref[...] = total.astype(BF16).reshape(frames, slots, width)
        x = x_ref[...].reshape(frames * slots, width).astype(F32)
        shift_grad = column_sum(total)
        gain_grad = (column_sum(total * x) - shift_ref[...][None] * shift_grad) / gain_ref[...][None]
        norm_ref[...] = jnp.concatenate([gain_grad, shift_grad, jnp.zeros((6, width), F32)], axis=0)


def temporal_bwd(x, q, k, v, grad, weight, gain, shift):
    frames, slots, width = x.shape
    groups = width // WIDE
    w = lambda part: pl.BlockSpec((width, WIDE), lambda g: (0, part * groups + g))
    one = pl.BlockSpec((frames, slots, WIDE), lambda g: (0, 0, g))
    return pl.pallas_call(
        temporal_bwd_body,
        grid=(groups,),
        in_specs=[fixed(x.shape), one, one, one, one, w(0), w(1), w(2), fixed((width,)), fixed((width,))],
        out_specs=[one, one, one, fixed(x.shape), pl.BlockSpec((8, WIDE), lambda g: (0, g)), fixed((8, width))],
        out_shape=[jax.ShapeDtypeStruct(x.shape, BF16)] * 4 + [jax.ShapeDtypeStruct((8, width), F32)] * 2,
        scratch_shapes=[pltpu.VMEM((frames * slots, width), F32)],
        cost_estimate=pl.CostEstimate(flops=35 * 10**9, bytes_accessed=30 * MIB, transcendentals=0),
        compiler_params=params(),
        name="temporal_bwd",
    )(x, q, k, v, grad, weight, weight, weight, gain, shift)


def middle_body(mixed_ref, video_ref, proj_ref, pb_ref, gain_ref, shift_ref, w_ref, bias_ref, first_ref, normed_ref, qkv_ref):
    slots, width = video_ref.shape
    first = video_ref[...].astype(F32) + (dot(joined_positions(mixed_ref, slots), proj_ref[...]) + pb_ref[...])
    first_ref[...] = first
    unit, _ = norm_parts(first)
    normed_ref[...] = (unit * gain_ref[...] + shift_ref[...]).astype(BF16)
    normed = normed_ref[...]
    q = dot(normed, w_ref[:, :width]) + bias_ref[:, :width]
    qkv_ref[:, :width] = (q * HEAD_DIM**-0.5).astype(BF16)
    qkv_ref[:, width : 2 * width] = dot(normed, w_ref[:, width : 2 * width]).astype(BF16)
    qkv_ref[:, 2 * width :] = (dot(normed, w_ref[:, 2 * width :]) + bias_ref[:, width:]).astype(BF16)


def middle(frame, mixed, video, proj, proj_bias, gain, shift, weight, bias):
    _, slots, width = video.shape
    return pl.pallas_call(
        middle_body,
        grid=(1,),
        in_specs=[
            fixed(mixed.shape), pl.BlockSpec((None, slots, width), lambda i: (frame, 0, 0)), fixed(proj.shape), fixed((width,)),
            fixed((width,)), fixed((width,)), fixed(weight.shape), fixed((1, 2 * width)),
        ],
        out_specs=[fixed((slots, width)), fixed((slots, width)), fixed((slots, 3 * width))],
        out_shape=[
            jax.ShapeDtypeStruct((slots, width), F32),
            jax.ShapeDtypeStruct((slots, width), BF16),
            jax.ShapeDtypeStruct((slots, 3 * width), BF16),
        ],
        cost_estimate=pl.CostEstimate(flops=11 * 10**9, bytes_accessed=14 * MIB, transcendentals=0),
        compiler_params=params(),
        name="middle",
    )(mixed, video, proj, proj_bias, gain, shift, weight, bias)


def gelu_both(value):
    half = 0.5 * (1.0 + lax.erf(value * 0.7071067811865476))
    density = jnp.exp(-0.5 * value * value) * 0.3989422804014327
    return value * half, half + value * density


def feed_body(
    cot_ref, proj_ref, pb_ref, gain_ref, shift_ref, fc1_ref, fb1_ref, fc2_ref, fb2_ref, *refs, sub, frames,
):
    firsts, mixeds, refs = refs[:frames], refs[frames : 2 * frames], refs[2 * frames :]
    out_ref, normed_ref, hidden_ref, gi_ref, gs_ref, gso_ref, gspace_ref, sums_ref, unitsum_ref, second, branch, gnorm = refs
    frame, chunk = pl.program_id(0), pl.program_id(1)
    slots, width = cot_ref.shape
    units = fc1_ref.shape[1]
    for place in range(frames):

        @pl.when(jnp.logical_and(chunk == 0, frame == place))
        def _(place=place):
            second[...] = firsts[place][...] + (dot(mixeds[place][...], proj_ref[...]) + pb_ref[...])

    @pl.when(chunk == 0)
    def _():
        value = second[...]
        unit, _ = norm_parts(value)
        normed_ref[...] = (unit * gain_ref[...] + shift_ref[...]).astype(BF16)
        branch[...] = jnp.zeros_like(branch)
        gnorm[...] = jnp.zeros_like(gnorm)

    @pl.when(jnp.logical_and(frame == 0, chunk == 0))
    def _():
        sums_ref[...] = jnp.zeros_like(sums_ref)
        unitsum_ref[...] = jnp.zeros_like(unitsum_ref)

    normed = normed_ref[...]
    cot = cot_ref[...]
    for start in range(0, units, sub):
        span = slice(start, start + sub)
        inner = dot(normed, fc1_ref[:, span]) + fb1_ref[0:1, span]
        grad_hidden = dot(cot, fc2_ref[:, span])
        act, slope = gelu_both(inner)
        hidden_ref[:, span] = act.astype(BF16)
        gi_ref[:, span] = (grad_hidden * slope).astype(BF16)
    branch[...] += dot_nt(hidden_ref[...], fc2_ref[...])
    gnorm[...] += dot_nt(gi_ref[...], fc1_ref[...])
    unitsum_ref[chunk, 0:1, :] += column_sum(gi_ref[...])

    @pl.when(chunk == pl.num_programs(1) - 1)
    def _():
        value = second[...]
        out_ref[...] = (value + (branch[...] + fb2_ref[...])).astype(BF16)
        unit, scale = norm_parts(value)
        grad = gnorm[...]
        cot_full = cot_ref[...].astype(F32)
        grad_second = cot_full + norm_grad(grad, unit, scale, gain_ref[...])
        gs_ref[...] = grad_second
        gso_ref[...] = grad_second.astype(BF16)
        gspace_ref[...] = dot_nt(gso_ref[...], proj_ref[...]).astype(BF16)
        sums_ref[0:1, :] += column_sum(grad * unit)
        sums_ref[1:2, :] += column_sum(grad)
        sums_ref[2:3, :] += column_sum(gso_ref[...])
        sums_ref[3:4, :] += column_sum(cot_full)


def feed(first, mixed, cot, proj, proj_bias, gain, shift, joint, fc1_bias, fc2_bias, sub=None):
    frames, slots, width = cot.shape
    chunks, _, units = fc1_bias.shape
    sub = sub or units
    per = pl.BlockSpec((None, slots, width), lambda f, c: (f, 0, 0))
    row = fixed((width,))
    hid = pl.BlockSpec((None, None, slots, units), lambda f, c: (c, f, 0, 0))
    hid_shape = jax.ShapeDtypeStruct((chunks, frames, slots, units), BF16)
    tok = lambda dtype: jax.ShapeDtypeStruct(cot.shape, dtype)
    return pl.pallas_call(
        functools.partial(feed_body, sub=sub, frames=frames),
        grid=(frames, chunks),
        in_specs=[
            per, fixed(proj.shape), row, row, row,
            pl.BlockSpec((None, width, units), lambda f, c: (c, 0, 0)),
            pl.BlockSpec((None, 1, units), lambda f, c: (c, 0, 0)),
            pl.BlockSpec((None, width, units), lambda f, c: (c, 0, 1)),
            row,
        ] + [fixed((slots, width))] * (2 * frames),
        out_specs=[per, per, hid, hid, per, per, per, fixed((8, width)), fixed((chunks, 8, units))],
        out_shape=[
            tok(BF16), tok(BF16), hid_shape, hid_shape, tok(F32), tok(BF16), tok(BF16),
            jax.ShapeDtypeStruct((8, width), F32), jax.ShapeDtypeStruct((chunks, 8, units), F32),
        ],
        scratch_shapes=[pltpu.VMEM((slots, width), F32)] * 3,
        cost_estimate=pl.CostEstimate(flops=56 * 10**9, bytes_accessed=60 * MIB, transcendentals=0),
        compiler_params=params(60),
        name="feed",
    )(cot, proj, proj_bias, gain, shift, joint, fc1_bias, joint, fc2_bias, *first, *mixed)


def middle_bwd_body(
    dq_ref, dk_ref, dv_ref, w_ref, first_ref, gs_ref, gain_ref, proj_ref, gf_ref, gto_ref, gt_ref, sums_ref
):
    slots, width = first_ref.shape
    dq, dk, dv = dq_ref[...], dk_ref[...], dv_ref[...]
    grad = dot_nt(dq, w_ref[:, :width]) + dot_nt(dk, w_ref[:, width : 2 * width]) + dot_nt(dv, w_ref[:, 2 * width :])
    unit, scale = norm_parts(first_ref[...])
    grad_first = gs_ref[...] + norm_grad(grad, unit, scale, gain_ref[...])
    gf_ref[...] = grad_first
    gto_ref[...] = grad_first.astype(BF16)
    split_positions(gt_ref, dot_nt(gto_ref[...], proj_ref[...]).astype(BF16))

    rows = [grad * unit, grad, dq, dv, gto_ref[...]]
    sums_ref[...] = jnp.concatenate([column_sum(value) for value in rows] + [jnp.zeros((3, width), F32)], axis=0)


def middle_bwd(frame, dq, dk, dv, weight, first, grad_second, gain, proj, parts, share):
    slots, width = first.shape
    return pl.pallas_call(
        middle_bwd_body,
        grid=(1,),
        in_specs=[
            fixed((slots, width)), fixed((slots, width)), fixed((slots, width)), fixed(weight.shape), fixed((slots, width)),
            pl.BlockSpec((None, slots, width), lambda i: (frame, 0, 0)), fixed((width,)), fixed(proj.shape),
        ],
        out_specs=[fixed((slots, width)), fixed((slots, width)), fixed((parts, share, width)), fixed((8, width))],
        out_shape=[
            jax.ShapeDtypeStruct(first.shape, F32), jax.ShapeDtypeStruct(first.shape, BF16),
            jax.ShapeDtypeStruct((parts, share, width), BF16), jax.ShapeDtypeStruct((8, width), F32),
        ],
        cost_estimate=pl.CostEstimate(flops=14 * 10**9, bytes_accessed=16 * MIB, transcendentals=0),
        compiler_params=params(60),
        name="middle_bwd",
    )(dq, dk, dv, weight, first, grad_second, gain, proj)


def norm_out_body(grad_ref, video_ref, gain_ref, *refs):
    *gf_refs, out_ref = refs
    slots = video_ref.shape[0]
    frame = pl.program_id(0)
    unit, scale = norm_parts(video_ref[...].astype(F32))
    result = norm_grad(joined_positions(grad_ref, slots).astype(F32), unit, scale, gain_ref[...])
    for place, gf_ref in enumerate(gf_refs):

        @pl.when(frame == place)
        def _(gf_ref=gf_ref):
            out_ref[...] = gf_ref[...] + result


def norm_out(grad, video, grad_first, gain):
    frames, slots, width = video.shape
    per = lambda rows: pl.BlockSpec((None, rows, width), lambda f: (f, 0, 0))
    return pl.pallas_call(
        norm_out_body,
        grid=(frames,),
        in_specs=[by_part(grad.shape[0], grad.shape[2], width), per(slots), fixed((width,))]
        + [fixed((slots, width))] * frames,
        out_specs=per(slots),
        out_shape=jax.ShapeDtypeStruct(video.shape, F32),
        cost_estimate=pl.CostEstimate(flops=1 * 10**9, bytes_accessed=25 * MIB, transcendentals=0),
        compiler_params=params(),
        name="norm_out",
    )(grad, video, gain, *grad_first)


def tn_body(*refs):
    *refs, out_ref = refs
    count = len(refs) // 2
    total = None
    for a_ref, b_ref in zip(refs[:count], refs[count:]):
        rows, width = b_ref.shape[0], a_ref.shape[-1]
        part = dot_tn(a_ref[...].reshape(-1, width)[:rows], b_ref[...])
        total = part if total is None else total + part
    out_ref[...] = total.astype(out_ref.dtype)


def weight_grad(a, b):
    if isinstance(b, list):
        rows, width = b[0].shape
        places = [0] * len(b)
    else:
        rows, width = b.shape[0] // len(a), b.shape[1]
        places, b = range(len(a)), [b] * len(a)
    return pl.pallas_call(
        tn_body,
        grid=(width // WIDE,),
        in_specs=[fixed(value.shape) for value in a] + [pl.BlockSpec((rows, WIDE), lambda i, p=p: (p, i)) for p in places],
        out_specs=pl.BlockSpec((width, WIDE), lambda i: (0, i)),
        out_shape=jax.ShapeDtypeStruct((width, width), BF16),
        cost_estimate=pl.CostEstimate(
            flops=2 * len(b) * rows * width * width, bytes_accessed=4 * len(b) * rows * width, transcendentals=0
        ),
        compiler_params=params(),
        name="weight_grad",
    )(*a, *b)


def fc_grads_body(normed_ref, cot_ref, gi_ref, hid_ref, out_ref):
    units = gi_ref.shape[1]
    out_ref[:, :units] = dot_tn(normed_ref[...], gi_ref[...]).astype(BF16)
    out_ref[:, units:] = dot_tn(cot_ref[...], hid_ref[...]).astype(BF16)


def fc_grads(normed, cot, grad_inner, hidden):
    chunks, frames, slots, units = hidden.shape
    width = normed.shape[-1]
    rows = frames * slots
    hid = pl.BlockSpec((None, rows, units), lambda c: (c, 0, 0))
    flat = lambda value: value.reshape(chunks, rows, units)
    return pl.pallas_call(
        fc_grads_body,
        grid=(chunks,),
        in_specs=[fixed((rows, width)), fixed((rows, width)), hid, hid],
        out_specs=pl.BlockSpec((None, width, 2 * units), lambda c: (c, 0, 0)),
        out_shape=jax.ShapeDtypeStruct((chunks, width, 2 * units), BF16),
        cost_estimate=pl.CostEstimate(
            flops=4 * rows * width * units * chunks, bytes_accessed=4 * rows * units * chunks, transcendentals=0
        ),
        compiler_params=params(),
        name="fc_grads",
    )(normed.reshape(rows, width), cot.reshape(rows, width), flat(grad_inner), flat(hidden))


def finish_body(time_ref, space_ref, space_proj_ref, time_proj_ref, time_out, space_out, space_proj_out, time_proj_out):
    for group in range(time_ref.shape[0]):
        time_out[:, group * WIDE : (group + 1) * WIDE] = time_ref[group].astype(F32)
    space_out[...] = space_ref[...].astype(F32)

    @pl.when(pl.program_id(0) == 0)
    def _():
        space_proj_out[...] = space_proj_ref[...].astype(F32)
        time_proj_out[...] = time_proj_ref[...].astype(F32)


def finish(matrices):
    width = matrices.shape[1]
    groups = width // WIDE
    one = lambda at: pl.BlockSpec((None, width, width), lambda i: (at, 0, 0))
    block = pl.BlockSpec((width, width), lambda i: (0, i))
    full = jax.ShapeDtypeStruct((width, 3 * width), F32)
    square = jax.ShapeDtypeStruct((width, width), F32)
    return pl.pallas_call(
        finish_body,
        grid=(3,),
        in_specs=[
            pl.BlockSpec((groups, width, WIDE), lambda i: (0, 0, i)),
            pl.BlockSpec((None, width, width), lambda i: (groups + i, 0, 0)), one(groups + 3), one(groups + 4),
        ],
        out_specs=[block, block, fixed((width, width)), fixed((width, width))],
        out_shape=[full, full, square, square],
        cost_estimate=pl.CostEstimate(flops=1 * 10**9, bytes_accessed=30 * MIB, transcendentals=0),
        compiler_params=params(),
        name="finish",
    )(matrices, matrices, matrices, matrices)


MESH = pl.DeviceIdType.MESH
EARLY_GAP = 3.0
HOP = 4.0


def bits_of(count):
    return [1 << i for i in range(count.bit_length() - 1)]


def reducible(width, planes, parts):
    return parts == 4 and planes >= 4 and planes & (planes - 1) == 0 and width % (planes * 2 * 16) == 0


class Ring:
    def __init__(self, planes):
        self.bits = bits_of(planes)
        self.deep = len(self.bits)
        self.plane, self.part = lax.axis_index("dp"), lax.axis_index("mp")
        self.by_bit = {bit: {"dp": self.plane + bit - 2 * bit * self.place(bit)} for bit in self.bits}
        self.beside = {"mp": self.part + 1 - 2 * (self.part % 2)}
        self.across = {"mp": 3 - self.part}
        self.third = {"mp": (self.part + 2) % 4}
        self.inner = ((self.part + 1) // 2) % 2 == 1
        self.outer = ((self.part + 1) // 2) % 2 == 0
        self.started = []

    def place(self, bit):
        return (self.plane // bit) % 2

    def greet(self):
        partners = [self.by_bit[bit] for bit in self.bits] + [self.beside, self.across, self.third]
        barrier = pltpu.get_barrier_semaphore()
        for partner in partners:
            pl.semaphore_signal(barrier, inc=1, device_id=partner, device_id_type=MESH)
        pl.semaphore_wait(barrier, len(partners))

    def order(self, stream):
        return self.bits if stream == 0 else self.bits[:1] + self.bits[1:][::-1]

    def send(self, source, target, sems, at, partner, when=None):
        send_sem, recv_sem = sems
        copy = pltpu.make_async_remote_copy(
            src_ref=source, dst_ref=target, send_sem=send_sem.at[at], recv_sem=recv_sem.at[at],
            device_id=partner, device_id_type=MESH,
        )
        if when is None:
            copy.start()
        else:
            pl.when(when)(copy.start)
        self.started.append((when, copy))
        return copy

    def finish(self):
        for when, copy in self.started:
            if when is None:
                copy.wait_send()
            else:
                pl.when(when)(copy.wait_send)

    def rows(self, chain, level, width):
        stream = chain % 2
        mine = self.order(stream)
        size = width // 2
        spot, length = self.place(mine[0]) * size + stream * (size // 2), size // 2
        for bit in mine[1:level]:
            length //= 2
            spot = spot + self.place(bit) * length
        return spot, length


def rows_at(offset, size):
    return pl.ds(pl.multiple_of(offset, 16), size)


class Reduction:
    def __init__(self, ring, own, got, line, piece, out, spots, sems, back_sems, out_sem):
        self.ring, self.own, self.got, self.line, self.piece, self.sems = ring, own, got, line, piece, sems
        self.out, self.spots, self.back_sems, self.out_sem = out, spots, back_sems, out_sem
        self.width = own.shape[1]
        self.waiting = {}
        self.local = {}
        self.steps = 2 * ring.deep + 4

    def back(self, chain, step):
        ring, matrix = self.ring, chain // 2
        level = ring.deep - step
        if step == 0:
            spot, length = ring.rows(chain, level, self.width)
            source, region = self.piece.at[chain], self.out.at[self.spots[matrix], rows_at(spot, length)]
            self.local[chain] = pltpu.make_async_copy(source, region, self.out_sem.at[chain])
            self.local[chain].start()
        else:
            if step == 1:
                self.local[chain].wait()
            self.waiting[chain].wait_recv()
            if step == ring.deep:
                return
            spot, length = ring.rows(chain, level, self.width)
            source = region = self.out.at[self.spots[matrix], rows_at(spot, length)]
        partner = ring.by_bit[ring.order(chain % 2)[level - 1]]
        self.waiting[chain] = ring.send(source, region, self.back_sems, (chain, step), partner)

    def advance(self, chain, step):
        ring, deep = self.ring, self.ring.deep
        matrix, stream = chain // 2, chain % 2
        mine = ring.order(stream)
        size = self.width // 2
        got = self.got
        if step < deep or step == deep:
            if step == 0:
                spot = (1 - ring.place(mine[0])) * size + stream * (size // 2)
                source = self.own.at[matrix, rows_at(spot, size // 2)]
            else:
                self.waiting[chain].wait_recv()
                count = got[step - 1].shape[1]
                if step == 1:
                    kept = self.own[matrix, rows_at(ring.place(mine[0]) * size + stream * (size // 2), count), :]
                else:
                    kept = got[step - 2][chain, rows_at(ring.place(mine[step - 1]) * count, count), :]
                got[step - 1][chain] = (kept.astype(F32) + got[step - 1][chain].astype(F32)).astype(BF16)
                if step < deep:
                    half = count // 2
                    source = got[step - 1].at[chain, rows_at((1 - ring.place(mine[step])) * half, half)]
            if step < deep:
                self.waiting[chain] = ring.send(
                    source, got[step].at[chain], self.sems, (chain, step), ring.by_bit[mine[step]]
                )
                return
        if step <= deep + 3:
            self.line.advance(chain, step - deep, got[deep - 1].at[chain])
        if step >= deep + 3:
            self.back(chain, step - deep - 3)


class Line:
    def __init__(self, ring, lines, piece, sems, first=0):
        self.ring, self.lines, self.piece, self.sems, self.first = ring, lines, piece, sems, first
        self.waiting = {}

    def advance(self, chain, step, source):
        ring, lines, at = self.ring, self.lines, chain - self.first
        if step == 0:
            self.waiting[chain] = ring.send(source, lines[0].at[at], self.sems, (at, 0), ring.beside, ring.outer)
        elif step == 1:
            first = self.waiting[chain]

            @pl.when(ring.inner)
            def _():
                first.wait_recv()
                lines[0][at] = (source[...].astype(F32) + lines[0][at].astype(F32)).astype(BF16)

            self.waiting[chain] = ring.send(lines[0].at[at], lines[1].at[at], self.sems, (at, 1), ring.across, ring.inner)
        elif step == 2:
            second = self.waiting[chain]

            @pl.when(ring.inner)
            def _():
                second.wait_recv()
                both = (lines[0][at].astype(F32) + lines[1][at].astype(F32)).astype(BF16)
                self.piece[chain - self.first] = both
                lines[2][at] = both

            self.waiting[chain] = ring.send(lines[2].at[at], lines[3].at[at], self.sems, (at, 2), ring.beside, ring.inner)
        else:
            third = self.waiting[chain]

            @pl.when(ring.outer)
            def _():
                third.wait_recv()
                self.piece[chain - self.first] = lines[3][at]


def reduction_scratch(chains, width, deep):
    length = width // 4
    sizes = [length >> i for i in range(deep)]
    shapes = [pltpu.VMEM((chains, size, width), BF16) for size in sizes + [sizes[-1]] * 4]
    return shapes + [pltpu.SemaphoreType.DMA((chains, deep))] * 2 + [pltpu.SemaphoreType.DMA((chains, 3))] * 2 + [
        pltpu.SemaphoreType.DMA((chains, deep))
    ] * 2 + [pltpu.SemaphoreType.DMA((chains,)), pltpu.VMEM((chains, sizes[-1], width), BF16)]


def temporal_tail_body(
    gain_ref, shift_ref, small_in, *refs, planes, early, taken, local,
):
    g_refs, (x_hbm, q_hbm, k_hbm, v_hbm, w_hbm), refs = refs[:local], refs[local : local + 5], refs[local + 5 :]
    early_hbm, refs = refs[:early], refs[early:]
    moved_ref, out_ref, small_out, refs = refs[0], refs[1], refs[2], refs[3:]
    x_ref, qkv_ref, w_ref, d_ref, dx_ref, own, load_sem, refs = *refs[:7], refs[7:]
    move_send, move_recv, move_local, small_ref, small_got, small_held, small_send, small_recv, refs = *refs[:8], refs[8:]
    ring = Ring(planes)
    deep = ring.deep
    got, lines, refs = refs[:deep], refs[deep : deep + 4], refs[deep + 4 :]
    sems, line_sems, back_sems, out_sem, piece_ref = refs[:2], refs[2:4], refs[4:6], refs[6], refs[7]
    frames, slots, width = x_ref.shape
    groups = width // WIDE
    rows = frames * STEP
    loads = {}

    def load(name, source, target, at):
        copy = pltpu.make_async_copy(source, target, load_sem.at[at])
        copy.start()
        loads[name] = copy

    def load_group(group):
        for place, ref in enumerate((q_hbm, k_hbm, v_hbm)):
            source = ref.at[:, :, pl.ds(group * WIDE, WIDE)]
            load(("qkv", group, place), source, qkv_ref.at[group % 2, place], early + 2 + 3 * group + place)

    load_group(0)
    for matrix in range(early):
        load(("own", matrix), early_hbm[matrix], own.at[matrix], matrix)
    load("x", x_hbm, x_ref, early)
    load("w", w_hbm, w_ref, early + 1)
    ring.greet()
    matrices = early + groups
    line = Line(ring, lines, piece_ref, line_sems)
    spots = [groups + matrix for matrix in range(early)] + list(range(groups))
    sums = Reduction(ring, own, got, line, piece_ref, out_ref, spots, sems, back_sems, out_sem)
    small_ref[...] = small_in[...]

    row = lax.broadcasted_iota(jnp.int32, (rows, rows), 0)
    col = lax.broadcasted_iota(jnp.int32, (rows, rows), 1)
    same = row % STEP == col % STEP
    shape = (frames, STEP, WIDE)
    starts = {}
    ready = {}

    def compute():
        for group in range(groups):
            if group + 1 < groups:
                load_group(group + 1)
            for place in range(3):
                loads[("qkv", group, place)].wait()
            slot = group % 2
            lanes = slice(group * WIDE, (group + 1) * WIDE)
            for step in range(slots // STEP):
                part = slice(step * STEP, (step + 1) * STEP)
                k = qkv_ref[slot, 1, :, part, :].reshape(rows, WIDE)
                v = qkv_ref[slot, 2, :, part, :].reshape(rows, WIDE)
                queries = stacked(qkv_ref[slot, 0, :, part, :].reshape(rows, WIDE), rows)
                grads = jnp.stack([g_ref[:, part, lanes] for g_ref in g_refs], axis=1)
                grads = stacked(grads.reshape(rows, WIDE), rows)
                scores = dot_nt(k, queries)
                grad_mixing = dot_nt(v, grads)
                mixing, grad_scores = [], []
                for head in range(GROUP):
                    span = slice(head * rows, (head + 1) * rows)
                    s = jnp.where(same, scores[:, span], -1e30)
                    e = jnp.exp(s - jnp.max(s, axis=0, keepdims=True))
                    p = e / jnp.sum(e, axis=0, keepdims=True)
                    gp = grad_mixing[:, span]
                    ds = p * (gp - jnp.sum(p * gp, axis=0, keepdims=True))
                    mixing.append(p.astype(BF16))
                    grad_scores.append(ds.astype(BF16))
                grad_scores = jnp.concatenate(grad_scores, axis=1)
                dv = dot(jnp.concatenate(mixing, axis=1), grads)
                dk = dot(grad_scores, queries)
                spread = dot_tn(grad_scores, k)
                dq = jnp.zeros((rows, WIDE), F32)
                for head in range(GROUP):
                    dq = dq + spread[head * rows : (head + 1) * rows] * head_lanes(rows, head, F32)
                d_ref[group, :, part, :WIDE] = (dq * HEAD_DIM**-0.5).astype(BF16).reshape(shape)
                d_ref[group, :, part, WIDE : 2 * WIDE] = dk.astype(BF16).reshape(shape)
                d_ref[group, :, part, 2 * WIDE :] = dv.astype(BF16).reshape(shape)
                if step % 4 == 3:
                    yield 2.0
            if group == 0:
                loads["x"].wait()
            d = d_ref[group].reshape(frames * slots, 3 * WIDE)
            x = x_ref[...].reshape(frames * slots, width)
            own[early + group] = dot_tn(x, d).astype(BF16)
            ready[early + group] = True
            yield 4.5
            small_ref[taken : taken + 1, lanes] = column_sum(d[:, :WIDE])
            small_ref[taken + 1 : taken + 2, lanes] = column_sum(d[:, 2 * WIDE :])
        loads["w"].wait()
        quarter = frames // 4
        shift_grad, product = jnp.zeros((1, width), F32), jnp.zeros((1, width), F32)
        for distance in (2, 3, 1, 0):
            part = (ring.part + distance) % 4
            some = pl.ds(part * quarter, quarter)
            total = jnp.zeros((quarter * slots, width), F32)
            for group in range(groups):
                d = d_ref[group, some].reshape(quarter * slots, 3 * WIDE)
                for place in range(3):
                    weight = w_ref[:, pl.ds(place * width + group * WIDE, WIDE)]
                    total = total + dot_nt(d[:, place * WIDE : (place + 1) * WIDE], weight)
            dx_ref[some] = total.astype(BF16).reshape(quarter, slots, width)
            if distance:
                moves.append(move(distance))
                moves[-1].start()
            else:
                keep = pltpu.make_async_copy(dx_ref.at[some], moved_ref.at[ring.part], move_local.at[0])
                keep.start()
                kept.append(keep)
            x = x_ref[some].reshape(quarter * slots, width)
            shift_grad += column_sum(total)
            product += column_sum(total * x.astype(F32))
            yield 3.5
        small_ref[taken + 2 : taken + 3, :] = (product - shift_ref[...][None] * shift_grad) / gain_ref[...][None]
        small_ref[taken + 3 : taken + 4, :] = shift_grad

    moves, kept = [], []

    def move(distance, arriving=False):
        target = (ring.part + distance) % 4
        source = (ring.part + 4 - distance) % 4 if arriving else ring.part
        return pltpu.make_async_remote_copy(
            src_ref=dx_ref.at[pl.ds(target * (frames // 4), frames // 4)], dst_ref=moved_ref.at[source],
            send_sem=move_send.at[distance], recv_sem=move_recv.at[source], device_id={"mp": target}, device_id_type=MESH,
        )

    partners = [ring.by_bit[bit] for bit in ring.bits] + [ring.beside, ring.third]
    small_wait = []

    def small_step(step):
        if step > 0:
            small_wait.pop().wait_recv()
            before = small_ref[...] if step == 1 else small_held[step - 2]
            value = before + small_got[step - 1]
            if step == len(partners):
                small_out[...] = value
                return
            small_held[step - 1] = value
        source = small_ref if step == 0 else small_held.at[step - 1]
        small_wait.append(ring.send(source, small_got.at[step], (small_send, small_recv), step, partners[step]))

    following = [0] * matrices
    due = [EARLY_GAP * matrix for matrix in range(matrices)]
    clock = 0.0

    def advance_all():
        for matrix in range(matrices):
            step = following[matrix]
            if step < sums.steps and clock >= due[matrix] and (matrix < early or matrix in ready):
                if step == 0 and matrix < early:
                    loads[("own", matrix)].wait()
                for chain in (2 * matrix, 2 * matrix + 1):
                    sums.advance(chain, step)
                following[matrix] += 1
                due[matrix] = clock + HOP

    advance_all()
    for spent in compute():
        clock += spent
        advance_all()
    small_at = 0
    while any(step < sums.steps for step in following) or small_at <= len(partners):
        clock += HOP
        advance_all()
        if small_at <= len(partners):
            small_step(small_at)
            small_at += 1
    for distance in (1, 2, 3):
        move(distance, True).wait_recv()
    for copy in moves:
        copy.wait_send()
    kept[0].wait()
    ring.finish()


def temporal_tail(x, q, k, v, grad, weight, gain, shift, early, small, taken, planes, number):
    frames, slots, width = x.shape
    groups = width // WIDE
    deep = len(bits_of(planes))
    chains = 2 * (len(early) + groups)
    anywhere = pl.BlockSpec(memory_space=pl.ANY)
    whole = pl.BlockSpec(memory_space=pltpu.VMEM)
    flops = 2 * frames * slots * width * width * 12
    return pl.pallas_call(
        functools.partial(temporal_tail_body, planes=planes, early=len(early), taken=taken, local=len(grad)),
        in_specs=[whole] * (3 + len(grad)) + [anywhere] * (5 + len(early)),
        out_specs=[anywhere, anywhere, whole],
        out_shape=[
            jax.ShapeDtypeStruct((4, frames // 4, slots, width), BF16),
            jax.ShapeDtypeStruct((len(early) + groups, width, width), BF16),
            jax.ShapeDtypeStruct(small.shape, F32),
        ],
        scratch_shapes=[
            pltpu.VMEM(x.shape, BF16), pltpu.VMEM((2, 3, frames, slots, WIDE), BF16), pltpu.VMEM(weight.shape, BF16),
            pltpu.VMEM((groups, frames, slots, 3 * WIDE), BF16), pltpu.VMEM(x.shape, BF16),
            pltpu.VMEM((len(early) + groups, width, width), BF16),
            pltpu.SemaphoreType.DMA((len(early) + 2 + 3 * groups,)),
            pltpu.SemaphoreType.DMA((4,)), pltpu.SemaphoreType.DMA((4,)), pltpu.SemaphoreType.DMA((1,)),
            pltpu.VMEM(small.shape, F32), pltpu.VMEM((deep + 2,) + small.shape, F32), pltpu.VMEM((deep + 1,) + small.shape, F32),
            pltpu.SemaphoreType.DMA((deep + 2,)), pltpu.SemaphoreType.DMA((deep + 2,)),
        ] + reduction_scratch(chains, width, deep),
        cost_estimate=pl.CostEstimate(flops=flops, bytes_accessed=60 * MIB, transcendentals=0),
        compiler_params=pltpu.CompilerParams(vmem_limit_bytes=62 * MIB, collective_id=number, has_side_effects=True),
        name="temporal_tail",
    )(gain, shift, small, *grad, x, q, k, v, weight, *early)


def temporal_head_body(video_ref, gain_ref, shift_ref, w_ref, bias_ref, *refs, chunks, local):
    x_out, q_out, k_out, v_out, refs = *refs[:4], refs[4:]
    o_outs, refs = refs[:local], refs[local:]
    normed, xs, qs, ks, vs, os, send_sem, recv_sem, out_sem = refs
    ring = Ring(lax.axis_size("dp"))
    me = ring.part
    frames, share, width = xs.shape
    slots = video_ref.shape[1]
    groups = width // WIDE
    barrier = pltpu.get_barrier_semaphore()
    for partner in (ring.beside, ring.across, ring.third):
        pl.semaphore_signal(barrier, inc=1, device_id=partner, device_id_type=MESH)
    pl.semaphore_wait(barrier, 3)
    sent, written = [], []

    def prepare(chunk):
        start, count = chunks[chunk]
        for part in range(4):
            for frame in range(local):
                first = part * share + start
                some = max(min(count, slots - first), 0)
                if some > 0:
                    unit, _ = norm_parts(video_ref[frame, first : first + some, :].astype(F32))
                    normed[part, frame, start : start + some, :] = (unit * gain_ref[...] + shift_ref[...]).astype(BF16)
                if some < count:
                    normed[part, frame, start + some : start + count, :] = jnp.zeros((count - some, width), BF16)
        for frame in range(local):
            xs[me * local + frame, start : start + count, :] = normed[me, frame, start : start + count, :]

    def move(chunk, distance, arriving=False):
        start, count = chunks[chunk]
        target = (me + distance) % 4
        source = (me + 4 - distance) % 4 if arriving else me
        return pltpu.make_async_remote_copy(
            src_ref=normed.at[target, :, pl.ds(start, count)],
            dst_ref=xs.at[pl.ds(source * local, local), pl.ds(start, count)],
            send_sem=send_sem.at[chunk, distance], recv_sem=recv_sem.at[chunk, source],
            device_id={"mp": target}, device_id_type=MESH,
        )

    def send(chunk):
        for distance in (2, 3, 1):
            copy = move(chunk, distance)
            copy.start()
            sent.append(copy)

    def write(source, target):
        copy = pltpu.make_async_copy(source, target, out_sem.at[len(written)])
        copy.start()
        written.append(copy)

    rows = frames * STEP
    row = lax.broadcasted_iota(jnp.int32, (rows, rows), 0)
    col = lax.broadcasted_iota(jnp.int32, (rows, rows), 1)
    same = row % STEP == col % STEP

    def compute(chunk):
        start, count = chunks[chunk]
        span = pl.ds(start, count)
        x = xs[:, start : start + count, :].reshape(frames * count, width)
        shape = (frames, count, WIDE)
        for group in range(groups):
            lanes = slice(group * WIDE, (group + 1) * WIDE)
            part = lambda place: slice(place * width + group * WIDE, place * width + (group + 1) * WIDE)
            q = (dot(x, w_ref[:, part(0)]) + bias_ref[:, part(0)]) * HEAD_DIM**-0.5
            v = dot(x, w_ref[:, part(2)]) + bias_ref[:, part(1)]
            qs[:, start : start + count, lanes] = q.astype(BF16).reshape(shape)
            ks[:, start : start + count, lanes] = dot(x, w_ref[:, part(1)]).astype(BF16).reshape(shape)
            vs[:, start : start + count, lanes] = v.astype(BF16).reshape(shape)
            for step in range(start // STEP, (start + count) // STEP):
                block = slice(step * STEP, (step + 1) * STEP)
                keys = stacked(ks[:, block, lanes].reshape(rows, WIDE), rows)
                values = stacked(vs[:, block, lanes].reshape(rows, WIDE), rows)
                scores = dot_nt(qs[:, block, lanes].reshape(rows, WIDE), keys)
                mixing = []
                for head in range(GROUP):
                    s = jnp.where(same, scores[:, head * rows : (head + 1) * rows], -1e30)
                    e = jnp.exp(s - jnp.max(s, axis=1, keepdims=True))
                    mixing.append((e / jnp.sum(e, axis=1, keepdims=True)).astype(BF16))
                o = dot(jnp.concatenate(mixing, axis=1), values).astype(BF16).reshape(4, local, STEP, WIDE)
                for frame in range(local):
                    os[frame, :, block, lanes] = o[:, frame]
        for frame in range(local):
            write(os.at[frame, :, span], o_outs[frame].at[:, span])
        for held, out in ((xs, x_out), (qs, q_out), (ks, k_out), (vs, v_out)):
            write(held.at[:, span], out.at[:, span])

    for chunk in range(len(chunks)):
        prepare(chunk)
        if chunk < 2:
            send(chunk)
    for chunk in range(len(chunks)):
        for distance in (1, 2, 3):
            move(chunk, distance, True).wait_recv()
        if chunk + 2 < len(chunks):
            send(chunk + 2)
        compute(chunk)
    for copy in sent:
        copy.wait_send()
    for copy in written:
        copy.wait()


def temporal_head(video, gain, shift, weight, bias, share, number):
    local, slots, width = video.shape
    frames = 4 * local
    blocks = share // STEP
    count = 4
    chunks, at = [], 0
    for i in range(count):
        size = (blocks // count + (1 if i < blocks % count else 0)) * STEP
        chunks.append((at, size))
        at += size
    whole = pl.BlockSpec(memory_space=pltpu.VMEM)
    anywhere = pl.BlockSpec(memory_space=pl.ANY)
    by_position = (frames, share, width)
    return pl.pallas_call(
        functools.partial(temporal_head_body, chunks=chunks, local=local),
        in_specs=[whole] * 5,
        out_specs=[anywhere] * (4 + local),
        out_shape=[jax.ShapeDtypeStruct(by_position, BF16)] * 4 + [jax.ShapeDtypeStruct((4, share, width), BF16)] * local,
        scratch_shapes=[pltpu.VMEM((4, local, share, width), BF16)] + [pltpu.VMEM(by_position, BF16)] * 4
        + [pltpu.VMEM((local, 4, share, width), BF16)]
        + [pltpu.SemaphoreType.DMA((count, 4))] * 2 + [pltpu.SemaphoreType.DMA((count * (4 + local),))],
        cost_estimate=pl.CostEstimate(flops=70 * 10**9, bytes_accessed=20 * MIB, transcendentals=0),
        compiler_params=pltpu.CompilerParams(vmem_limit_bytes=56 * MIB, collective_id=number, has_side_effects=True),
        name="temporal_head",
    )(video, gain, shift, weight, bias)


def middle_and_space(frame, mixed, video, proj, proj_bias, gain, shift, weight, bias, patch_width):
    first, normed, qkv = middle(frame, mixed, video, proj, proj_bias, gain, shift, weight, bias)
    space_mixed, lse = spatial_fwd(patch_width, qkv, 1, video.shape[1])
    return first, normed, qkv, space_mixed, lse


def shards(
    video,
    patch_width,
    temporal_gain,
    temporal_shift,
    temporal_qkv,
    temporal_qv_bias,
    temporal_proj,
    temporal_proj_bias,
    spatial_gain,
    spatial_shift,
    spatial_qkv,
    spatial_qv_bias,
    spatial_proj,
    spatial_proj_bias,
    mlp_gain,
    mlp_shift,
    fc1_weight,
    fc1_bias,
    fc2_weight,
    fc2_bias,
    cotangent,
):
    frames, sets, slots, width = video.shape
    units = fc1_weight.shape[1]
    parts, planes = lax.axis_size("mp"), lax.axis_size("dp")
    share = -(-slots // (parts * STEP)) * STEP
    row = lambda value: value.astype(F32).reshape(1, -1)
    video = video.reshape(frames * sets, slots, width)
    cot = cotangent.reshape(frames * sets, slots, width)

    joint = jnp.concatenate([fc1_weight, fc2_weight.T], axis=1)
    piece = width // planes
    own = lax.dynamic_slice_in_dim(joint, lax.axis_index("dp") * piece, piece, 0)
    bias_rows = jnp.pad(fc1_bias.reshape(1, units), ((0, 15), (0, units)))
    own = jnp.concatenate([own, bias_rows], axis=0)[None]

    def exchange(value):
        return lax.all_to_all(value, "mp", split_axis=0, concat_axis=0, tiled=True)

    by_position = lambda value: value.reshape(parts * frames, share, width)
    by_device = lambda value: value.reshape(parts, frames, share, width)
    column = lax.all_gather(own, "mp", axis=0, tiled=True)
    if reducible(width, planes, parts):
        x, tq, tk, tv, *time_mixed = temporal_head(
            video, temporal_gain, temporal_shift, temporal_qkv, row(temporal_qv_bias), share, 2
        )
    else:
        x = by_position(exchange(norm_in(video, temporal_gain, temporal_shift, parts, share)))
        tq, tk, tv, *time_mixed = temporal_fwd(x, temporal_qkv, row(temporal_qv_bias), frames)
    column, *time_mixed = lax.optimization_barrier((column, *time_mixed))
    fb1 = column[:, piece : piece + 1, :units].astype(F32)
    joint = lax.all_gather(column[:, :piece], "dp", axis=1, tiled=True)
    time_back = [exchange(value) for value in time_mixed]

    several = lambda results: [list(values) for values in zip(*results)]
    spatial = []
    for f in range(frames):
        if f > 0:
            time_back[f], lse_before = lax.optimization_barrier((time_back[f], spatial[-1][-1]))
            spatial[-1] = spatial[-1][:-1] + (lse_before,)
        spatial.append(
            middle_and_space(
                f, time_back[f], video, temporal_proj, temporal_proj_bias, spatial_gain, spatial_shift, spatial_qkv,
                row(spatial_qv_bias), patch_width,
            )
        )
    first, normed_mid, space_qkv, space_mixed, lse = several(spatial)

    output, normed_out, hidden, grad_inner, grad_second, grad_space_out, grad_space, feed_sums, unit_sums = feed(
        first, [value[0] for value in space_mixed], cot, spatial_proj, spatial_proj_bias, mlp_gain, mlp_shift, joint, fb1, fc2_bias
    )
    fc_part = fc_grads(normed_out, cot, grad_inner, hidden)
    fc_part = lax.psum_scatter(fc_part, "dp", scatter_dimension=1, tiled=True)

    dq, dk, dv, grad_first, grad_time_out, mid_sums, grad_slot = [], [], [], [], [], [], []
    for f in range(frames):
        q_f, k_f, v_f = spatial_bwd(f, patch_width, space_qkv[f], space_mixed[f], lse[f], grad_space, 1, slots)
        if f > 0:
            grad_slot[-1], q_f = lax.optimization_barrier((grad_slot[-1], q_f))
        first_f, out_f, time_f, sums_f = middle_bwd(
            f, q_f[0], k_f[0], v_f[0], spatial_qkv, first[f], grad_second, spatial_gain, temporal_proj, parts, share
        )
        if f + 1 < frames:
            time_f, grad_space = lax.optimization_barrier((time_f, grad_space))
        grad_slot.append(exchange(time_f))
        for kept, value in zip(
            (dq, dk, dv, grad_first, grad_time_out, mid_sums), (q_f[0], k_f[0], v_f[0], first_f, out_f, sums_f)
        ):
            kept.append(value)
    early = [
        weight_grad(normed_mid, dq),
        weight_grad(normed_mid, dk),
        weight_grad(normed_mid, dv),
        weight_grad([value[0] for value in space_mixed], grad_space_out.reshape(-1, width)),
        weight_grad(time_back, grad_time_out),
    ]
    fc_part, grad_first[-1] = lax.optimization_barrier((fc_part, grad_first[-1]))
    fc_part = lax.psum_scatter(fc_part, "mp", scatter_dimension=0, tiled=True)[0].astype(F32)
    fc1_weight_grad = fc_part[:, :units]
    fc2_weight_grad = fc_part[:, units:].T

    own_sums = [unit_sums[:, 0, :].reshape(-1, width), feed_sums[:4], sum(mid_sums)[:5]]
    weights = (temporal_qkv, temporal_gain, temporal_shift)
    wide = lambda blocks: jnp.concatenate([block.astype(F32) for block in blocks], axis=1)
    if reducible(width, planes, parts):
        taken = sum(rows.shape[0] for rows in own_sums)
        small = jnp.concatenate(own_sums + [jnp.zeros((4 + -(taken + 4) % 8, width), F32)], axis=0)
        grad_in, matrices, small = temporal_tail(x, tq, tk, tv, grad_slot, *weights, early, small, taken, planes, 1)
        temporal_qkv_grad, spatial_qkv_grad, spatial_proj_grad, temporal_proj_grad = finish(matrices)
    else:
        gq, gk, gv, grad_x, bias_sums, norm_sums = temporal_bwd(x, tq, tk, tv, by_position(jnp.stack(grad_slot, axis=1)), *weights)
        grad_in = exchange(by_device(grad_x))
        small = jnp.concatenate(own_sums + [bias_sums[:2], norm_sums[:2]], axis=0)
        flat = lambda value: value.reshape(-1, width)
        late = [weight_grad([flat(x)], [flat(value)]) for value in (gq, gk, gv)]
        matrices, small = lax.psum((jnp.stack(early + late), small), ("dp", "mp"))
        temporal_qkv_grad = wide([matrices[5 + p] for p in range(3)])
        spatial_qkv_grad = wide([matrices[p] for p in range(3)])
        spatial_proj_grad, temporal_proj_grad = matrices[3].astype(F32), matrices[4].astype(F32)
    video_grad = norm_out(grad_in, video, grad_first, temporal_gain)
    count = parts * units // width
    fc1_bias_grad = small[:count].reshape(-1)
    (
        mlp_gain_grad, mlp_shift_grad, spatial_proj_bias_grad, fc2_bias_grad,
        spatial_gain_grad, spatial_shift_grad, space_q_sum, space_v_sum, temporal_proj_bias_grad,
        time_q_sum, time_v_sum, temporal_gain_grad, temporal_shift_grad,
    ) = [small[count + i] for i in range(13)]
    return (
        output.reshape(frames, sets, slots, width),
        video_grad.reshape(frames, sets, slots, width),
        temporal_gain_grad,
        temporal_shift_grad,
        temporal_qkv_grad,
        jnp.concatenate([time_q_sum, time_v_sum]),
        temporal_proj_grad,
        temporal_proj_bias_grad,
        spatial_gain_grad,
        spatial_shift_grad,
        spatial_qkv_grad,
        jnp.concatenate([space_q_sum, space_v_sum]),
        spatial_proj_grad,
        spatial_proj_bias_grad,
        mlp_gain_grad,
        mlp_shift_grad,
        fc1_weight_grad,
        fc1_bias_grad,
        fc2_weight_grad,
        fc2_bias_grad,
    )


def solution(mesh):
    tokens = P("mp", "dp", None, None)
    return jax.shard_map(
        shards,
        mesh=mesh,
        in_specs=(tokens, P("dp")) + (P(),) * 14 + (P(None, "mp"), P("mp"), P("mp", None), P(), tokens),
        out_specs=(tokens, tokens) + (P(),) * 14 + (P("dp", "mp"), P(), P("mp", "dp"), P()),
        check_vma=False,
    )
```

```python
import functools
import jax
import jax.numpy as jnp
from jax import lax
from jax.experimental import pallas as pl
from jax.experimental.pallas import tpu as pltpu
from jax.sharding import PartitionSpec as P

HEADS = 12
HEAD_DIM = 64
GROUP = 4
WIDE = GROUP * HEAD_DIM
EPSILON = 1e-06
F32 = jnp.float32
BF16 = jnp.bfloat16
MIB = 1 << 20


def params(mib=56):
    return pltpu.CompilerParams(vmem_limit_bytes=mib * MIB)


def dot(a, b):
    return jnp.dot(a, b, preferred_element_type=F32)


def dot_nt(a, b):
    return lax.dot_general(a, b, (((1,), (1,)), ((), ())), preferred_element_type=F32)


def dot_tn(a, b):
    return lax.dot_general(a, b, (((0,), (0,)), ((), ())), preferred_element_type=F32)


def head_lanes(rows, head, dtype):
    lane = lax.broadcasted_iota(jnp.int32, (rows, WIDE), 1)
    return (lane // HEAD_DIM == head).astype(dtype)


def windows(slots, clips, rows):
    size = slots // clips
    found = []
    for start in range(0, slots, rows):
        stop = min(start + rows, slots)
        low = start // size * size // 16 * 16
        high = min(-(-(-(-stop // size) * size) // 16) * 16, slots)
        found.append((start, stop, low, high))
    return found


def spatial_fwd_body(width_ref, q_ref, k_ref, v_ref, o_ref, l_ref, *, slots, rows, narrow):
    def attend(chunks, size):
        stats = []
        for start, stop, low, high in chunks:
            count = stop - start
            q = q_ref[start:stop, :]
            k = k_ref[low:high, :]
            v = v_ref[low:high, :]
            if size < slots:
                query_clip = (lax.broadcasted_iota(jnp.int32, (count, high - low), 0) + start) // size
                key_clip = (lax.broadcasted_iota(jnp.int32, (count, high - low), 1) + low) // size
                same = query_clip == key_clip
            total = jnp.zeros((count, WIDE), F32)
            lse = jnp.zeros((count, 128), F32)
            lane = lax.broadcasted_iota(jnp.int32, (count, 128), 1)
            for head in range(GROUP):
                s = dot_nt(q * head_lanes(count, head, BF16), k)
                if size < slots:
                    s = jnp.where(same, s, -1e30)
                top = jnp.max(s, axis=1, keepdims=True)
                e = jnp.exp(s - top)
                norm = jnp.sum(e, axis=1, keepdims=True)
                o = dot(e.astype(BF16), v)
                total = total + o * (head_lanes(count, head, F32) / norm)
                lse = jnp.where(lane == head, top + jnp.log(norm), lse)
            o_ref[start:stop, :] = total.astype(BF16)
            stats.append(lse)
        l_ref[...] = jnp.concatenate(stats, axis=0).T[:8, :]

    wide = width_ref[0] == slots

    @pl.when(wide)
    def _():
        attend(windows(slots, 1, rows or slots), slots)

    @pl.when(jnp.logical_not(wide))
    def _():
        attend(windows(slots, 4, narrow), slots // 4)


def spatial_fwd(width, qkv, frames, slots, rows=None, narrow=256):
    groups = HEADS // GROUP
    qkv = qkv.reshape(frames, slots, -1)
    spec = lambda part: pl.BlockSpec((None, slots, WIDE), lambda f, g, w: (f, 0, part * groups + g))
    out = pl.pallas_call(
        functools.partial(spatial_fwd_body, slots=slots, rows=rows, narrow=narrow),
        grid_spec=pltpu.PrefetchScalarGridSpec(
            num_scalar_prefetch=1,
            grid=(frames, groups),
            in_specs=[spec(0), spec(1), spec(2)],
            out_specs=[
                pl.BlockSpec((None, slots, WIDE), lambda f, g, w: (f, 0, g)),
                pl.BlockSpec((None, None, 8, slots), lambda f, g, w: (f, g, 0, 0)),
            ],
        ),
        out_shape=[
            jax.ShapeDtypeStruct((frames, slots, HEADS * HEAD_DIM), BF16),
            jax.ShapeDtypeStruct((frames, groups, 8, slots), F32),
        ],
        cost_estimate=pl.CostEstimate(flops=20 * 10**9, bytes_accessed=5 * MIB, transcendentals=0),
        compiler_params=params(),
        name="spatial_fwd",
    )(width, qkv, qkv, qkv)
    return out


def spatial_bwd_body(width_ref, q_ref, k_ref, v_ref, o_ref, l_ref, g_ref, dq_ref, dk_ref, dv_ref, dqt, *, slots, rows, narrow):
    prod = g_ref[...].astype(F32) * o_ref[...].astype(F32)
    high_part = prod.astype(BF16)
    low_part = (prod - high_part.astype(F32)).astype(BF16)
    lane = lax.broadcasted_iota(jnp.int32, (8, WIDE), 1)
    row = lax.broadcasted_iota(jnp.int32, (8, WIDE), 0)
    picks = (lane // HEAD_DIM == row).astype(BF16)
    delta = dot_nt(picks, high_part) + dot_nt(picks, low_part)

    def attend(chunks, size):
        dqt[...] = jnp.zeros_like(dqt)
        kt = k_ref[...].T
        for start, stop, low, high in chunks:
            count = stop - start
            k = k_ref[start:stop, :]
            v = v_ref[start:stop, :]
            q = q_ref[low:high, :]
            g = g_ref[low:high, :]
            if size < slots:
                key_clip = (lax.broadcasted_iota(jnp.int32, (count, high - low), 0) + start) // size
                query_clip = (lax.broadcasted_iota(jnp.int32, (count, high - low), 1) + low) // size
                same = query_clip == key_clip
            dk = jnp.zeros((count, WIDE), F32)
            dv = jnp.zeros((count, WIDE), F32)
            for head in range(GROUP):
                mask = head_lanes(count, head, BF16)
                s = dot_nt(k * mask, q)
                p = jnp.exp(s - l_ref[head : head + 1, low:high])
                if size < slots:
                    p = jnp.where(same, p, 0.0)
                dp = dot_nt(v * mask, g)
                ds = (p * (dp - delta[head : head + 1, low:high])).astype(BF16)
                keep = head_lanes(count, head, F32)
                dv = dv + dot(p.astype(BF16), g) * keep
                dk = dk + dot(ds, q) * keep
                span = slice(head * HEAD_DIM, (head + 1) * HEAD_DIM)
                dqt[span, low:high] += dot(kt[span, start:stop], ds)
            dk_ref[start:stop, :] = dk.astype(BF16)
            dv_ref[start:stop, :] = dv.astype(BF16)
        dq_ref[...] = (dqt[...] * HEAD_DIM**-0.5).T.astype(BF16)

    wide = width_ref[0] == slots

    @pl.when(wide)
    def _():
        attend(windows(slots, 1, rows or slots), slots)

    @pl.when(jnp.logical_not(wide))
    def _():
        attend(windows(slots, 4, narrow), slots // 4)


def spatial_bwd(frame, width, qkv, mixed, lse, grad, frames, slots, rows=None, narrow=208):
    groups = HEADS // GROUP
    width_all = HEADS * HEAD_DIM
    qkv = qkv.reshape(frames, slots, -1)
    spec = lambda part: pl.BlockSpec((None, slots, WIDE), lambda f, g, w: (f, 0, part * groups + g))
    one = pl.BlockSpec((None, slots, WIDE), lambda f, g, w: (f, 0, g))
    out = pl.pallas_call(
        functools.partial(spatial_bwd_body, slots=slots, rows=rows, narrow=narrow),
        grid_spec=pltpu.PrefetchScalarGridSpec(
            num_scalar_prefetch=1,
            grid=(frames, groups),
            in_specs=[
                spec(0), spec(1), spec(2), one,
                pl.BlockSpec((None, None, 8, slots), lambda f, g, w: (f, g, 0, 0)),
                pl.BlockSpec((None, slots, WIDE), lambda f, g, w: (frame + f, 0, g)),
            ],
            out_specs=[one, one, one],
            scratch_shapes=[pltpu.VMEM((WIDE, slots), F32)],
        ),
        out_shape=[jax.ShapeDtypeStruct((frames, slots, width_all), BF16)] * 3,
        cost_estimate=pl.CostEstimate(flops=32 * 10**9, bytes_accessed=9 * MIB, transcendentals=0),
        compiler_params=params(),
        name="spatial_bwd",
    )(width, qkv, qkv, qkv, mixed, lse, grad)
    return out


def fixed(shape):
    return pl.BlockSpec(shape, lambda *_: (0,) * len(shape))


def norm_parts(value):
    centered = value - jnp.mean(value, axis=-1, keepdims=True)
    scale = lax.rsqrt(jnp.mean(centered * centered, axis=-1, keepdims=True) + EPSILON)
    return centered * scale, scale


def norm_grad(grad, unit, scale, gain):
    inner = grad * gain
    return scale * (
        inner
        - jnp.mean(inner, axis=-1, keepdims=True)
        - unit * jnp.mean(inner * unit, axis=-1, keepdims=True)
    )


def column_sum(value):
    return jnp.sum(value.astype(F32), axis=0, keepdims=True)


def by_part(parts, share, width):
    return pl.BlockSpec((parts, None, share, width), lambda f: (0, f, 0, 0))


def norm_in_body(video_ref, gain_ref, shift_ref, out_ref):
    unit, _ = norm_parts(video_ref[...].astype(F32))
    split_positions(out_ref, (unit * gain_ref[...] + shift_ref[...]).astype(BF16))


def split_positions(out_ref, value):
    parts, share, width = out_ref.shape
    slots = value.shape[0]
    for part in range(parts):
        start = part * share
        count = min(max(slots - start, 0), share)
        if count > 0:
            out_ref[part, :count, :] = value[start : start + count, :]
        if count < share:
            out_ref[part, count:, :] = jnp.zeros((share - count, width), value.dtype)


def joined_positions(ref, slots):
    parts, share, width = ref.shape
    return ref[...].reshape(parts * share, width)[:slots, :]


def norm_in(video, gain, shift, parts, share):
    frames, slots, width = video.shape
    return pl.pallas_call(
        norm_in_body,
        grid=(frames,),
        in_specs=[pl.BlockSpec((None, slots, width), lambda f: (f, 0, 0)), fixed((width,)), fixed((width,))],
        out_specs=by_part(parts, share, width),
        out_shape=jax.ShapeDtypeStruct((parts, frames, share, width), BF16),
        cost_estimate=pl.CostEstimate(flops=1 * 10**9, bytes_accessed=10 * MIB, transcendentals=0),
        compiler_params=params(),
        name="norm_in",
    )(video, gain, shift)


STEP = 16


def stacked(block, rows):
    return jnp.concatenate([block * head_lanes(rows, head, BF16) for head in range(GROUP)], axis=0)


def temporal_fwd_body(x_ref, wq_ref, wk_ref, wv_ref, bq_ref, bv_ref, q_ref, k_ref, v_ref, *o_refs):
    frames, slots, width = x_ref.shape
    x = x_ref[...].reshape(frames * slots, width)
    shape = (frames, slots, WIDE)
    q_ref[...] = ((dot(x, wq_ref[...]) + bq_ref[...]) * HEAD_DIM**-0.5).astype(BF16).reshape(shape)
    k_ref[...] = dot(x, wk_ref[...]).astype(BF16).reshape(shape)
    v_ref[...] = (dot(x, wv_ref[...]) + bv_ref[...]).astype(BF16).reshape(shape)
    rows = frames * STEP
    row = lax.broadcasted_iota(jnp.int32, (rows, rows), 0)
    col = lax.broadcasted_iota(jnp.int32, (rows, rows), 1)
    same = row % STEP == col % STEP
    for step in range(slots // STEP):
        part = slice(step * STEP, (step + 1) * STEP)
        q = q_ref[:, part, :].reshape(rows, WIDE)
        keys = stacked(k_ref[:, part, :].reshape(rows, WIDE), rows)
        values = stacked(v_ref[:, part, :].reshape(rows, WIDE), rows)
        scores = dot_nt(q, keys)
        mixing = []
        for head in range(GROUP):
            s = jnp.where(same, scores[:, head * rows : (head + 1) * rows], -1e30)
            e = jnp.exp(s - jnp.max(s, axis=1, keepdims=True))
            mixing.append((e / jnp.sum(e, axis=1, keepdims=True)).astype(BF16))
        o = dot(jnp.concatenate(mixing, axis=1), values)
        o = o.astype(BF16).reshape(frames // len(o_refs), len(o_refs), STEP, WIDE)
        for place, o_ref in enumerate(o_refs):
            o_ref[:, part, :] = o[:, place]


def temporal_fwd(x, weight, bias, local):
    frames, slots, width = x.shape
    groups = width // WIDE
    w = lambda part: pl.BlockSpec((width, WIDE), lambda g: (0, part * groups + g))
    b = lambda part: pl.BlockSpec((1, WIDE), lambda g: (0, part * groups + g))
    one = pl.BlockSpec((frames, slots, WIDE), lambda g: (0, 0, g))
    return pl.pallas_call(
        temporal_fwd_body,
        grid=(groups,),
        in_specs=[fixed(x.shape), w(0), w(1), w(2), b(0), b(1)],
        out_specs=[one] * 3 + [pl.BlockSpec((frames // local, slots, WIDE), lambda g: (0, 0, g))] * local,
        out_shape=[jax.ShapeDtypeStruct(x.shape, BF16)] * 3
        + [jax.ShapeDtypeStruct((frames // local, slots, width), BF16)] * local,
        cost_estimate=pl.CostEstimate(flops=30 * 10**9, bytes_accessed=16 * MIB, transcendentals=0),
        compiler_params=params(),
        name="temporal_fwd",
    )(x, weight, weight, weight, bias, bias)


def temporal_bwd_body(
    x_ref, q_ref, k_ref, v_ref, g_ref, wq_ref, wk_ref, wv_ref, gain_ref, shift_ref,
    dq_ref, dk_ref, dv_ref, dx_ref, sums_ref, norm_ref, total_ref,
):
    frames, slots, width = x_ref.shape
    rows = frames * STEP
    row = lax.broadcasted_iota(jnp.int32, (rows, rows), 0)
    col = lax.broadcasted_iota(jnp.int32, (rows, rows), 1)
    same = row % STEP == col % STEP
    shape = (frames, STEP, WIDE)
    for step in range(slots // STEP):
        part = slice(step * STEP, (step + 1) * STEP)
        k = k_ref[:, part, :].reshape(rows, WIDE)
        v = v_ref[:, part, :].reshape(rows, WIDE)
        queries = stacked(q_ref[:, part, :].reshape(rows, WIDE), rows)
        grads = stacked(g_ref[:, part, :].reshape(rows, WIDE), rows)
        scores = dot_nt(k, queries)
        grad_mixing = dot_nt(v, grads)
        mixing, grad_scores = [], []
        for head in range(GROUP):
            span = slice(head * rows, (head + 1) * rows)
            s = jnp.where(same, scores[:, span], -1e30)
            e = jnp.exp(s - jnp.max(s, axis=0, keepdims=True))
            p = e / jnp.sum(e, axis=0, keepdims=True)
            gp = grad_mixing[:, span]
            ds = p * (gp - jnp.sum(p * gp, axis=0, keepdims=True))
            mixing.append(p.astype(BF16))
            grad_scores.append(ds.astype(BF16))
        grad_scores = jnp.concatenate(grad_scores, axis=1)
        dv_ref[:, part, :] = dot(jnp.concatenate(mixing, axis=1), grads).astype(BF16).reshape(shape)
        dk_ref[:, part, :] = dot(grad_scores, queries).astype(BF16).reshape(shape)
        spread = dot_tn(grad_scores, k)
        dq = jnp.zeros((rows, WIDE), F32)
        for head in range(GROUP):
            dq = dq + spread[head * rows : (head + 1) * rows] * head_lanes(rows, head, F32)
        dq_ref[:, part, :] = (dq * HEAD_DIM**-0.5).astype(BF16).reshape(shape)
    flat = (frames * slots, WIDE)
    dq, dk, dv = dq_ref[...].reshape(flat), dk_ref[...].reshape(flat), dv_ref[...].reshape(flat)
    sums_ref[...] = jnp.concatenate([column_sum(dq), column_sum(dv), jnp.zeros((6, WIDE), F32)], axis=0)
    update = dot_nt(dq, wq_ref[...]) + dot_nt(dk, wk_ref[...]) + dot_nt(dv, wv_ref[...])
    group = pl.program_id(0)

    @pl.when(group == 0)
    def _():
        total_ref[...] = update

    @pl.when(group > 0)
    def _():
        total_ref[...] += update

    @pl.when(group == pl.num_programs(0) - 1)
    def _():
        total = total_ref[...]
        dx_ref[...] = total.astype(BF16).reshape(frames, slots, width)
        x = x_ref[...].reshape(frames * slots, width).astype(F32)
        shift_grad = column_sum(total)
        gain_grad = (column_sum(total * x) - shift_ref[...][None] * shift_grad) / gain_ref[...][None]
        norm_ref[...] = jnp.concatenate([gain_grad, shift_grad, jnp.zeros((6, width), F32)], axis=0)


def temporal_bwd(x, q, k, v, grad, weight, gain, shift):
    frames, slots, width = x.shape
    groups = width // WIDE
    w = lambda part: pl.BlockSpec((width, WIDE), lambda g: (0, part * groups + g))
    one = pl.BlockSpec((frames, slots, WIDE), lambda g: (0, 0, g))
    return pl.pallas_call(
        temporal_bwd_body,
        grid=(groups,),
        in_specs=[fixed(x.shape), one, one, one, one, w(0), w(1), w(2), fixed((width,)), fixed((width,))],
        out_specs=[one, one, one, fixed(x.shape), pl.BlockSpec((8, WIDE), lambda g: (0, g)), fixed((8, width))],
        out_shape=[jax.ShapeDtypeStruct(x.shape, BF16)] * 4 + [jax.ShapeDtypeStruct((8, width), F32)] * 2,
        scratch_shapes=[pltpu.VMEM((frames * slots, width), F32)],
        cost_estimate=pl.CostEstimate(flops=35 * 10**9, bytes_accessed=30 * MIB, transcendentals=0),
        compiler_params=params(),
        name="temporal_bwd",
    )(x, q, k, v, grad, weight, weight, weight, gain, shift)


def middle_body(mixed_ref, video_ref, proj_ref, pb_ref, gain_ref, shift_ref, w_ref, bias_ref, first_ref, normed_ref, qkv_ref):
    slots, width = video_ref.shape
    first = video_ref[...].astype(F32) + (dot(joined_positions(mixed_ref, slots), proj_ref[...]) + pb_ref[...])
    first_ref[...] = first
    unit, _ = norm_parts(first)
    normed_ref[...] = (unit * gain_ref[...] + shift_ref[...]).astype(BF16)
    normed = normed_ref[...]
    q = dot(normed, w_ref[:, :width]) + bias_ref[:, :width]
    qkv_ref[:, :width] = (q * HEAD_DIM**-0.5).astype(BF16)
    qkv_ref[:, width : 2 * width] = dot(normed, w_ref[:, width : 2 * width]).astype(BF16)
    qkv_ref[:, 2 * width :] = (dot(normed, w_ref[:, 2 * width :]) + bias_ref[:, width:]).astype(BF16)


def middle(frame, mixed, video, proj, proj_bias, gain, shift, weight, bias):
    _, slots, width = video.shape
    return pl.pallas_call(
        middle_body,
        grid=(1,),
        in_specs=[
            fixed(mixed.shape), pl.BlockSpec((None, slots, width), lambda i: (frame, 0, 0)), fixed(proj.shape), fixed((width,)),
            fixed((width,)), fixed((width,)), fixed(weight.shape), fixed((1, 2 * width)),
        ],
        out_specs=[fixed((slots, width)), fixed((slots, width)), fixed((slots, 3 * width))],
        out_shape=[
            jax.ShapeDtypeStruct((slots, width), F32),
            jax.ShapeDtypeStruct((slots, width), BF16),
            jax.ShapeDtypeStruct((slots, 3 * width), BF16),
        ],
        cost_estimate=pl.CostEstimate(flops=11 * 10**9, bytes_accessed=14 * MIB, transcendentals=0),
        compiler_params=params(),
        name="middle",
    )(mixed, video, proj, proj_bias, gain, shift, weight, bias)


def gelu_both(value):
    half = 0.5 * (1.0 + lax.erf(value * 0.7071067811865476))
    density = jnp.exp(-0.5 * value * value) * 0.3989422804014327
    return value * half, half + value * density


def feed_body(
    cot_ref, proj_ref, pb_ref, gain_ref, shift_ref, fc1_ref, fb1_ref, fc2_ref, fb2_ref, *refs, sub, frames,
):
    firsts, mixeds, refs = refs[:frames], refs[frames : 2 * frames], refs[2 * frames :]
    out_ref, normed_ref, hidden_ref, gi_ref, gs_ref, gso_ref, gspace_ref, sums_ref, unitsum_ref, second, branch, gnorm = refs
    frame, chunk = pl.program_id(0), pl.program_id(1)
    slots, width = cot_ref.shape
    units = fc1_ref.shape[1]
    for place in range(frames):

        @pl.when(jnp.logical_and(chunk == 0, frame == place))
        def _(place=place):
            second[...] = firsts[place][...] + (dot(mixeds[place][...], proj_ref[...]) + pb_ref[...])

    @pl.when(chunk == 0)
    def _():
        value = second[...]
        unit, _ = norm_parts(value)
        normed_ref[...] = (unit * gain_ref[...] + shift_ref[...]).astype(BF16)
        branch[...] = jnp.zeros_like(branch)
        gnorm[...] = jnp.zeros_like(gnorm)

    @pl.when(jnp.logical_and(frame == 0, chunk == 0))
    def _():
        sums_ref[...] = jnp.zeros_like(sums_ref)
        unitsum_ref[...] = jnp.zeros_like(unitsum_ref)

    normed = normed_ref[...]
    cot = cot_ref[...]
    for start in range(0, units, sub):
        span = slice(start, start + sub)
        inner = dot(normed, fc1_ref[:, span]) + fb1_ref[0:1, span]
        grad_hidden = dot(cot, fc2_ref[:, span])
        act, slope = gelu_both(inner)
        hidden_ref[:, span] = act.astype(BF16)
        gi_ref[:, span] = (grad_hidden * slope).astype(BF16)
    branch[...] += dot_nt(hidden_ref[...], fc2_ref[...])
    gnorm[...] += dot_nt(gi_ref[...], fc1_ref[...])
    unitsum_ref[chunk, 0:1, :] += column_sum(gi_ref[...])

    @pl.when(chunk == pl.num_programs(1) - 1)
    def _():
        value = second[...]
        out_ref[...] = (value + (branch[...] + fb2_ref[...])).astype(BF16)
        unit, scale = norm_parts(value)
        grad = gnorm[...]
        cot_full = cot_ref[...].astype(F32)
        grad_second = cot_full + norm_grad(grad, unit, scale, gain_ref[...])
        gs_ref[...] = grad_second
        gso_ref[...] = grad_second.astype(BF16)
        gspace_ref[...] = dot_nt(gso_ref[...], proj_ref[...]).astype(BF16)
        sums_ref[0:1, :] += column_sum(grad * unit)
        sums_ref[1:2, :] += column_sum(grad)
        sums_ref[2:3, :] += column_sum(gso_ref[...])
        sums_ref[3:4, :] += column_sum(cot_full)


def feed(first, mixed, cot, proj, proj_bias, gain, shift, joint, fc1_bias, fc2_bias, sub=None):
    frames, slots, width = cot.shape
    chunks, _, units = fc1_bias.shape
    sub = sub or units
    per = pl.BlockSpec((None, slots, width), lambda f, c: (f, 0, 0))
    row = fixed((width,))
    hid = pl.BlockSpec((None, None, slots, units), lambda f, c: (c, f, 0, 0))
    hid_shape = jax.ShapeDtypeStruct((chunks, frames, slots, units), BF16)
    tok = lambda dtype: jax.ShapeDtypeStruct(cot.shape, dtype)
    return pl.pallas_call(
        functools.partial(feed_body, sub=sub, frames=frames),
        grid=(frames, chunks),
        in_specs=[
            per, fixed(proj.shape), row, row, row,
            pl.BlockSpec((None, width, units), lambda f, c: (c, 0, 0)),
            pl.BlockSpec((None, 1, units), lambda f, c: (c, 0, 0)),
            pl.BlockSpec((None, width, units), lambda f, c: (c, 0, 1)),
            row,
        ] + [fixed((slots, width))] * (2 * frames),
        out_specs=[per, per, hid, hid, per, per, per, fixed((8, width)), fixed((chunks, 8, units))],
        out_shape=[
            tok(BF16), tok(BF16), hid_shape, hid_shape, tok(F32), tok(BF16), tok(BF16),
            jax.ShapeDtypeStruct((8, width), F32), jax.ShapeDtypeStruct((chunks, 8, units), F32),
        ],
        scratch_shapes=[pltpu.VMEM((slots, width), F32)] * 3,
        cost_estimate=pl.CostEstimate(flops=56 * 10**9, bytes_accessed=60 * MIB, transcendentals=0),
        compiler_params=params(60),
        name="feed",
    )(cot, proj, proj_bias, gain, shift, joint, fc1_bias, joint, fc2_bias, *first, *mixed)


def middle_bwd_body(
    dq_ref, dk_ref, dv_ref, w_ref, first_ref, gs_ref, gain_ref, proj_ref, gf_ref, gto_ref, gt_ref, sums_ref
):
    slots, width = first_ref.shape
    dq, dk, dv = dq_ref[...], dk_ref[...], dv_ref[...]
    grad = dot_nt(dq, w_ref[:, :width]) + dot_nt(dk, w_ref[:, width : 2 * width]) + dot_nt(dv, w_ref[:, 2 * width :])
    unit, scale = norm_parts(first_ref[...])
    grad_first = gs_ref[...] + norm_grad(grad, unit, scale, gain_ref[...])
    gf_ref[...] = grad_first
    gto_ref[...] = grad_first.astype(BF16)
    split_positions(gt_ref, dot_nt(gto_ref[...], proj_ref[...]).astype(BF16))

    rows = [grad * unit, grad, dq, dv, gto_ref[...]]
    sums_ref[...] = jnp.concatenate([column_sum(value) for value in rows] + [jnp.zeros((3, width), F32)], axis=0)


def middle_bwd(frame, dq, dk, dv, weight, first, grad_second, gain, proj, parts, share):
    slots, width = first.shape
    return pl.pallas_call(
        middle_bwd_body,
        grid=(1,),
        in_specs=[
            fixed((slots, width)), fixed((slots, width)), fixed((slots, width)), fixed(weight.shape), fixed((slots, width)),
            pl.BlockSpec((None, slots, width), lambda i: (frame, 0, 0)), fixed((width,)), fixed(proj.shape),
        ],
        out_specs=[fixed((slots, width)), fixed((slots, width)), fixed((parts, share, width)), fixed((8, width))],
        out_shape=[
            jax.ShapeDtypeStruct(first.shape, F32), jax.ShapeDtypeStruct(first.shape, BF16),
            jax.ShapeDtypeStruct((parts, share, width), BF16), jax.ShapeDtypeStruct((8, width), F32),
        ],
        cost_estimate=pl.CostEstimate(flops=14 * 10**9, bytes_accessed=16 * MIB, transcendentals=0),
        compiler_params=params(60),
        name="middle_bwd",
    )(dq, dk, dv, weight, first, grad_second, gain, proj)


def norm_out_body(grad_ref, video_ref, gain_ref, *refs):
    *gf_refs, out_ref = refs
    slots = video_ref.shape[0]
    frame = pl.program_id(0)
    unit, scale = norm_parts(video_ref[...].astype(F32))
    result = norm_grad(joined_positions(grad_ref, slots).astype(F32), unit, scale, gain_ref[...])
    for place, gf_ref in enumerate(gf_refs):

        @pl.when(frame == place)
        def _(gf_ref=gf_ref):
            out_ref[...] = gf_ref[...] + result


def norm_out(grad, video, grad_first, gain):
    frames, slots, width = video.shape
    per = lambda rows: pl.BlockSpec((None, rows, width), lambda f: (f, 0, 0))
    return pl.pallas_call(
        norm_out_body,
        grid=(frames,),
        in_specs=[by_part(grad.shape[0], grad.shape[2], width), per(slots), fixed((width,))]
        + [fixed((slots, width))] * frames,
        out_specs=per(slots),
        out_shape=jax.ShapeDtypeStruct(video.shape, F32),
        cost_estimate=pl.CostEstimate(flops=1 * 10**9, bytes_accessed=25 * MIB, transcendentals=0),
        compiler_params=params(),
        name="norm_out",
    )(grad, video, gain, *grad_first)


def tn_body(*refs):
    *refs, out_ref = refs
    count = len(refs) // 2
    total = None
    for a_ref, b_ref in zip(refs[:count], refs[count:]):
        rows, width = b_ref.shape[0], a_ref.shape[-1]
        part = dot_tn(a_ref[...].reshape(-1, width)[:rows], b_ref[...])
        total = part if total is None else total + part
    out_ref[...] = total.astype(out_ref.dtype)


def weight_grad(a, b):
    if isinstance(b, list):
        rows, width = b[0].shape
        places = [0] * len(b)
    else:
        rows, width = b.shape[0] // len(a), b.shape[1]
        places, b = range(len(a)), [b] * len(a)
    return pl.pallas_call(
        tn_body,
        grid=(width // WIDE,),
        in_specs=[fixed(value.shape) for value in a] + [pl.BlockSpec((rows, WIDE), lambda i, p=p: (p, i)) for p in places],
        out_specs=pl.BlockSpec((width, WIDE), lambda i: (0, i)),
        out_shape=jax.ShapeDtypeStruct((width, width), BF16),
        cost_estimate=pl.CostEstimate(
            flops=2 * len(b) * rows * width * width, bytes_accessed=4 * len(b) * rows * width, transcendentals=0
        ),
        compiler_params=params(),
        name="weight_grad",
    )(*a, *b)


def fc_grads_body(normed_ref, cot_ref, gi_ref, hid_ref, out_ref):
    units = gi_ref.shape[1]
    out_ref[:, :units] = dot_tn(normed_ref[...], gi_ref[...]).astype(BF16)
    out_ref[:, units:] = dot_tn(cot_ref[...], hid_ref[...]).astype(BF16)


def fc_grads(normed, cot, grad_inner, hidden):
    chunks, frames, slots, units = hidden.shape
    width = normed.shape[-1]
    rows = frames * slots
    hid = pl.BlockSpec((None, rows, units), lambda c: (c, 0, 0))
    flat = lambda value: value.reshape(chunks, rows, units)
    return pl.pallas_call(
        fc_grads_body,
        grid=(chunks,),
        in_specs=[fixed((rows, width)), fixed((rows, width)), hid, hid],
        out_specs=pl.BlockSpec((None, width, 2 * units), lambda c: (c, 0, 0)),
        out_shape=jax.ShapeDtypeStruct((chunks, width, 2 * units), BF16),
        cost_estimate=pl.CostEstimate(
            flops=4 * rows * width * units * chunks, bytes_accessed=4 * rows * units * chunks, transcendentals=0
        ),
        compiler_params=params(),
        name="fc_grads",
    )(normed.reshape(rows, width), cot.reshape(rows, width), flat(grad_inner), flat(hidden))


def finish_body(time_ref, space_ref, space_proj_ref, time_proj_ref, time_out, space_out, space_proj_out, time_proj_out):
    for group in range(time_ref.shape[0]):
        time_out[:, group * WIDE : (group + 1) * WIDE] = time_ref[group].astype(F32)
    space_out[...] = space_ref[...].astype(F32)

    @pl.when(pl.program_id(0) == 0)
    def _():
        space_proj_out[...] = space_proj_ref[...].astype(F32)
        time_proj_out[...] = time_proj_ref[...].astype(F32)


def finish(matrices):
    width = matrices.shape[1]
    groups = width // WIDE
    one = lambda at: pl.BlockSpec((None, width, width), lambda i: (at, 0, 0))
    block = pl.BlockSpec((width, width), lambda i: (0, i))
    full = jax.ShapeDtypeStruct((width, 3 * width), F32)
    square = jax.ShapeDtypeStruct((width, width), F32)
    return pl.pallas_call(
        finish_body,
        grid=(3,),
        in_specs=[
            pl.BlockSpec((groups, width, WIDE), lambda i: (0, 0, i)),
            pl.BlockSpec((None, width, width), lambda i: (groups + i, 0, 0)), one(groups + 3), one(groups + 4),
        ],
        out_specs=[block, block, fixed((width, width)), fixed((width, width))],
        out_shape=[full, full, square, square],
        cost_estimate=pl.CostEstimate(flops=1 * 10**9, bytes_accessed=30 * MIB, transcendentals=0),
        compiler_params=params(),
        name="finish",
    )(matrices, matrices, matrices, matrices)


MESH = pl.DeviceIdType.MESH
EARLY_GAP = 3.0
HOP = 4.0
RATE = 1


def cuts_of(rows, count):
    blocks, cuts, at = rows // 16, [], 0
    for i in range(count):
        size = (blocks // count + (1 if i < blocks % count else 0)) * 16
        cuts.append((at, size))
        at += size
    return cuts


def bits_of(count):
    return [1 << i for i in range(count.bit_length() - 1)]


def reducible(width, planes, parts):
    return parts == 4 and planes >= 4 and planes & (planes - 1) == 0 and width % (planes * 2 * 16) == 0


class Ring:
    def __init__(self, planes):
        self.bits = bits_of(planes)
        self.deep = len(self.bits)
        self.plane, self.part = lax.axis_index("dp"), lax.axis_index("mp")
        self.by_bit = {bit: {"dp": self.plane + bit - 2 * bit * self.place(bit)} for bit in self.bits}
        self.beside = {"mp": self.part + 1 - 2 * (self.part % 2)}
        self.across = {"mp": 3 - self.part}
        self.third = {"mp": (self.part + 2) % 4}
        self.inner = ((self.part + 1) // 2) % 2 == 1
        self.outer = ((self.part + 1) // 2) % 2 == 0
        self.started = []

    def place(self, bit):
        return (self.plane // bit) % 2

    def greet(self):
        partners = [self.by_bit[bit] for bit in self.bits] + [self.beside, self.across, self.third]
        barrier = pltpu.get_barrier_semaphore()
        for partner in partners:
            pl.semaphore_signal(barrier, inc=1, device_id=partner, device_id_type=MESH)
        pl.semaphore_wait(barrier, len(partners))

    def order(self, stream):
        return self.bits if stream == 0 else self.bits[:1] + self.bits[1:][::-1]

    def send(self, source, target, sems, at, partner, when=None):
        send_sem, recv_sem = sems
        copy = pltpu.make_async_remote_copy(
            src_ref=source, dst_ref=target, send_sem=send_sem.at[at], recv_sem=recv_sem.at[at],
            device_id=partner, device_id_type=MESH,
        )
        if when is None:
            copy.start()
        else:
            pl.when(when)(copy.start)
        self.started.append((when, copy))
        return copy

    def finish(self):
        for when, copy in self.started:
            if when is None:
                copy.wait_send()
            else:
                pl.when(when)(copy.wait_send)

    def rows(self, chain, level, width):
        stream = chain % 2
        mine = self.order(stream)
        size = width // 2
        spot, length = self.place(mine[0]) * size + stream * (size // 2), size // 2
        for bit in mine[1:level]:
            length //= 2
            spot = spot + self.place(bit) * length
        return spot, length


def rows_at(offset, size):
    return pl.ds(pl.multiple_of(offset, 16), size)


class Reduction:
    def __init__(self, ring, own, got, line, piece, out, spots, sems, back_sems, out_sem):
        self.ring, self.own, self.got, self.line, self.piece, self.sems = ring, own, got, line, piece, sems
        self.out, self.spots, self.back_sems, self.out_sem = out, spots, back_sems, out_sem
        self.width = own.shape[1]
        self.waiting = {}
        self.local = {}
        self.steps = 2 * ring.deep + 4

    def back(self, chain, step):
        ring, matrix = self.ring, chain // 2
        level = ring.deep - step
        if step == 0:
            spot, length = ring.rows(chain, level, self.width)
            source, region = self.piece.at[chain], self.out.at[self.spots[matrix], rows_at(spot, length)]
            self.local[chain] = pltpu.make_async_copy(source, region, self.out_sem.at[chain])
            self.local[chain].start()
        else:
            if step == 1:
                self.local[chain].wait()
            self.waiting[chain].wait_recv()
            if step == ring.deep:
                return
            spot, length = ring.rows(chain, level, self.width)
            source = region = self.out.at[self.spots[matrix], rows_at(spot, length)]
        partner = ring.by_bit[ring.order(chain % 2)[level - 1]]
        self.waiting[chain] = ring.send(source, region, self.back_sems, (chain, step), partner)

    def advance(self, chain, step):
        ring, deep = self.ring, self.ring.deep
        matrix, stream = chain // 2, chain % 2
        mine = ring.order(stream)
        size = self.width // 2
        got = self.got
        if step < deep or step == deep:
            if step == 0:
                spot = (1 - ring.place(mine[0])) * size + stream * (size // 2)
                source = self.own.at[matrix, rows_at(spot, size // 2)]
            else:
                self.waiting[chain].wait_recv()
                count = got[step - 1].shape[1]
                if step == 1:
                    kept = self.own[matrix, rows_at(ring.place(mine[0]) * size + stream * (size // 2), count), :]
                else:
                    kept = got[step - 2][chain, rows_at(ring.place(mine[step - 1]) * count, count), :]
                got[step - 1][chain] = (kept.astype(F32) + got[step - 1][chain].astype(F32)).astype(BF16)
                if step < deep:
                    half = count // 2
                    source = got[step - 1].at[chain, rows_at((1 - ring.place(mine[step])) * half, half)]
            if step < deep:
                self.waiting[chain] = ring.send(
                    source, got[step].at[chain], self.sems, (chain, step), ring.by_bit[mine[step]]
                )
                return
        if step <= deep + 3:
            self.line.advance(chain, step - deep, got[deep - 1].at[chain])
        if step >= deep + 3:
            self.back(chain, step - deep - 3)


class Line:
    def __init__(self, ring, lines, piece, sems, first=0):
        self.ring, self.lines, self.piece, self.sems, self.first = ring, lines, piece, sems, first
        self.waiting = {}

    def advance(self, chain, step, source):
        ring, lines, at = self.ring, self.lines, chain - self.first
        if step == 0:
            self.waiting[chain] = ring.send(source, lines[0].at[at], self.sems, (at, 0), ring.beside, ring.outer)
        elif step == 1:
            first = self.waiting[chain]

            @pl.when(ring.inner)
            def _():
                first.wait_recv()
                lines[0][at] = (source[...].astype(F32) + lines[0][at].astype(F32)).astype(BF16)

            self.waiting[chain] = ring.send(lines[0].at[at], lines[1].at[at], self.sems, (at, 1), ring.across, ring.inner)
        elif step == 2:
            second = self.waiting[chain]

            @pl.when(ring.inner)
            def _():
                second.wait_recv()
                both = (lines[0][at].astype(F32) + lines[1][at].astype(F32)).astype(BF16)
                self.piece[chain - self.first] = both
                lines[2][at] = both

            self.waiting[chain] = ring.send(lines[2].at[at], lines[3].at[at], self.sems, (at, 2), ring.beside, ring.inner)
        else:
            third = self.waiting[chain]

            @pl.when(ring.outer)
            def _():
                third.wait_recv()
                self.piece[chain - self.first] = lines[3][at]


def reduction_scratch(chains, width, deep):
    length = width // 4
    sizes = [length >> i for i in range(deep)]
    shapes = [pltpu.VMEM((chains, size, width), BF16) for size in sizes + [sizes[-1]] * 4]
    return shapes + [pltpu.SemaphoreType.DMA((chains, deep))] * 2 + [pltpu.SemaphoreType.DMA((chains, 3))] * 2 + [
        pltpu.SemaphoreType.DMA((chains, deep))
    ] * 2 + [pltpu.SemaphoreType.DMA((chains,)), pltpu.VMEM((chains, sizes[-1], width), BF16)]


def temporal_tail_body(
    gain_ref, shift_ref, small_in, *refs, planes, early, taken, local,
):
    g_refs, (x_hbm, q_hbm, k_hbm, v_hbm, w_hbm), refs = refs[:local], refs[local : local + 5], refs[local + 5 :]
    early_hbm, refs = refs[:early], refs[early:]
    moved_ref, out_ref, small_out, refs = refs[0], refs[1], refs[2], refs[3:]
    x_ref, qkv_ref, w_ref, d_ref, dx_ref, own, load_sem, refs = *refs[:7], refs[7:]
    move_send, move_recv, move_local, small_ref, small_got, small_held, small_send, small_recv, refs = *refs[:8], refs[8:]
    ring = Ring(planes)
    deep = ring.deep
    got, lines, refs = refs[:deep], refs[deep : deep + 4], refs[deep + 4 :]
    sems, line_sems, back_sems, out_sem, piece_ref = refs[:2], refs[2:4], refs[4:6], refs[6], refs[7]
    frames, slots, width = x_ref.shape
    groups = width // WIDE
    rows = frames * STEP
    loads = {}

    def load(name, source, target, at):
        copy = pltpu.make_async_copy(source, target, load_sem.at[at])
        copy.start()
        loads[name] = copy

    def load_group(group):
        for place, ref in enumerate((q_hbm, k_hbm, v_hbm)):
            source = ref.at[:, :, pl.ds(group * WIDE, WIDE)]
            load(("qkv", group, place), source, qkv_ref.at[group % 2, place], early + 2 + 3 * group + place)

    load_group(0)
    for matrix in range(early):
        load(("own", matrix), early_hbm[matrix], own.at[matrix], matrix)
    load("x", x_hbm, x_ref, early)
    load("w", w_hbm, w_ref, early + 1)
    ring.greet()
    matrices = early + groups
    line = Line(ring, lines, piece_ref, line_sems)
    spots = [groups + matrix for matrix in range(early)] + list(range(groups))
    sums = Reduction(ring, own, got, line, piece_ref, out_ref, spots, sems, back_sems, out_sem)
    small_ref[...] = small_in[...]

    row = lax.broadcasted_iota(jnp.int32, (rows, rows), 0)
    col = lax.broadcasted_iota(jnp.int32, (rows, rows), 1)
    same = row % STEP == col % STEP
    shape = (frames, STEP, WIDE)
    starts = {}
    ready = {}

    def compute():
        for group in range(groups):
            if group + 1 < groups:
                load_group(group + 1)
            for place in range(3):
                loads[("qkv", group, place)].wait()
            slot = group % 2
            lanes = slice(group * WIDE, (group + 1) * WIDE)
            for step in range(slots // STEP):
                part = slice(step * STEP, (step + 1) * STEP)
                k = qkv_ref[slot, 1, :, part, :].reshape(rows, WIDE)
                v = qkv_ref[slot, 2, :, part, :].reshape(rows, WIDE)
                queries = stacked(qkv_ref[slot, 0, :, part, :].reshape(rows, WIDE), rows)
                grads = jnp.stack([g_ref[:, part, lanes] for g_ref in g_refs], axis=1)
                grads = stacked(grads.reshape(rows, WIDE), rows)
                scores = dot_nt(k, queries)
                grad_mixing = dot_nt(v, grads)
                mixing, grad_scores = [], []
                for head in range(GROUP):
                    span = slice(head * rows, (head + 1) * rows)
                    s = jnp.where(same, scores[:, span], -1e30)
                    e = jnp.exp(s - jnp.max(s, axis=0, keepdims=True))
                    p = e / jnp.sum(e, axis=0, keepdims=True)
                    gp = grad_mixing[:, span]
                    ds = p * (gp - jnp.sum(p * gp, axis=0, keepdims=True))
                    mixing.append(p.astype(BF16))
                    grad_scores.append(ds.astype(BF16))
                grad_scores = jnp.concatenate(grad_scores, axis=1)
                dv = dot(jnp.concatenate(mixing, axis=1), grads)
                dk = dot(grad_scores, queries)
                spread = dot_tn(grad_scores, k)
                dq = jnp.zeros((rows, WIDE), F32)
                for head in range(GROUP):
                    dq = dq + spread[head * rows : (head + 1) * rows] * head_lanes(rows, head, F32)
                d_ref[group, :, part, :WIDE] = (dq * HEAD_DIM**-0.5).astype(BF16).reshape(shape)
                d_ref[group, :, part, WIDE : 2 * WIDE] = dk.astype(BF16).reshape(shape)
                d_ref[group, :, part, 2 * WIDE :] = dv.astype(BF16).reshape(shape)
                if step % 4 == 3:
                    yield 2.0
            if group == 0:
                loads["x"].wait()
            d = d_ref[group].reshape(frames * slots, 3 * WIDE)
            x = x_ref[...].reshape(frames * slots, width)
            own[early + group] = dot_tn(x, d).astype(BF16)
            ready[early + group] = True
            yield 4.5
            small_ref[taken : taken + 1, lanes] = column_sum(d[:, :WIDE])
            small_ref[taken + 1 : taken + 2, lanes] = column_sum(d[:, 2 * WIDE :])
        loads["w"].wait()
        quarter = frames // 4
        shift_grad, product = jnp.zeros((1, width), F32), jnp.zeros((1, width), F32)
        for distance in (2, 3, 1, 0):
            part = (ring.part + distance) % 4
            some = pl.ds(part * quarter, quarter)
            total = jnp.zeros((quarter * slots, width), F32)
            for group in range(groups):
                d = d_ref[group, some].reshape(quarter * slots, 3 * WIDE)
                for place in range(3):
                    weight = w_ref[:, pl.ds(place * width + group * WIDE, WIDE)]
                    total = total + dot_nt(d[:, place * WIDE : (place + 1) * WIDE], weight)
            dx_ref[some] = total.astype(BF16).reshape(quarter, slots, width)
            if distance:
                queue.extend((distance, cut) for cut in range(len(cuts)))
            else:
                keep = pltpu.make_async_copy(dx_ref.at[some], moved_ref.at[ring.part], move_local.at[0])
                keep.start()
                kept.append(keep)
            x = x_ref[some].reshape(quarter * slots, width)
            shift_grad += column_sum(total)
            product += column_sum(total * x.astype(F32))
            yield 3.5
        small_ref[taken + 2 : taken + 3, :] = (product - shift_ref[...][None] * shift_grad) / gain_ref[...][None]
        small_ref[taken + 3 : taken + 4, :] = shift_grad

    moves, kept, queue = [], [], []
    cuts = cuts_of(slots, 4)

    def move(distance, cut, arriving=False):
        target = (ring.part + distance) % 4
        source = (ring.part + 4 - distance) % 4 if arriving else ring.part
        span = pl.ds(*cuts[cut])
        return pltpu.make_async_remote_copy(
            src_ref=dx_ref.at[pl.ds(target * (frames // 4), frames // 4), span], dst_ref=moved_ref.at[source, :, span],
            send_sem=move_send.at[distance, cut], recv_sem=move_recv.at[source, cut],
            device_id={"mp": target}, device_id_type=MESH,
        )

    def send_some():
        for _ in range(RATE):
            if queue:
                moves.append(move(*queue.pop(0)))
                moves[-1].start()

    partners = [ring.by_bit[bit] for bit in ring.bits] + [ring.beside, ring.third]
    small_wait = []

    def small_step(step):
        if step > 0:
            small_wait.pop().wait_recv()
            before = small_ref[...] if step == 1 else small_held[step - 2]
            value = before + small_got[step - 1]
            if step == len(partners):
                small_out[...] = value
                return
            small_held[step - 1] = value
        source = small_ref if step == 0 else small_held.at[step - 1]
        small_wait.append(ring.send(source, small_got.at[step], (small_send, small_recv), step, partners[step]))

    following = [0] * matrices
    due = [EARLY_GAP * matrix for matrix in range(matrices)]
    clock = 0.0

    def advance_all():
        for matrix in range(matrices):
            step = following[matrix]
            if step < sums.steps and clock >= due[matrix] and (matrix < early or matrix in ready):
                if step == 0 and matrix < early:
                    loads[("own", matrix)].wait()
                for chain in (2 * matrix, 2 * matrix + 1):
                    sums.advance(chain, step)
                following[matrix] += 1
                due[matrix] = clock + HOP

    advance_all()
    for spent in compute():
        clock += spent
        send_some()
        advance_all()
    small_at = 0
    while any(step < sums.steps for step in following) or small_at <= len(partners) or queue:
        clock += HOP
        send_some()
        advance_all()
        if small_at <= len(partners):
            small_step(small_at)
            small_at += 1
    for distance in (1, 2, 3):
        for cut in range(len(cuts)):
            move(distance, cut, True).wait_recv()
    for copy in moves:
        copy.wait_send()
    kept[0].wait()
    ring.finish()


def temporal_tail(x, q, k, v, grad, weight, gain, shift, early, small, taken, planes, number):
    frames, slots, width = x.shape
    groups = width // WIDE
    deep = len(bits_of(planes))
    chains = 2 * (len(early) + groups)
    anywhere = pl.BlockSpec(memory_space=pl.ANY)
    whole = pl.BlockSpec(memory_space=pltpu.VMEM)
    flops = 2 * frames * slots * width * width * 12
    return pl.pallas_call(
        functools.partial(temporal_tail_body, planes=planes, early=len(early), taken=taken, local=len(grad)),
        in_specs=[whole] * (3 + len(grad)) + [anywhere] * (5 + len(early)),
        out_specs=[anywhere, anywhere, whole],
        out_shape=[
            jax.ShapeDtypeStruct((4, frames // 4, slots, width), BF16),
            jax.ShapeDtypeStruct((len(early) + groups, width, width), BF16),
            jax.ShapeDtypeStruct(small.shape, F32),
        ],
        scratch_shapes=[
            pltpu.VMEM(x.shape, BF16), pltpu.VMEM((2, 3, frames, slots, WIDE), BF16), pltpu.VMEM(weight.shape, BF16),
            pltpu.VMEM((groups, frames, slots, 3 * WIDE), BF16), pltpu.VMEM(x.shape, BF16),
            pltpu.VMEM((len(early) + groups, width, width), BF16),
            pltpu.SemaphoreType.DMA((len(early) + 2 + 3 * groups,)),
            pltpu.SemaphoreType.DMA((4, 4)), pltpu.SemaphoreType.DMA((4, 4)), pltpu.SemaphoreType.DMA((1,)),
            pltpu.VMEM(small.shape, F32), pltpu.VMEM((deep + 2,) + small.shape, F32), pltpu.VMEM((deep + 1,) + small.shape, F32),
            pltpu.SemaphoreType.DMA((deep + 2,)), pltpu.SemaphoreType.DMA((deep + 2,)),
        ] + reduction_scratch(chains, width, deep),
        cost_estimate=pl.CostEstimate(flops=flops, bytes_accessed=60 * MIB, transcendentals=0),
        compiler_params=pltpu.CompilerParams(vmem_limit_bytes=62 * MIB, collective_id=number, has_side_effects=True),
        name="temporal_tail",
    )(gain, shift, small, *grad, x, q, k, v, weight, *early)


AHEAD = 2


def temporal_head_body(video_ref, gain_ref, shift_ref, w_ref, bias_ref, *refs, chunks, local):
    x_out, q_out, k_out, v_out, refs = *refs[:4], refs[4:]
    o_outs, refs = refs[:local], refs[local:]
    normed, xs, qs, ks, vs, os, send_sem, recv_sem, out_sem = refs
    ring = Ring(lax.axis_size("dp"))
    me = ring.part
    frames, share, width = xs.shape
    slots = video_ref.shape[1]
    groups = width // WIDE
    barrier = pltpu.get_barrier_semaphore()
    for partner in (ring.beside, ring.across, ring.third):
        pl.semaphore_signal(barrier, inc=1, device_id=partner, device_id_type=MESH)
    pl.semaphore_wait(barrier, 3)
    sent, written = [], []

    def prepare(chunk):
        start, count = chunks[chunk]
        for part in range(4):
            for frame in range(local):
                first = part * share + start
                some = max(min(count, slots - first), 0)
                if some > 0:
                    unit, _ = norm_parts(video_ref[frame, first : first + some, :].astype(F32))
                    normed[part, frame, start : start + some, :] = (unit * gain_ref[...] + shift_ref[...]).astype(BF16)
                if some < count:
                    normed[part, frame, start + some : start + count, :] = jnp.zeros((count - some, width), BF16)
        for frame in range(local):
            xs[me * local + frame, start : start + count, :] = normed[me, frame, start : start + count, :]

    def move(chunk, distance, arriving=False):
        start, count = chunks[chunk]
        target = (me + distance) % 4
        source = (me + 4 - distance) % 4 if arriving else me
        return pltpu.make_async_remote_copy(
            src_ref=normed.at[target, :, pl.ds(start, count)],
            dst_ref=xs.at[pl.ds(source * local, local), pl.ds(start, count)],
            send_sem=send_sem.at[chunk, distance], recv_sem=recv_sem.at[chunk, source],
            device_id={"mp": target}, device_id_type=MESH,
        )

    def send(chunk):
        for distance in (2, 3, 1):
            copy = move(chunk, distance)
            copy.start()
            sent.append(copy)

    def write(source, target):
        copy = pltpu.make_async_copy(source, target, out_sem.at[len(written)])
        copy.start()
        written.append(copy)

    rows = frames * STEP
    row = lax.broadcasted_iota(jnp.int32, (rows, rows), 0)
    col = lax.broadcasted_iota(jnp.int32, (rows, rows), 1)
    same = row % STEP == col % STEP

    def compute(chunk):
        start, count = chunks[chunk]
        span = pl.ds(start, count)
        x = xs[:, start : start + count, :].reshape(frames * count, width)
        shape = (frames, count, WIDE)
        for group in range(groups):
            lanes = slice(group * WIDE, (group + 1) * WIDE)
            part = lambda place: slice(place * width + group * WIDE, place * width + (group + 1) * WIDE)
            q = (dot(x, w_ref[:, part(0)]) + bias_ref[:, part(0)]) * HEAD_DIM**-0.5
            v = dot(x, w_ref[:, part(2)]) + bias_ref[:, part(1)]
            qs[:, start : start + count, lanes] = q.astype(BF16).reshape(shape)
            ks[:, start : start + count, lanes] = dot(x, w_ref[:, part(1)]).astype(BF16).reshape(shape)
            vs[:, start : start + count, lanes] = v.astype(BF16).reshape(shape)
            for step in range(start // STEP, (start + count) // STEP):
                block = slice(step * STEP, (step + 1) * STEP)
                keys = stacked(ks[:, block, lanes].reshape(rows, WIDE), rows)
                values = stacked(vs[:, block, lanes].reshape(rows, WIDE), rows)
                scores = dot_nt(qs[:, block, lanes].reshape(rows, WIDE), keys)
                mixing = []
                for head in range(GROUP):
                    s = jnp.where(same, scores[:, head * rows : (head + 1) * rows], -1e30)
                    e = jnp.exp(s - jnp.max(s, axis=1, keepdims=True))
                    mixing.append((e / jnp.sum(e, axis=1, keepdims=True)).astype(BF16))
                o = dot(jnp.concatenate(mixing, axis=1), values).astype(BF16).reshape(4, local, STEP, WIDE)
                for frame in range(local):
                    os[frame, :, block, lanes] = o[:, frame]
        for frame in range(local):
            write(os.at[frame, :, span], o_outs[frame].at[:, span])
        for held, out in ((xs, x_out), (qs, q_out), (ks, k_out), (vs, v_out)):
            write(held.at[:, span], out.at[:, span])

    for chunk in range(len(chunks)):
        prepare(chunk)
        if chunk < AHEAD:
            send(chunk)
    for chunk in range(len(chunks)):
        for distance in (1, 2, 3):
            move(chunk, distance, True).wait_recv()
        if chunk + AHEAD < len(chunks):
            send(chunk + AHEAD)
        compute(chunk)
    for copy in sent:
        copy.wait_send()
    for copy in written:
        copy.wait()


def temporal_head(video, gain, shift, weight, bias, share, number):
    local, slots, width = video.shape
    frames = 4 * local
    count = 4
    chunks = cuts_of(share, count)
    whole = pl.BlockSpec(memory_space=pltpu.VMEM)
    anywhere = pl.BlockSpec(memory_space=pl.ANY)
    by_position = (frames, share, width)
    return pl.pallas_call(
        functools.partial(temporal_head_body, chunks=chunks, local=local),
        in_specs=[whole] * 5,
        out_specs=[anywhere] * (4 + local),
        out_shape=[jax.ShapeDtypeStruct(by_position, BF16)] * 4 + [jax.ShapeDtypeStruct((4, share, width), BF16)] * local,
        scratch_shapes=[pltpu.VMEM((4, local, share, width), BF16)] + [pltpu.VMEM(by_position, BF16)] * 4
        + [pltpu.VMEM((local, 4, share, width), BF16)]
        + [pltpu.SemaphoreType.DMA((count, 4))] * 2 + [pltpu.SemaphoreType.DMA((count * (4 + local),))],
        cost_estimate=pl.CostEstimate(flops=70 * 10**9, bytes_accessed=20 * MIB, transcendentals=0),
        compiler_params=pltpu.CompilerParams(vmem_limit_bytes=56 * MIB, collective_id=number, has_side_effects=True),
        name="temporal_head",
    )(video, gain, shift, weight, bias)


def middle_and_space(frame, mixed, video, proj, proj_bias, gain, shift, weight, bias, patch_width):
    first, normed, qkv = middle(frame, mixed, video, proj, proj_bias, gain, shift, weight, bias)
    space_mixed, lse = spatial_fwd(patch_width, qkv, 1, video.shape[1])
    return first, normed, qkv, space_mixed, lse


def shards(
    video,
    patch_width,
    temporal_gain,
    temporal_shift,
    temporal_qkv,
    temporal_qv_bias,
    temporal_proj,
    temporal_proj_bias,
    spatial_gain,
    spatial_shift,
    spatial_qkv,
    spatial_qv_bias,
    spatial_proj,
    spatial_proj_bias,
    mlp_gain,
    mlp_shift,
    fc1_weight,
    fc1_bias,
    fc2_weight,
    fc2_bias,
    cotangent,
):
    frames, sets, slots, width = video.shape
    units = fc1_weight.shape[1]
    parts, planes = lax.axis_size("mp"), lax.axis_size("dp")
    share = -(-slots // (parts * STEP)) * STEP
    row = lambda value: value.astype(F32).reshape(1, -1)
    video = video.reshape(frames * sets, slots, width)
    cot = cotangent.reshape(frames * sets, slots, width)

    joint = jnp.concatenate([fc1_weight, fc2_weight.T], axis=1)
    piece = width // planes
    own = lax.dynamic_slice_in_dim(joint, lax.axis_index("dp") * piece, piece, 0)
    bias_rows = jnp.pad(fc1_bias.reshape(1, units), ((0, 15), (0, units)))
    own = jnp.concatenate([own, bias_rows], axis=0)[None]

    def exchange(value):
        return lax.all_to_all(value, "mp", split_axis=0, concat_axis=0, tiled=True)

    by_position = lambda value: value.reshape(parts * frames, share, width)
    by_device = lambda value: value.reshape(parts, frames, share, width)
    column = lax.all_gather(own, "mp", axis=0, tiled=True)
    if reducible(width, planes, parts):
        x, tq, tk, tv, *time_mixed = temporal_head(
            video, temporal_gain, temporal_shift, temporal_qkv, row(temporal_qv_bias), share, 2
        )
    else:
        x = by_position(exchange(norm_in(video, temporal_gain, temporal_shift, parts, share)))
        tq, tk, tv, *time_mixed = temporal_fwd(x, temporal_qkv, row(temporal_qv_bias), frames)
    column, *time_mixed = lax.optimization_barrier((column, *time_mixed))
    fb1 = column[:, piece : piece + 1, :units].astype(F32)
    joint = lax.all_gather(column[:, :piece], "dp", axis=1, tiled=True)
    time_back = [exchange(value) for value in time_mixed]

    several = lambda results: [list(values) for values in zip(*results)]
    spatial = []
    for f in range(frames):
        if f > 0:
            time_back[f], lse_before = lax.optimization_barrier((time_back[f], spatial[-1][-1]))
            spatial[-1] = spatial[-1][:-1] + (lse_before,)
        spatial.append(
            middle_and_space(
                f, time_back[f], video, temporal_proj, temporal_proj_bias, spatial_gain, spatial_shift, spatial_qkv,
                row(spatial_qv_bias), patch_width,
            )
        )
    first, normed_mid, space_qkv, space_mixed, lse = several(spatial)

    output, normed_out, hidden, grad_inner, grad_second, grad_space_out, grad_space, feed_sums, unit_sums = feed(
        first, [value[0] for value in space_mixed], cot, spatial_proj, spatial_proj_bias, mlp_gain, mlp_shift, joint, fb1, fc2_bias
    )
    fc_part = fc_grads(normed_out, cot, grad_inner, hidden)
    fc_part = lax.psum_scatter(fc_part, "dp", scatter_dimension=1, tiled=True)

    dq, dk, dv, grad_first, grad_time_out, mid_sums, grad_slot = [], [], [], [], [], [], []
    for f in range(frames):
        q_f, k_f, v_f = spatial_bwd(f, patch_width, space_qkv[f], space_mixed[f], lse[f], grad_space, 1, slots)
        if f > 0:
            grad_slot[-1], q_f = lax.optimization_barrier((grad_slot[-1], q_f))
        first_f, out_f, time_f, sums_f = middle_bwd(
            f, q_f[0], k_f[0], v_f[0], spatial_qkv, first[f], grad_second, spatial_gain, temporal_proj, parts, share
        )
        if f + 1 < frames:
            time_f, grad_space = lax.optimization_barrier((time_f, grad_space))
        grad_slot.append(exchange(time_f))
        for kept, value in zip(
            (dq, dk, dv, grad_first, grad_time_out, mid_sums), (q_f[0], k_f[0], v_f[0], first_f, out_f, sums_f)
        ):
            kept.append(value)
    early = [
        weight_grad(normed_mid, dq),
        weight_grad(normed_mid, dk),
        weight_grad(normed_mid, dv),
        weight_grad([value[0] for value in space_mixed], grad_space_out.reshape(-1, width)),
        weight_grad(time_back, grad_time_out),
    ]
    fc_part, grad_first[-1] = lax.optimization_barrier((fc_part, grad_first[-1]))
    fc_part = lax.psum_scatter(fc_part, "mp", scatter_dimension=0, tiled=True)[0].astype(F32)
    fc1_weight_grad = fc_part[:, :units]
    fc2_weight_grad = fc_part[:, units:].T

    own_sums = [unit_sums[:, 0, :].reshape(-1, width), feed_sums[:4], sum(mid_sums)[:5]]
    weights = (temporal_qkv, temporal_gain, temporal_shift)
    wide = lambda blocks: jnp.concatenate([block.astype(F32) for block in blocks], axis=1)
    if reducible(width, planes, parts):
        taken = sum(rows.shape[0] for rows in own_sums)
        small = jnp.concatenate(own_sums + [jnp.zeros((4 + -(taken + 4) % 8, width), F32)], axis=0)
        grad_in, matrices, small = temporal_tail(x, tq, tk, tv, grad_slot, *weights, early, small, taken, planes, 1)
        temporal_qkv_grad, spatial_qkv_grad, spatial_proj_grad, temporal_proj_grad = finish(matrices)
    else:
        gq, gk, gv, grad_x, bias_sums, norm_sums = temporal_bwd(x, tq, tk, tv, by_position(jnp.stack(grad_slot, axis=1)), *weights)
        grad_in = exchange(by_device(grad_x))
        small = jnp.concatenate(own_sums + [bias_sums[:2], norm_sums[:2]], axis=0)
        flat = lambda value: value.reshape(-1, width)
        late = [weight_grad([flat(x)], [flat(value)]) for value in (gq, gk, gv)]
        matrices, small = lax.psum((jnp.stack(early + late), small), ("dp", "mp"))
        temporal_qkv_grad = wide([matrices[5 + p] for p in range(3)])
        spatial_qkv_grad = wide([matrices[p] for p in range(3)])
        spatial_proj_grad, temporal_proj_grad = matrices[3].astype(F32), matrices[4].astype(F32)
    video_grad = norm_out(grad_in, video, grad_first, temporal_gain)
    count = parts * units // width
    fc1_bias_grad = small[:count].reshape(-1)
    (
        mlp_gain_grad, mlp_shift_grad, spatial_proj_bias_grad, fc2_bias_grad,
        spatial_gain_grad, spatial_shift_grad, space_q_sum, space_v_sum, temporal_proj_bias_grad,
        time_q_sum, time_v_sum, temporal_gain_grad, temporal_shift_grad,
    ) = [small[count + i] for i in range(13)]
    return (
        output.reshape(frames, sets, slots, width),
        video_grad.reshape(frames, sets, slots, width),
        temporal_gain_grad,
        temporal_shift_grad,
        temporal_qkv_grad,
        jnp.concatenate([time_q_sum, time_v_sum]),
        temporal_proj_grad,
        temporal_proj_bias_grad,
        spatial_gain_grad,
        spatial_shift_grad,
        spatial_qkv_grad,
        jnp.concatenate([space_q_sum, space_v_sum]),
        spatial_proj_grad,
        spatial_proj_bias_grad,
        mlp_gain_grad,
        mlp_shift_grad,
        fc1_weight_grad,
        fc1_bias_grad,
        fc2_weight_grad,
        fc2_bias_grad,
    )


def solution(mesh):
    tokens = P("mp", "dp", None, None)
    return jax.shard_map(
        shards,
        mesh=mesh,
        in_specs=(tokens, P("dp")) + (P(),) * 14 + (P(None, "mp"), P("mp"), P("mp", None), P(), tokens),
        out_specs=(tokens, tokens) + (P(),) * 14 + (P("dp", "mp"), P(), P("mp", "dp"), P()),
        check_vma=False,
    )
```
